256 devices in a mesh: row: 16 (over z, core), col: 16 (over y, x).
Axes of the slice: x: 4, y: 4, z: 8, core: 2. Of those that a mesh axis runs over, the one named last changes fastest.
Arguments:
- sample_inputs: bfloat16 [65536, 256], P(('row', 'col')), may hold values from -6 to 6
- shard_extents: int32 [256], P(('row', 'col')), may hold values from 128 to 256, as said below
- upstream_adjoint: bfloat16 [65536, 256], P(('row', 'col')), may hold values from -6 to 6
- first_normalizer_factor: float32 [2, 256], replicated, may hold values from 0.5 to 1.5
- assignment_mapping: bfloat16 [2, 256, 256], replicated, may hold values from -0.375 to 0.375
- pooled_mapping: bfloat16 [2, 256, 256], replicated, may hold values from -0.375 to 0.375
- energy_mapping: float32 [2, 8, 32, 64], replicated, may hold values from -1 to 1
- softness_coefficients: float32 [2, 8, 32], replicated, may hold values from -1 to 1
- request_coefficients: float32 [2, 8, 32, 32], replicated, may hold values from -1 to 1
- lookup_coefficients: float32 [2, 8, 32, 32], replicated, may hold values from -1 to 1
- content_coefficients: float32 [2, 8, 32, 32], replicated, may hold values from -1 to 1
- output_mapping: bfloat16 [2, 256, 256], replicated, may hold values from -0.375 to 0.375
- second_normalizer_factor: float32 [2, 256], replicated, may hold values from 0.5 to 1.5
- perceptron_entrance: bfloat16 [2, 256, 1024], replicated, may hold values from -0.375 to 0.375
- perceptron_exit: bfloat16 [2, 1024, 256], replicated, may hold values from -0.1875 to 0.1875
Outputs:
- point_grad: float32 [65536, 256], P(('row', 'col'))
- ln1_grad: float32 [2, 256], replicated
- proj_x_grad: float32 [2, 256, 256], replicated
- proj_f_grad: float32 [2, 256, 256], replicated
- slice_grad: float32 [2, 8, 32, 64], replicated
- temp_grad: float32 [2, 8, 32], replicated
- query_grad: float32 [2, 8, 32, 32], replicated
- key_grad: float32 [2, 8, 32, 32], replicated
- value_grad: float32 [2, 8, 32, 32], replicated
- out_grad: float32 [2, 256, 256], replicated
- ln2_grad: float32 [2, 256], replicated
- mlp_in_grad: float32 [2, 256, 1024], replicated
- mlp_out_grad: float32 [2, 1024, 256], replicated
The draws below stay inside these ranges and needn't reach their ends.
Inputs may be any that keep to these rules, and one draw needn't show every extreme that they name: shard_extents[s] counts the live points of shard s, the first shard_extents[s] slots of that shard; one shard is full in every draw.
All inputs are finite; a program needn't handle non-finite values.
Results may differ from the reference program's by a relative error of at most 0.012.
Values sent between devices are 32-bit elements; how exact they have to be, the bound alone decides.
No kernel may reach another device: no remote copies, remote signals or barrier semaphores. Data moves between devices by JAX's collectives and lax.ppermute only.
A program may use at most 128 MiB of HBM per device.

```python
import math
import jax
import jax.numpy as jnp
from jax import lax

D = 256
FOCUS_GROUPS = 8
GROUP_BREADTH = 32
SLICES = 64
FF = 1024
PTS_DEV = 256
BLOCK_DEPTH = 2
SHARDS = 256
POINTS = 65536


def draw_shard_extents(key, part):
    key = jax.random.fold_in(key, 7)
    first_key, second_key = jax.random.split(key)
    shard_counts = jax.random.randint(first_key, (SHARDS,), PTS_DEV // 2, PTS_DEV + 1)
    full_shard = jax.random.randint(second_key, (), 0, SHARDS)
    return jnp.where(jnp.arange(SHARDS) == full_shard, PTS_DEV, shard_counts).astype(jnp.int32)


def block_scale(stream_key, extent, cuts, smallest, high):
    loudness = 1.0
    for axis_at, shards_of in cuts:
        heights = jax.random.uniform(jax.random.fold_in(jax.random.fold_in(stream_key, 6), axis_at), (shards_of,), jnp.float32, smallest / len(cuts), high / len(cuts))
        loudness = loudness * jnp.repeat(jnp.exp(heights), extent[axis_at] // shards_of).reshape((-1,) + (1,) * (len(extent) - 1 - axis_at))
    return loudness


def gaussian(own_key, extent, width, reach, pieces=(), held_as=jnp.bfloat16):
    factor_of = block_scale(own_key, extent, pieces, -0.22, 0.18) if pieces else 1.0
    entries = jax.random.normal(own_key, extent, jnp.float32) * width * factor_of
    return jnp.minimum(jnp.maximum(entries, -reach), reach).astype(held_as)


def setup_inputs(seed: int = 0) -> dict:
    seeds = jax.random.split(jax.random.key(seed), 16)
    sample_inputs = gaussian(seeds[0], (POINTS, D), 1.0, 6.0, ((0, 256),))
    shard_extents = draw_shard_extents(jax.random.fold_in(seeds[15], 71), 0)
    upstream_adjoint = gaussian(seeds[2], (POINTS, D), 1.0, 6.0, ((0, 256),))
    first_normalizer_factor = jnp.clip(1.0 + 0.1 * jax.random.normal(seeds[3], (BLOCK_DEPTH, D), jnp.float32), 0.5, 1.5)
    assignment_mapping = gaussian(seeds[4], (BLOCK_DEPTH, D, D), D ** -0.5, 0.375)
    pooled_mapping = gaussian(seeds[5], (BLOCK_DEPTH, D, D), D ** -0.5, 0.375)
    energy_mapping = gaussian(seeds[6], (BLOCK_DEPTH, FOCUS_GROUPS, GROUP_BREADTH, SLICES), GROUP_BREADTH ** -0.5, 1.0, (), jnp.float32)
    softness_coefficients = gaussian(seeds[7], (BLOCK_DEPTH, FOCUS_GROUPS, GROUP_BREADTH), GROUP_BREADTH ** -0.5, 1.0, (), jnp.float32)
    request_coefficients = gaussian(seeds[8], (BLOCK_DEPTH, FOCUS_GROUPS, GROUP_BREADTH, GROUP_BREADTH), GROUP_BREADTH ** -0.5, 1.0, (), jnp.float32)
    lookup_coefficients = gaussian(seeds[9], (BLOCK_DEPTH, FOCUS_GROUPS, GROUP_BREADTH, GROUP_BREADTH), GROUP_BREADTH ** -0.5, 1.0, (), jnp.float32)
    content_coefficients = gaussian(seeds[10], (BLOCK_DEPTH, FOCUS_GROUPS, GROUP_BREADTH, GROUP_BREADTH), GROUP_BREADTH ** -0.5, 1.0, (), jnp.float32)
    output_mapping = gaussian(seeds[11], (BLOCK_DEPTH, D, D), D ** -0.5, 0.375)
    second_normalizer_factor = jnp.clip(1.0 + 0.1 * jax.random.normal(seeds[12], (BLOCK_DEPTH, D), jnp.float32), 0.5, 1.5)
    perceptron_entrance = gaussian(seeds[13], (BLOCK_DEPTH, D, FF), D ** -0.5, 0.375)
    perceptron_exit = gaussian(seeds[14], (BLOCK_DEPTH, FF, D), FF ** -0.5, 0.1875)
    return dict(sample_inputs=sample_inputs, shard_extents=shard_extents, upstream_adjoint=upstream_adjoint, first_normalizer_factor=first_normalizer_factor, assignment_mapping=assignment_mapping, pooled_mapping=pooled_mapping, energy_mapping=energy_mapping, softness_coefficients=softness_coefficients, request_coefficients=request_coefficients, lookup_coefficients=lookup_coefficients, content_coefficients=content_coefficients, output_mapping=output_mapping, second_normalizer_factor=second_normalizer_factor, perceptron_entrance=perceptron_entrance, perceptron_exit=perceptron_exit)


EXACT_ARITHMETIC = lax.Precision.HIGHEST

def layer_norm(values, normalizer_factor):
    centered = values - lax.optimization_barrier(jnp.mean(values, axis=-1, keepdims=True))
    variance = lax.optimization_barrier(jnp.mean(centered * centered, axis=-1, keepdims=True))
    return centered * lax.rsqrt(variance + 1e-05) * normalizer_factor

def assignment_shares(assignment_source, energy_mapping, softness_coefficients):
    head_count, head_width, slice_count = energy_mapping.shape
    group_partitioning = assignment_source.reshape(assignment_source.shape[0], head_count, head_width)
    assignment_energies = jnp.einsum('nhd,hdm->nhm', group_partitioning, energy_mapping, precision=EXACT_ARITHMETIC)
    group_softness = 0.5 + jax.nn.softplus(jnp.einsum('fco,co->fc', group_partitioning, softness_coefficients, precision=EXACT_ARITHMETIC))
    return jax.nn.softmax(assignment_energies / group_softness[:, :, None], axis=-1)

def leading_onward_sweep(sample_section, live_sample_indicator, normalizer_factor, assignment_mapping, pooled_mapping, energy_mapping, softness_coefficients):
    normed = layer_norm(sample_section, normalizer_factor).astype(jnp.bfloat16)
    assignment_source = jnp.dot(normed, assignment_mapping, preferred_element_type=jnp.float32)
    feature_rows = jnp.dot(normed, pooled_mapping, preferred_element_type=jnp.float32)
    sample_assignment_share = assignment_shares(assignment_source, energy_mapping, softness_coefficients)
    masked_weight = sample_assignment_share * live_sample_indicator[:, None, None]
    group_partitioning = feature_rows.reshape(feature_rows.shape[0], energy_mapping.shape[0], -1)
    slice_numerator = jnp.einsum('fsa,fsg->sag', masked_weight, group_partitioning, precision=EXACT_ARITHMETIC)
    return (sample_assignment_share, slice_numerator, lax.optimization_barrier(jnp.sum(masked_weight, axis=0)))

def token_mix(slice_numerator, slice_total, request_coefficients, lookup_coefficients, content_coefficients):
    slice_tokens = slice_numerator / (slice_total[:, :, None] + 1e-05)
    query_matrix_rows = jnp.einsum('plc,pcu->plu', slice_tokens, request_coefficients, precision=EXACT_ARITHMETIC)
    key_matrix_rows = jnp.einsum('plc,pcu->plu', slice_tokens, lookup_coefficients, precision=EXACT_ARITHMETIC)
    value_matrix_rows = jnp.einsum('plc,pcu->plu', slice_tokens, content_coefficients, precision=EXACT_ARITHMETIC)
    attention_score_scale = 1.0 / math.sqrt(request_coefficients.shape[1])
    attention_scores = jnp.einsum('uev,ufv->uef', query_matrix_rows, key_matrix_rows, precision=EXACT_ARITHMETIC) * attention_score_scale
    slice_attention = jax.nn.softmax(attention_scores, axis=-1)
    return jnp.einsum('clq,cqg->clg', slice_attention, value_matrix_rows, precision=EXACT_ARITHMETIC)

def finish_parts(sample_section, sample_assignment_share, mixed_tokens, output_mapping, normalizer_factor, perceptron_entrance):
    spread_to_points = jnp.einsum('xlz,lzt->xlt', sample_assignment_share, mixed_tokens, precision=EXACT_ARITHMETIC)
    spread_to_points = spread_to_points.reshape(sample_section.shape[0], -1).astype(jnp.bfloat16)
    after_attn = sample_section + jnp.dot(spread_to_points, output_mapping, preferred_element_type=jnp.float32)
    normed = layer_norm(after_attn, normalizer_factor).astype(jnp.bfloat16)
    inner_act = jnp.dot(normed, perceptron_entrance, preferred_element_type=jnp.float32)
    hidden = jax.nn.gelu(inner_act).astype(jnp.bfloat16)
    return (spread_to_points, after_attn, normed, inner_act, hidden)

def finish_forward(sample_section, sample_assignment_share, mixed_tokens, output_mapping, normalizer_factor, perceptron_entrance, perceptron_exit):
    spread_to_points, after_attn, normed, inner_act, hidden = finish_parts(sample_section, sample_assignment_share, mixed_tokens, output_mapping, normalizer_factor, perceptron_entrance)
    return after_attn + jnp.dot(hidden, perceptron_exit, preferred_element_type=jnp.float32)

def finish_back(sample_section, sample_assignment_share, mixed_tokens, output_mapping, normalizer_factor, perceptron_entrance, perceptron_exit, upstream):
    spread_to_points, after_attn, normed, inner_act, hidden = finish_parts(sample_section, sample_assignment_share, mixed_tokens, output_mapping, normalizer_factor, perceptron_entrance)
    up_low = upstream.astype(jnp.bfloat16)
    grad_mlp_out = jnp.dot(hidden.T, up_low, preferred_element_type=jnp.float32)
    grad_hidden = jnp.dot(up_low, perceptron_exit.T, preferred_element_type=jnp.float32)
    gelu_value, gelu_back = jax.vjp(jax.nn.gelu, inner_act)
    grad_inner = gelu_back(grad_hidden)[0].astype(jnp.bfloat16)
    grad_mlp_in = jnp.dot(normed.T, grad_inner, preferred_element_type=jnp.float32)
    grad_normed = jnp.dot(grad_inner, perceptron_entrance.T, preferred_element_type=jnp.float32)
    norm_value, norm_back = jax.vjp(layer_norm, after_attn, normalizer_factor)
    grad_after, grad_gain = norm_back(grad_normed)
    grad_after = grad_after + upstream
    after_low = grad_after.astype(jnp.bfloat16)
    grad_out_proj = jnp.dot(spread_to_points.T, after_low, preferred_element_type=jnp.float32)
    grad_spread_tokens = jnp.dot(after_low, output_mapping.T, preferred_element_type=jnp.float32)
    grad_spread_tokens = grad_spread_tokens.reshape(sample_assignment_share.shape[0], sample_assignment_share.shape[1], -1)
    grad_token_mixed = jnp.einsum('fsa,fsg->sag', sample_assignment_share, grad_spread_tokens, precision=EXACT_ARITHMETIC)
    adjoint_assignment_share = jnp.einsum('tra,rwa->trw', grad_spread_tokens, mixed_tokens, precision=EXACT_ARITHMETIC)
    return (grad_after, adjoint_assignment_share, grad_token_mixed, (grad_out_proj, grad_gain, grad_mlp_in, grad_mlp_out))

def leading_reverse_sweep(sample_section, live_sample_indicator, normalizer_factor, assignment_mapping, pooled_mapping, energy_mapping, softness_coefficients, adjoint_assignment_share, adjoint_dividend, adjoint_share_denominator):
    normed = layer_norm(sample_section, normalizer_factor).astype(jnp.bfloat16)
    assignment_source = jnp.dot(normed, assignment_mapping, preferred_element_type=jnp.float32)
    feature_rows = jnp.dot(normed, pooled_mapping, preferred_element_type=jnp.float32)
    sample_assignment_share, share_reverse_sweep = jax.vjp(assignment_shares, assignment_source, energy_mapping, softness_coefficients)
    row_count = sample_section.shape[0]
    group_partitioning = feature_rows.reshape(row_count, energy_mapping.shape[0], -1)
    from_slice_sums = jnp.einsum('oqu,fou->foq', adjoint_dividend, group_partitioning, precision=EXACT_ARITHMETIC) + adjoint_share_denominator[None]
    grad_all = adjoint_assignment_share + from_slice_sums * live_sample_indicator[:, None, None]
    grad_features = jnp.einsum('xlz,lzt->xlt', sample_assignment_share * live_sample_indicator[:, None, None], adjoint_dividend, precision=EXACT_ARITHMETIC)
    grad_features = grad_features.reshape(row_count, -1).astype(jnp.bfloat16)
    grad_input, grad_slice, grad_temp = share_reverse_sweep(grad_all)
    input_low = grad_input.astype(jnp.bfloat16)
    grad_proj_x = jnp.dot(normed.T, input_low, preferred_element_type=jnp.float32)
    grad_proj_f = jnp.dot(normed.T, grad_features, preferred_element_type=jnp.float32)
    grad_normed = jnp.dot(input_low, assignment_mapping.T, preferred_element_type=jnp.float32) + jnp.dot(grad_features, pooled_mapping.T, preferred_element_type=jnp.float32)
    norm_value, norm_back = jax.vjp(layer_norm, sample_section, normalizer_factor)
    grad_block, grad_gain = norm_back(grad_normed)
    return (grad_block, (grad_gain, grad_proj_x, grad_proj_f, grad_slice, grad_temp))

def zeros_like_tree(tree):
    return jax.tree.map(lambda arr: jnp.zeros(arr.shape, jnp.float32), tree)

def reference(sample_inputs, shard_extents, upstream_adjoint, first_normalizer_factor, assignment_mapping, pooled_mapping, energy_mapping, softness_coefficients, request_coefficients, lookup_coefficients, content_coefficients, output_mapping, second_normalizer_factor, perceptron_entrance, perceptron_exit):
    shard_count = shard_extents.shape[0]
    slot_count = sample_inputs.shape[0] // shard_count
    carried = sample_inputs.astype(jnp.float32).reshape(shard_count, slot_count, -1)
    live_all = (jnp.arange(slot_count, dtype=jnp.int32)[None, :] < shard_extents[:, None]).astype(jnp.float32)
    layer_count = assignment_mapping.shape[0]
    saved_layers = []
    for block_ordinal in range(layer_count):
        leading_coefficients = (first_normalizer_factor[block_ordinal], assignment_mapping[block_ordinal], pooled_mapping[block_ordinal], energy_mapping[block_ordinal], softness_coefficients[block_ordinal])
        finish_params = (output_mapping[block_ordinal], second_normalizer_factor[block_ordinal], perceptron_entrance[block_ordinal], perceptron_exit[block_ordinal])

        def add_part(running, scan_item):
            sample_assignment_share, slice_numerator, slice_total = leading_onward_sweep(scan_item[0], scan_item[1], *leading_coefficients)
            return ((running[0] + slice_numerator, running[1] + slice_total), None)
        start = (jnp.zeros(energy_mapping.shape[1:2] + energy_mapping.shape[3:] + energy_mapping.shape[2:3], jnp.float32), jnp.zeros((energy_mapping.shape[1], energy_mapping.shape[3]), jnp.float32))
        (slice_numerator, slice_total), unused = lax.scan(add_part, start, (carried, live_all))
        mixed_tokens = token_mix(slice_numerator, slice_total, request_coefficients[block_ordinal], lookup_coefficients[block_ordinal], content_coefficients[block_ordinal])
        saved_layers.append((carried, slice_numerator, slice_total, mixed_tokens))

        def advance(scan_item):
            sample_assignment_share, numerator_part, total_part = leading_onward_sweep(scan_item[0], scan_item[1], *leading_coefficients)
            return finish_forward(scan_item[0], sample_assignment_share, mixed_tokens, *finish_params)
        carried = lax.map(advance, (carried, live_all))
    point_grad = upstream_adjoint.astype(jnp.float32).reshape(shard_count, slot_count, -1) * live_all[:, :, None]
    front_all = [None] * layer_count
    finish_all = [None] * layer_count
    token_all = [None] * layer_count
    for block_ordinal in reversed(range(layer_count)):
        leading_coefficients = (first_normalizer_factor[block_ordinal], assignment_mapping[block_ordinal], pooled_mapping[block_ordinal], energy_mapping[block_ordinal], softness_coefficients[block_ordinal])
        finish_params = (output_mapping[block_ordinal], second_normalizer_factor[block_ordinal], perceptron_entrance[block_ordinal], perceptron_exit[block_ordinal])
        layer_input, slice_numerator, slice_total, mixed_tokens = saved_layers[block_ordinal]

        def finish_step(running, scan_item):
            sample_assignment_share, numerator_part, total_part = leading_onward_sweep(scan_item[0], scan_item[1], *leading_coefficients)
            grad_after, adjoint_assignment_share, grad_token_mixed, finish_grads = finish_back(scan_item[0], sample_assignment_share, mixed_tokens, *finish_params, scan_item[2])
            return ((running[0] + grad_token_mixed, jax.tree.map(jnp.add, running[1], finish_grads)), (grad_after, adjoint_assignment_share))
        start = (jnp.zeros(mixed_tokens.shape, jnp.float32), zeros_like_tree(finish_params))
        (grad_token_mixed, finish_grads), (grad_after, adjoint_assignment_share) = lax.scan(finish_step, start, (layer_input, live_all, point_grad))
        token_value, token_back = jax.vjp(token_mix, slice_numerator, slice_total, request_coefficients[block_ordinal], lookup_coefficients[block_ordinal], content_coefficients[block_ordinal])
        adjoint_dividend, adjoint_share_denominator, grad_query, grad_key, grad_value = token_back(grad_token_mixed)

        def front_step(running, scan_item):
            grad_block, front_grads = leading_reverse_sweep(scan_item[0], scan_item[1], *leading_coefficients, scan_item[2], adjoint_dividend, adjoint_share_denominator)
            return (jax.tree.map(jnp.add, running, front_grads), grad_block)
        front_grads, grad_blocks = lax.scan(front_step, zeros_like_tree(leading_coefficients), (layer_input, live_all, adjoint_assignment_share))
        point_grad = grad_after + grad_blocks
        front_all[block_ordinal] = front_grads
        finish_all[block_ordinal] = finish_grads
        token_all[block_ordinal] = (grad_query, grad_key, grad_value)

    def stacked(source, position):
        return jnp.stack([source[index_l][position] for index_l in range(layer_count)])
    return (point_grad.reshape(sample_inputs.shape[0], -1), stacked(front_all, 0), stacked(front_all, 1), stacked(front_all, 2), stacked(front_all, 3), stacked(front_all, 4), stacked(token_all, 0), stacked(token_all, 1), stacked(token_all, 2), stacked(finish_all, 0), stacked(finish_all, 1), stacked(finish_all, 2), stacked(finish_all, 3))
```

```python
import math

import jax
import jax.numpy as jnp
from jax import lax
from jax.sharding import PartitionSpec as P

EXACT_ARITHMETIC = lax.Precision.HIGHEST


def layer_norm(values, normalizer_factor):
    centered = values - jnp.mean(values, axis=-1, keepdims=True)
    variance = jnp.mean(centered * centered, axis=-1, keepdims=True)
    return centered * lax.rsqrt(variance + 1e-05) * normalizer_factor


def assignment_shares(assignment_source, energy_mapping, softness_coefficients):
    head_count, head_width, slice_count = energy_mapping.shape
    group_partitioning = assignment_source.reshape(
        assignment_source.shape[0], head_count, head_width
    )
    assignment_energies = jnp.einsum(
        "nhd,hdm->nhm", group_partitioning, energy_mapping, precision=EXACT_ARITHMETIC
    )
    group_softness = 0.5 + jax.nn.softplus(
        jnp.einsum(
            "fco,co->fc", group_partitioning, softness_coefficients, precision=EXACT_ARITHMETIC
        )
    )
    return jax.nn.softmax(assignment_energies / group_softness[:, :, None], axis=-1)


def leading_onward_sweep(
    sample_section,
    live_sample_indicator,
    normalizer_factor,
    assignment_mapping,
    pooled_mapping,
    energy_mapping,
    softness_coefficients,
):
    normed = layer_norm(sample_section, normalizer_factor).astype(jnp.bfloat16)
    assignment_source = jnp.dot(normed, assignment_mapping, preferred_element_type=jnp.float32)
    feature_rows = jnp.dot(normed, pooled_mapping, preferred_element_type=jnp.float32)
    sample_assignment_share = assignment_shares(
        assignment_source, energy_mapping, softness_coefficients
    )
    masked_weight = sample_assignment_share * live_sample_indicator[:, None, None]
    group_partitioning = feature_rows.reshape(feature_rows.shape[0], energy_mapping.shape[0], -1)
    slice_numerator = jnp.einsum(
        "fsa,fsg->sag", masked_weight, group_partitioning, precision=EXACT_ARITHMETIC
    )
    return (sample_assignment_share, slice_numerator, jnp.sum(masked_weight, axis=0))


def token_mix(
    slice_numerator, slice_total, request_coefficients, lookup_coefficients, content_coefficients
):
    slice_tokens = slice_numerator / (slice_total[:, :, None] + 1e-05)
    query_matrix_rows = jnp.einsum(
        "plc,pcu->plu", slice_tokens, request_coefficients, precision=EXACT_ARITHMETIC
    )
    key_matrix_rows = jnp.einsum(
        "plc,pcu->plu", slice_tokens, lookup_coefficients, precision=EXACT_ARITHMETIC
    )
    value_matrix_rows = jnp.einsum(
        "plc,pcu->plu", slice_tokens, content_coefficients, precision=EXACT_ARITHMETIC
    )
    attention_score_scale = 1.0 / math.sqrt(request_coefficients.shape[1])
    attention_scores = (
        jnp.einsum("uev,ufv->uef", query_matrix_rows, key_matrix_rows, precision=EXACT_ARITHMETIC)
        * attention_score_scale
    )
    slice_attention = jax.nn.softmax(attention_scores, axis=-1)
    return jnp.einsum(
        "clq,cqg->clg", slice_attention, value_matrix_rows, precision=EXACT_ARITHMETIC
    )


def finish_parts(
    sample_section,
    sample_assignment_share,
    mixed_tokens,
    output_mapping,
    normalizer_factor,
    perceptron_entrance,
):
    spread_to_points = jnp.einsum(
        "xlz,lzt->xlt", sample_assignment_share, mixed_tokens, precision=EXACT_ARITHMETIC
    )
    spread_to_points = spread_to_points.reshape(sample_section.shape[0], -1).astype(jnp.bfloat16)
    after_attn = sample_section + jnp.dot(
        spread_to_points, output_mapping, preferred_element_type=jnp.float32
    )
    normed = layer_norm(after_attn, normalizer_factor).astype(jnp.bfloat16)
    inner_act = jnp.dot(normed, perceptron_entrance, preferred_element_type=jnp.float32)
    hidden = jax.nn.gelu(inner_act).astype(jnp.bfloat16)
    return (spread_to_points, after_attn, normed, inner_act, hidden)


def finish_forward(
    sample_section,
    sample_assignment_share,
    mixed_tokens,
    output_mapping,
    normalizer_factor,
    perceptron_entrance,
    perceptron_exit,
):
    spread_to_points, after_attn, normed, inner_act, hidden = finish_parts(
        sample_section,
        sample_assignment_share,
        mixed_tokens,
        output_mapping,
        normalizer_factor,
        perceptron_entrance,
    )
    return after_attn + jnp.dot(hidden, perceptron_exit, preferred_element_type=jnp.float32)


def finish_back(
    sample_section,
    sample_assignment_share,
    mixed_tokens,
    output_mapping,
    normalizer_factor,
    perceptron_entrance,
    perceptron_exit,
    upstream,
):
    spread_to_points, after_attn, normed, inner_act, hidden = finish_parts(
        sample_section,
        sample_assignment_share,
        mixed_tokens,
        output_mapping,
        normalizer_factor,
        perceptron_entrance,
    )
    up_low = upstream.astype(jnp.bfloat16)
    grad_mlp_out = jnp.dot(hidden.T, up_low, preferred_element_type=jnp.float32)
    grad_hidden = jnp.dot(up_low, perceptron_exit.T, preferred_element_type=jnp.float32)
    gelu_value, gelu_back = jax.vjp(jax.nn.gelu, inner_act)
    grad_inner = gelu_back(grad_hidden)[0].astype(jnp.bfloat16)
    grad_mlp_in = jnp.dot(normed.T, grad_inner, preferred_element_type=jnp.float32)
    grad_normed = jnp.dot(grad_inner, perceptron_entrance.T, preferred_element_type=jnp.float32)
    norm_value, norm_back = jax.vjp(layer_norm, after_attn, normalizer_factor)
    grad_after, grad_gain = norm_back(grad_normed)
    grad_after = grad_after + upstream
    after_low = grad_after.astype(jnp.bfloat16)
    grad_out_proj = jnp.dot(spread_to_points.T, after_low, preferred_element_type=jnp.float32)
    grad_spread_tokens = jnp.dot(after_low, output_mapping.T, preferred_element_type=jnp.float32)
    grad_spread_tokens = grad_spread_tokens.reshape(
        sample_assignment_share.shape[0], sample_assignment_share.shape[1], -1
    )
    grad_token_mixed = jnp.einsum(
        "fsa,fsg->sag", sample_assignment_share, grad_spread_tokens, precision=EXACT_ARITHMETIC
    )
    adjoint_assignment_share = jnp.einsum(
        "tra,rwa->trw", grad_spread_tokens, mixed_tokens, precision=EXACT_ARITHMETIC
    )
    return (
        grad_after,
        adjoint_assignment_share,
        grad_token_mixed,
        (grad_out_proj, grad_gain, grad_mlp_in, grad_mlp_out),
    )


def leading_reverse_sweep(
    sample_section,
    live_sample_indicator,
    normalizer_factor,
    assignment_mapping,
    pooled_mapping,
    energy_mapping,
    softness_coefficients,
    adjoint_assignment_share,
    adjoint_dividend,
    adjoint_share_denominator,
):
    normed = layer_norm(sample_section, normalizer_factor).astype(jnp.bfloat16)
    assignment_source = jnp.dot(normed, assignment_mapping, preferred_element_type=jnp.float32)
    feature_rows = jnp.dot(normed, pooled_mapping, preferred_element_type=jnp.float32)
    sample_assignment_share, share_reverse_sweep = jax.vjp(
        assignment_shares, assignment_source, energy_mapping, softness_coefficients
    )
    row_count = sample_section.shape[0]
    group_partitioning = feature_rows.reshape(row_count, energy_mapping.shape[0], -1)
    from_slice_sums = (
        jnp.einsum("oqu,fou->foq", adjoint_dividend, group_partitioning, precision=EXACT_ARITHMETIC)
        + adjoint_share_denominator[None]
    )
    grad_all = adjoint_assignment_share + from_slice_sums * live_sample_indicator[:, None, None]
    grad_features = jnp.einsum(
        "xlz,lzt->xlt",
        sample_assignment_share * live_sample_indicator[:, None, None],
        adjoint_dividend,
        precision=EXACT_ARITHMETIC,
    )
    grad_features = grad_features.reshape(row_count, -1).astype(jnp.bfloat16)
    grad_input, grad_slice, grad_temp = share_reverse_sweep(grad_all)
    input_low = grad_input.astype(jnp.bfloat16)
    grad_proj_x = jnp.dot(normed.T, input_low, preferred_element_type=jnp.float32)
    grad_proj_f = jnp.dot(normed.T, grad_features, preferred_element_type=jnp.float32)
    grad_normed = jnp.dot(
        input_low, assignment_mapping.T, preferred_element_type=jnp.float32
    ) + jnp.dot(grad_features, pooled_mapping.T, preferred_element_type=jnp.float32)
    norm_value, norm_back = jax.vjp(layer_norm, sample_section, normalizer_factor)
    grad_block, grad_gain = norm_back(grad_normed)
    return (grad_block, (grad_gain, grad_proj_x, grad_proj_f, grad_slice, grad_temp))


AXES = ("row", "col")


def linear(z, c, y, x):
    return (z * 2 + c) * 16 + y * 4 + x


def swap(v, zm=0, cm=0, ym=0, xm=0):
    pairs = [
        (linear(z, c, y, x), linear(z ^ zm, c ^ cm, y ^ ym, x ^ xm))
        for z in range(8)
        for c in range(2)
        for y in range(4)
        for x in range(4)
    ]
    return lax.ppermute(v, AXES, pairs)


def coords():
    r = lax.axis_index("row")
    q = lax.axis_index("col")
    return r // 2, r % 2, q // 4, q % 4


def gray(v):
    return ((v ^ (v >> 1)) & 1, v >> 1)


def steps():
    z, c, y, x = coords()
    x0, x1 = gray(x)
    y0, y1 = gray(y)
    return dict(
        c=(c, dict(cm=1)),
        x0=(x0, dict(xm=1)),
        x1=(x1, dict(xm=3)),
        y0=(y0, dict(ym=1)),
        y1=(y1, dict(ym=3)),
    )


def halve(v, st):
    b, k = st
    h = v.shape[0] // 2
    mine = lax.dynamic_slice_in_dim(v, b * h, h, 0)
    other = lax.dynamic_slice_in_dim(v, (1 - b) * h, h, 0)
    return mine + swap(other, **k)


def double(v, st):
    b, k = st
    o = swap(v, **k)
    return jnp.where(b == 0, jnp.concatenate([v, o]), jnp.concatenate([o, v]))


def four(m, *ks):
    p, q, r = (swap(m, **k) for k in ks)
    return (m + p) + (q + r)


def along_z(m):
    m = four(m, dict(zm=1), dict(zm=7), dict(zm=6))
    return m + swap(m, zm=2)


def small_sum(v):
    st = steps()
    m = halve(v, st["c"])
    m = four(m, dict(xm=1), dict(xm=2), dict(xm=3))
    m = four(m, dict(ym=1), dict(ym=2), dict(ym=3))
    m = along_z(m)
    return double(m, st["c"])


ORDERS = (
    ("x0", "x1", "y0", "y1"),
    ("y0", "y1", "x0", "x1"),
    ("x1", "x0", "y1", "y0"),
    ("y1", "y0", "x1", "x0"),
)


def big_sum(v):
    st = steps()
    n = len(ORDERS)
    m = halve(v, st["c"])
    h = m.shape[0] // n
    parts = [m[i * h : (i + 1) * h] for i in range(n)]
    for k in range(4):
        parts = [halve(p, st[ORDERS[i][k]]) for i, p in enumerate(parts)]
    m = along_z(jnp.concatenate(parts))
    h = m.shape[0] // n
    parts = [m[i * h : (i + 1) * h] for i in range(n)]
    for k in (3, 2, 1, 0):
        parts = [double(p, st[ORDERS[i][k]]) for i, p in enumerate(parts)]
    return double(jnp.concatenate(parts), st["c"])


def padded_rows(pieces, rows):
    flat = jnp.concatenate([p.reshape(-1) for p in pieces])
    return jnp.pad(flat, (0, rows * 128 - flat.size)).reshape(rows, 128)


def reduce_grads(packed):
    rows = -(-packed.size // (128 * 1024)) * 1024
    return big_sum(padded_rows([packed], rows)).reshape(-1)


def reduce_tokens(numer, total):
    summed = small_sum(padded_rows([numer, total], 144)).reshape(-1)
    k = numer.size
    return summed[:k].reshape(numer.shape), summed[k : k + total.size].reshape(total.shape)


def body(
    sample_inputs,
    shard_extents,
    upstream_adjoint,
    first_normalizer_factor,
    assignment_mapping,
    pooled_mapping,
    energy_mapping,
    softness_coefficients,
    request_coefficients,
    lookup_coefficients,
    content_coefficients,
    output_mapping,
    second_normalizer_factor,
    perceptron_entrance,
    perceptron_exit,
):
    slot_count = sample_inputs.shape[0]
    live_sample_indicator = (jnp.arange(slot_count, dtype=jnp.int32) < shard_extents[0]).astype(
        jnp.float32
    )
    layer_count = assignment_mapping.shape[0]
    carried = sample_inputs.astype(jnp.float32)
    saved_layers = []
    for block_ordinal in range(layer_count):
        leading_coefficients = (
            first_normalizer_factor[block_ordinal],
            assignment_mapping[block_ordinal],
            pooled_mapping[block_ordinal],
            energy_mapping[block_ordinal],
            softness_coefficients[block_ordinal],
        )
        finish_params = (
            output_mapping[block_ordinal],
            second_normalizer_factor[block_ordinal],
            perceptron_entrance[block_ordinal],
            perceptron_exit[block_ordinal],
        )
        sample_assignment_share, numer_part, total_part = leading_onward_sweep(
            carried, live_sample_indicator, *leading_coefficients
        )
        slice_numerator, slice_total = reduce_tokens(numer_part, total_part)
        mixed_tokens = token_mix(
            slice_numerator,
            slice_total,
            request_coefficients[block_ordinal],
            lookup_coefficients[block_ordinal],
            content_coefficients[block_ordinal],
        )
        saved_layers.append((carried, slice_numerator, slice_total, mixed_tokens))
        carried = finish_forward(carried, sample_assignment_share, mixed_tokens, *finish_params)
    point_grad = upstream_adjoint.astype(jnp.float32) * live_sample_indicator[:, None]
    front_all = [None] * layer_count
    finish_all = [None] * layer_count
    token_all = [None] * layer_count
    for block_ordinal in reversed(range(layer_count)):
        leading_coefficients = (
            first_normalizer_factor[block_ordinal],
            assignment_mapping[block_ordinal],
            pooled_mapping[block_ordinal],
            energy_mapping[block_ordinal],
            softness_coefficients[block_ordinal],
        )
        finish_params = (
            output_mapping[block_ordinal],
            second_normalizer_factor[block_ordinal],
            perceptron_entrance[block_ordinal],
            perceptron_exit[block_ordinal],
        )
        layer_input, slice_numerator, slice_total, mixed_tokens = saved_layers[block_ordinal]
        sample_assignment_share, numer_part, total_part = leading_onward_sweep(
            layer_input, live_sample_indicator, *leading_coefficients
        )
        grad_after, adjoint_assignment_share, mixed_part, finish_grads = finish_back(
            layer_input, sample_assignment_share, mixed_tokens, *finish_params, point_grad
        )
        grad_token_mixed = small_sum(mixed_part.reshape(128, 128)).reshape(mixed_part.shape)
        token_value, token_back = jax.vjp(
            token_mix,
            slice_numerator,
            slice_total,
            request_coefficients[block_ordinal],
            lookup_coefficients[block_ordinal],
            content_coefficients[block_ordinal],
        )
        adjoint_dividend, adjoint_share_denominator, grad_query, grad_key, grad_value = token_back(
            grad_token_mixed
        )
        grad_block, front_grads = leading_reverse_sweep(
            layer_input,
            live_sample_indicator,
            *leading_coefficients,
            adjoint_assignment_share,
            adjoint_dividend,
            adjoint_share_denominator
        )
        point_grad = grad_after + grad_block
        front_all[block_ordinal] = front_grads
        finish_all[block_ordinal] = finish_grads
        token_all[block_ordinal] = (grad_query, grad_key, grad_value)
    flat_list = []
    for block_ordinal in range(layer_count):
        flat_list.extend(front_all[block_ordinal])
        flat_list.extend(finish_all[block_ordinal])
    packed = jnp.concatenate([piece.reshape(-1) for piece in flat_list])
    summed = reduce_grads(packed)
    restored = []
    offset = 0
    for piece in flat_list:
        piece_length = piece.size
        restored.append(summed[offset : offset + piece_length].reshape(piece.shape))
        offset = offset + piece_length

    def stacked_summed(position):
        return jnp.stack([restored[index_l * 9 + position] for index_l in range(layer_count)])

    def stacked_token(position):
        return jnp.stack([token_all[index_l][position] for index_l in range(layer_count)])

    return (
        point_grad,
        stacked_summed(0),
        stacked_summed(1),
        stacked_summed(2),
        stacked_summed(3),
        stacked_summed(4),
        stacked_token(0),
        stacked_token(1),
        stacked_token(2),
        stacked_summed(5),
        stacked_summed(6),
        stacked_summed(7),
        stacked_summed(8),
    )


def solution(mesh):
    in_specs = (
        P(("row", "col"), None),
        P(("row", "col")),
        P(("row", "col"), None),
        P(),
        P(),
        P(),
        P(),
        P(),
        P(),
        P(),
        P(),
        P(),
        P(),
        P(),
        P(),
    )
    out_specs = (
        P(("row", "col"), None),
        P(),
        P(),
        P(),
        P(),
        P(),
        P(),
        P(),
        P(),
        P(),
        P(),
        P(),
        P(),
    )
    return jax.shard_map(body, mesh=mesh, in_specs=in_specs, out_specs=out_specs, check_vma=False)
```

```python
import functools
import math

import jax
import jax.numpy as jnp
from jax import lax
from jax.experimental import pallas as pl
from jax.experimental.pallas import tpu as pltpu
from jax.sharding import PartitionSpec as P

BF = jnp.bfloat16
F32 = jnp.float32
PTS = 256
D = 256
FF = 1024
HEADS = 8
WIDTH = 32
SLICES = 64
PAIRS = HEADS // 2
EPS = 1e-05


def dot(a, b, ca=1, cb=0):
    return lax.dot_general(a, b, (((ca,), (cb,)), ((), ())), preferred_element_type=F32)


def exact(a, b, ca=1, cb=0):
    return lax.dot_general(
        a,
        b,
        (((ca,), (cb,)), ((), ())),
        precision=lax.Precision.HIGHEST,
        preferred_element_type=F32,
    )


def head(v, h, n=WIDTH):
    return v[h * n : (h + 1) * n]


def stack(pieces):
    return jnp.concatenate(pieces, axis=0)


def iota(shape, axis):
    return lax.broadcasted_iota(jnp.int32, shape, axis)


def column(row):
    return jnp.transpose(jnp.broadcast_to(row, (PTS, D)))


def row_sum(v):
    return jnp.sum(jnp.transpose(v), axis=0, keepdims=True)


def normed(x):
    c = x - jnp.mean(x, axis=0, keepdims=True)
    r = lax.rsqrt(jnp.mean(c * c, axis=0, keepdims=True) + EPS)
    return c * r, r


def norm_back(xhat, r, gain, g):
    dh = g * gain
    return r * (
        dh
        - jnp.mean(dh, axis=0, keepdims=True)
        - xhat * jnp.mean(dh * xhat, axis=0, keepdims=True)
    )


def live_rows(n):
    keep = (iota((8, PTS), 0) == 0) & (iota((8, PTS), 1) < n)
    return jnp.where(keep, 1.0, 0.0)


def softness_rows(s):
    wide = jnp.concatenate([s] * HEADS, axis=1)
    return jnp.where((iota((HEADS, D), 1) >> 5) == iota((HEADS, D), 0), wide, 0.0)


def block_diagonal(w):
    wide = jnp.concatenate([w.reshape(D, WIDTH)] * HEADS, axis=1)
    return jnp.where((iota((D, D), 0) >> 5) == (iota((D, D), 1) >> 5), wide, 0.0)


def pair_rows(r):
    return jnp.where(iota((WIDTH, 128), 1) < SLICES, r[:WIDTH], r[WIDTH : 2 * WIDTH])


def front(x, gain, wx, wf, energy, softness, live8):
    xhat, _ = normed(x)
    a = (xhat * gain).astype(BF)
    xm = dot(wx, a, 0, 0)
    fm = dot(wf, a, 0, 0)
    s = exact(softness_rows(softness), xm)
    temp = 0.5 + jnp.maximum(s, 0.0) + jnp.log1p(jnp.exp(-jnp.abs(s)))
    es, ws = [], []
    for h in range(HEADS):
        e = exact(energy[h], head(xm, h), 0, 0) / temp[h : h + 1]
        p = jnp.exp(e - jnp.max(e, axis=0, keepdims=True))
        es.append(e)
        ws.append(p / jnp.sum(p, axis=0, keepdims=True))
    w = stack(ws)
    masked = fm * live8[:1]
    rows = []
    for j in range(PAIRS):
        r = exact(stack([head(masked, j, 64), live8]), head(w, j, 128), 1, 1)
        rows += [pair_rows(r), r[64:72]]
    return a, xm, fm, s, stack(es), w, stack(rows)


def token_mix(numer, wq, wk, wv):
    toks, invs = [], []
    for j in range(PAIRS):
        inv = 1.0 / (numer[40 * j + 32 : 40 * j + 33] + EPS)
        t = numer[40 * j : 40 * j + 32] / (numer[40 * j + 32 : 40 * j + 33] + EPS)
        inv = jnp.broadcast_to(inv, (WIDTH, 128))
        toks += [t[:, :SLICES], t[:, SLICES:]]
        invs += [inv[:, :SLICES], inv[:, SLICES:]]
    tok = stack(toks)
    q, k, v = (exact(block_diagonal(w), tok, 0, 0) for w in (wq, wk, wv))
    attns, mixes = [], []
    for h in range(HEADS):
        sc = exact(head(k, h), head(q, h), 0, 0) * (1.0 / math.sqrt(WIDTH))
        p = jnp.exp(sc - jnp.max(sc, axis=0, keepdims=True))
        attn = p / jnp.sum(p, axis=0, keepdims=True)
        attns.append(attn)
        mixes.append(exact(head(v, h), attn))
    return (tok, q, k, v, stack(invs), stack(mixes)), stack(attns)


def token_back(dmix, toks, attn, wq, wk, wv):
    tok, q, k, v, inv = (toks[i] for i in range(5))
    dqs, dks, dvs = [], [], []
    for h in range(HEADS):
        at, dm = head(attn, h, SLICES), head(dmix, h)
        dvs.append(exact(dm, at, 1, 1))
        da = exact(head(v, h), dm, 0, 0)
        ds = at * (da - jnp.sum(at * da, axis=0, keepdims=True)) * (1.0 / math.sqrt(WIDTH))
        dqs.append(exact(head(k, h), ds))
        dks.append(exact(head(q, h), ds, 1, 1))
    dq, dk, dv = stack(dqs), stack(dks), stack(dvs)
    dtok = exact(block_diagonal(wq), dq) + exact(block_diagonal(wk), dk)
    dtok = dtok + exact(block_diagonal(wv), dv)
    dnumer = dtok * inv
    return dnumer, dnumer * tok, (dq, dk, dv)


def finish(x, w, mixed, wo, gain, w1):
    y = stack([exact(head(mixed, h), head(w, h, SLICES)) for h in range(HEADS)]).astype(BF)
    x1 = x + dot(wo, y, 0, 0)
    xhat, _ = normed(x1)
    b = (xhat * gain).astype(BF)
    return y, x1, b, dot(w1, b, 0, 0)


C0 = math.sqrt(2.0 / math.pi)
C1 = 0.044715


def gelu(u):
    return 0.5 * u * (1.0 + jnp.tanh(C0 * (u + C1 * (u * u * u))))


def gelu_slope(u):
    t = jnp.tanh(C0 * (u + C1 * (u * u * u)))
    return 0.5 * (1.0 + t) + 0.5 * u * (1.0 - t * t) * (C0 * (1.0 + 3.0 * C1 * (u * u)))


def finish_back(up, x1, u, w, mixed, wo, gain, w1, w2):
    low = up.astype(BF)
    du = (dot(w2, low) * gelu_slope(u)).astype(BF)
    db = dot(w1, du)
    xhat, r = normed(x1)
    dgain = row_sum(db * xhat)
    after = norm_back(xhat, r, gain, db) + up
    after_low = after.astype(BF)
    dy = dot(wo, after_low)
    dmix = stack(
        [
            pair_rows(exact(head(dy, j, 64), head(w, j, 128), 1, 1))
            for j in range(PAIRS)
        ]
    )
    dw = stack([exact(head(mixed, h), head(dy, h), 0, 0) for h in range(HEADS)])
    return low, du, after, after_low, dgain, dmix, dw


def unpair(v):
    out = []
    for j in range(PAIRS):
        blk = head(v, j)
        out += [blk[:, :SLICES], blk[:, SLICES:]]
    return stack(out)


def front_back(dnumer, share, dw, x, gain, fm, s, e, w, wx, wf, energy, softness, live8):
    live = live8[:1]
    masked = fm * live
    temp = 0.5 + jnp.maximum(s, 0.0) + jnp.log1p(jnp.exp(-jnp.abs(s)))
    inv_temp = 1.0 / temp
    first = iota((8, SLICES), 0) == 0
    dls, dts, dfs, dxs = [], [], [], []
    for h in range(HEADS):
        dn, wh = head(dnumer, h), head(w, h, SLICES)
        dtot = jnp.where(first, -jnp.sum(head(share, h), axis=0, keepdims=True), 0.0)
        dwh = head(dw, h, SLICES) + exact(
            stack([dn, dtot]), stack([head(masked, h), live8]), 0, 0
        )
        de = wh * (dwh - jnp.sum(wh * dwh, axis=0, keepdims=True))
        dl = de * inv_temp[h : h + 1]
        dts.append(-jnp.sum(dl * head(e, h, SLICES), axis=0, keepdims=True))
        dls.append(dl)
        dfs.append(exact(dn, wh))
        dxs.append(exact(energy[h], dl))
    ds = stack(dts) / (1.0 + jnp.exp(-s))
    dx = (stack(dxs) + exact(softness_rows(softness), ds, 0, 0)).astype(BF)
    df = (stack(dfs) * live).astype(BF)
    da = dot(wx, dx) + dot(wf, df)
    xhat, r = normed(x)
    return dx, df, stack(dls), ds, norm_back(xhat, r, gain, da), row_sum(da * xhat)


def put(refs, values):
    for ref, value in zip(refs, values):
        ref[...] = value


def first_kernel(n, x, g1, wx, wf, en, so, xt, *out):
    v = jnp.transpose(x[...].astype(F32))
    xt[...] = v
    put(out, front(v, column(g1[0:1]), wx[...], wf[...], en[...], so[0], live_rows(n[0])))


def save_tokens(toks, attn, tok_ref, attn_ref):
    for i, t in enumerate(toks):
        tok_ref[i] = t
    attn_ref[...] = attn


def middle_kernel(
    n, numer, x, w, wq, wk, wv, wo, g2, w1, w2, g1, wx, wf, en, so,
    tok_ref, attn_ref, y_ref, x1_ref, b_ref, u_ref, hid_ref, xt, *out
):
    toks, attn = token_mix(numer[...], wq[...], wk[...], wv[...])
    save_tokens(toks, attn, tok_ref, attn_ref)
    y, x1, b, u = finish(x[...], w[...], toks[5], wo[...], column(g2[0:1]), w1[...])
    hid = gelu(u).astype(BF)
    put((y_ref, x1_ref, b_ref, u_ref, hid_ref), (y, x1, b, u, hid))
    v = x1 + dot(w2[...], hid, 0, 0)
    xt[...] = v
    put(out, front(v, column(g1[1:2]), wx[...], wf[...], en[...], so[1], live_rows(n[0])))


def turn_kernel(
    n, numer, x, w, wq, wk, wv, wo, g2, w1, w2, up,
    tok_ref, attn_ref, y_ref, b_ref, hid_ref, *out
):
    toks, attn = token_mix(numer[...], wq[...], wk[...], wv[...])
    save_tokens(toks, attn, tok_ref, attn_ref)
    gain = column(g2[1:2])
    y, x1, b, u = finish(x[...], w[...], toks[5], wo[...], gain, w1[...])
    put((y_ref, b_ref, hid_ref), (y, b, gelu(u).astype(BF)))
    upt = jnp.transpose(up[...].astype(F32)) * live_rows(n[0])[:1]
    put(out, finish_back(upt, x1, u, w[...], toks[5], wo[...], gain, w1[...], w2[...]))


def token_grads(tok, dqkv, refs):
    for ref, d in zip(refs, dqkv):
        for h in range(HEADS):
            ref[h] = exact(head(tok, h), head(d, h), 1, 1)


def reverse(layer, n, dmix, tok_ref, attn, wq, wk, wv, dw, x, fm, s, e, w, g1, wx, wf, en, so):
    dnumer, share, dqkv = token_back(
        unpair(dmix[...]), tok_ref, attn[...], wq[...], wk[...], wv[...]
    )
    out = front_back(
        dnumer, share, dw[...], x[...], column(g1[layer : layer + 1]), fm[...], s[...],
        e[...], w[...], wx[...], wf[...], en[...], so[layer], live_rows(n[0]),
    )
    return out, dqkv


def back_kernel(
    n, dmix, tok_ref, attn, wq, wk, wv, dw, x, fm, s, e, w, g1, wx, wf, en, so,
    after, x1, u, w_below, tok_below, wo, g2, w1, w2,
    dwq, dwk, dwv, dx, df, dl, ds, dg, *out
):
    r, dqkv = reverse(1, n, dmix, tok_ref, attn, wq, wk, wv, dw, x, fm, s, e, w, g1, wx, wf, en, so)
    put((dx, df, dl, ds), r[:4])
    dg[...] = r[5]
    up = after[...] + r[4]
    put(
        out,
        finish_back(
            up, x1[...], u[...], w_below[...], tok_below[5], wo[...], column(g2[0:1]),
            w1[...], w2[...],
        ),
    )
    token_grads(tok_ref[0], dqkv, (dwq, dwk, dwv))


def last_kernel(
    n, dmix, tok_ref, attn, wq, wk, wv, dw, x, fm, s, e, w, g1, wx, wf, en, so, after,
    dwq, dwk, dwv, dx, df, dl, ds, dg, point
):
    r, dqkv = reverse(0, n, dmix, tok_ref, attn, wq, wk, wv, dw, x, fm, s, e, w, g1, wx, wf, en, so)
    put((dx, df, dl, ds), r[:4])
    dg[...] = r[5]
    point[...] = jnp.transpose(after[...] + r[4])
    token_grads(tok_ref[0], dqkv, (dwq, dwk, dwv))


def first_row(v):
    return jnp.where(iota((8, D), 0) == 0, v, 0.0)


FINISH_ROWS = 2312
FRONT_ROWS = 584


def finish_grads_kernel(hid, up, b, du, y, after, dg, out):
    out[0:1024] = dot(hid[...], up[...], 1, 1)
    for k in range(4):
        out[1024 + 256 * k : 1280 + 256 * k] = dot(b[...], du[256 * k : 256 * (k + 1)], 1, 1)
    out[2048:2304] = dot(y[...], after[...], 1, 1)
    out[2304:2312] = first_row(dg[...])
    if out.shape[0] > FINISH_ROWS:
        out[FINISH_ROWS:] = jnp.zeros((out.shape[0] - FINISH_ROWS, D), F32)


def front_grads_kernel(a, dx, df, xm, dl, ds, dg, out):
    out[0:256] = dot(a[...], dx[...], 1, 1)
    out[256:512] = dot(a[...], df[...], 1, 1)
    for j in range(PAIRS):
        r = exact(xm[64 * j : 64 * (j + 1)], dl[128 * j : 128 * (j + 1)], 1, 1)
        row, lane = 512 + 32 * (j // 2), 128 * (j % 2)
        out[row : row + 32, lane : lane + 128] = pair_rows(r)
    t = exact(ds[...], xm[...], 1, 1)
    t = jnp.where((iota((HEADS, D), 1) >> 5) == iota((HEADS, D), 0), t, 0.0)
    t = jnp.sum(t, axis=0, keepdims=True)
    out[576:584] = first_row(dg[...]) + jnp.where(iota((8, D), 0) == 1, t, 0.0)
    if out.shape[0] > FRONT_ROWS:
        out[FRONT_ROWS:] = jnp.zeros((out.shape[0] - FRONT_ROWS, D), F32)


def unpack_kernel(fin0, fro0, fin1, fro1, ln1, gx, gf, ge, gs, go, ln2, g1, g2):
    for l, (fin, fro) in enumerate(((fin0, fro0), (fin1, fro1))):
        g2[l] = fin[0:1024]
        for k in range(4):
            g1[l, :, 256 * k : 256 * (k + 1)] = fin[1024 + 256 * k : 1280 + 256 * k]
        go[l] = fin[2048:2304]
        ln2[l : l + 1] = fin[2304:2305]
        gx[l] = fro[0:256]
        gf[l] = fro[256:512]
        for h in range(HEADS):
            j, i = h // 2, h % 2
            row, lane = 512 + 32 * (j // 2), 128 * (j % 2)
            ge[l, h] = fro[row : row + 32, lane : lane + 128][:, 64 * i : 64 * (i + 1)]
            gs[l, h : h + 1] = fro[577:578, 32 * h : 32 * (h + 1)]
        ln1[l : l + 1] = fro[576:577]


AXES = ("row", "col")


def linear(z, c, y, x):
    return (z * 2 + c) * 16 + y * 4 + x


def swap(v, zm=0, cm=0, ym=0, xm=0):
    pairs = [
        (linear(z, c, y, x), linear(z ^ zm, c ^ cm, y ^ ym, x ^ xm))
        for z in range(8)
        for c in range(2)
        for y in range(4)
        for x in range(4)
    ]
    return lax.ppermute(v, AXES, pairs)


def coords():
    r = lax.axis_index("row")
    q = lax.axis_index("col")
    return r // 2, r % 2, q // 4, q % 4


def gray(v):
    return ((v ^ (v >> 1)) & 1, v >> 1)


def steps():
    z, c, y, x = coords()
    x0, x1 = gray(x)
    y0, y1 = gray(y)
    return dict(
        c=(c, dict(cm=1)),
        x0=(x0, dict(xm=1)),
        x1=(x1, dict(xm=3)),
        y0=(y0, dict(ym=1)),
        y1=(y1, dict(ym=3)),
    )


def halve(v, st):
    b, k = st
    h = v.shape[0] // 2
    mine = lax.dynamic_slice_in_dim(v, b * h, h, 0)
    other = lax.dynamic_slice_in_dim(v, (1 - b) * h, h, 0)
    return mine + swap(other, **k)


def double(v, st):
    b, k = st
    o = swap(v, **k)
    return jnp.where(b == 0, jnp.concatenate([v, o]), jnp.concatenate([o, v]))


def four(m, *ks):
    p, q, r = (swap(m, **k) for k in ks)
    return (m + p) + (q + r)


def along_z(m):
    m = four(m, dict(zm=1), dict(zm=7), dict(zm=6))
    return m + swap(m, zm=2)


def small_sum(v):
    st = steps()
    m = halve(v, st["c"])
    m = four(m, dict(xm=1), dict(xm=2), dict(xm=3))
    m = four(m, dict(ym=1), dict(ym=2), dict(ym=3))
    m = along_z(m)
    return double(m, st["c"])


ORDERS = (
    ("x0", "x1", "y0", "y1"),
    ("y0", "y1", "x0", "x1"),
    ("x1", "x0", "y1", "y0"),
    ("y1", "y0", "x1", "x0"),
)


def big_sum(v, n):
    st = steps()
    m = halve(v, st["c"])
    h = m.shape[0] // n
    parts = [m[i * h : (i + 1) * h] for i in range(n)]
    for k in range(4):
        parts = [halve(p, st[ORDERS[i][k]]) for i, p in enumerate(parts)]
    m = along_z(jnp.concatenate(parts))
    h = m.shape[0] // n
    parts = [m[i * h : (i + 1) * h] for i in range(n)]
    for k in (3, 2, 1, 0):
        parts = [double(p, st[ORDERS[i][k]]) for i, p in enumerate(parts)]
    return double(jnp.concatenate(parts), st["c"])


FINISH_PAD = 2560
FRONT_PAD = 768


def finish_sum(v):
    return big_sum(v, 2)


def second_sum(fro, fin):
    s = big_sum(jnp.concatenate([fro, fin]), 2)
    return s[:FRONT_PAD], s[FRONT_PAD:]


def front_sum(v):
    return big_sum(v, 1)


def call(kernel, args, outs, name):
    specs, values = [], []
    for a in args:
        if isinstance(a, tuple):
            v, layer = a
            block = (None,) + v.shape[1:]
            zeros = (0,) * (v.ndim - 1)
            specs.append(pl.BlockSpec(block, functools.partial(lambda t, i: t, (layer,) + zeros)))
        else:
            v = a
            if v.dtype == jnp.int32:
                specs.append(pl.BlockSpec(memory_space=pltpu.SMEM))
            else:
                specs.append(
                    pl.BlockSpec(v.shape, functools.partial(lambda t, i: t, (0,) * v.ndim))
                )
        values.append(v)
    out_shape = [jax.ShapeDtypeStruct(s, t) for s, t in outs]
    out_specs = [
        pl.BlockSpec(s, functools.partial(lambda t, i: t, (0,) * len(s))) for s, t in outs
    ]
    return pl.pallas_call(
        kernel,
        grid=(1,),
        in_specs=specs,
        out_specs=out_specs,
        out_shape=out_shape,
        name=name,
        compiler_params=pltpu.CompilerParams(vmem_limit_bytes=48 * 1024 * 1024),
    )(*values)


WIDE = ((D, PTS), F32)
LOW = ((D, PTS), BF)
BY_SLICE = ((HEADS * SLICES, PTS), F32)
BY_HEAD = ((HEADS, PTS), F32)
HIDDEN = ((FF, PTS), BF)
ROW = ((1, D), F32)
FRONT_OUTS = [LOW, WIDE, WIDE, BY_HEAD, BY_SLICE, BY_SLICE, ((160, 128), F32)]
TOKEN_OUTS = [((6, D, SLICES), F32), ((HEADS * SLICES, SLICES), F32)]
BACK_OUTS = [LOW, HIDDEN, WIDE, LOW, ROW, ((128, 128), F32), BY_SLICE]
TOKEN_GRADS = [((HEADS, WIDTH, WIDTH), F32)] * 3
REVERSE_OUTS = TOKEN_GRADS + [LOW, LOW, BY_SLICE, BY_HEAD, ROW]


def body(x, n, up, g1, wx, wf, en, so, wq, wk, wv, wo, g2, w1, w2):
    def lead(l):
        return (g1, (wx, l), (wf, l), (en, l), so)

    def mix(l):
        return ((wq, l), (wk, l), (wv, l))

    x0, a0, xm0, fm0, s0, e0, p0, part = call(
        first_kernel, (n, x, *lead(0)), [WIDE] + FRONT_OUTS, "first"
    )
    numer = small_sum(part)
    tok0, attn0, y0, mid0, b0, u0, hid0, x1, a1, xm1, fm1, s1, e1, p1, part = call(
        middle_kernel,
        (n, numer, x0, p0, *mix(0), (wo, 0), g2, (w1, 0), (w2, 0), *lead(1)),
        TOKEN_OUTS + [LOW, WIDE, LOW, ((FF, PTS), F32), HIDDEN, WIDE] + FRONT_OUTS,
        "middle",
    )
    numer = small_sum(part)
    tok1, attn1, y1, b1, hid1, low1, du1, after1, alow1, dg1, part, dw1 = call(
        turn_kernel,
        (n, numer, x1, p1, *mix(1), (wo, 1), g2, (w1, 1), (w2, 1), up),
        TOKEN_OUTS + [LOW, LOW, HIDDEN] + BACK_OUTS,
        "turn",
    )
    dmix = small_sum(part)
    fin1 = finish_sum(
        call(
            finish_grads_kernel,
            (hid1, low1, b1, du1, y1, alow1, dg1),
            [((FINISH_PAD, D), F32)],
            "finish_grads_1",
        )[0]
    )
    (gq1, gk1, gv1, dx1, df1, dl1, ds1, dn1, low0, du0, after0, alow0, dg0, part, dw0) = call(
        back_kernel,
        (n, dmix, tok1, attn1, *mix(1), dw1, x1, fm1, s1, e1, p1, *lead(1))
        + (after1, mid0, u0, p0, tok0, (wo, 0), g2, (w1, 0), (w2, 0)),
        REVERSE_OUTS + BACK_OUTS,
        "back",
    )
    dmix = small_sum(part)
    fro1 = call(
        front_grads_kernel, (a1, dx1, df1, xm1, dl1, ds1, dn1), [((FRONT_PAD, D), F32)], "front_grads_1"
    )[0]
    fin0 = call(
        finish_grads_kernel,
        (hid0, low0, b0, du0, y0, alow0, dg0),
        [((FINISH_PAD, D), F32)],
        "finish_grads_0",
    )[0]
    fro1, fin0 = second_sum(fro1, fin0)
    gq0, gk0, gv0, dx0, df0, dl0, ds0, dn0, point = call(
        last_kernel,
        (n, dmix, tok0, attn0, *mix(0), dw0, x0, fm0, s0, e0, p0, *lead(0), after0),
        REVERSE_OUTS + [((PTS, D), F32)],
        "last",
    )
    fro0 = front_sum(
        call(
            front_grads_kernel,
            (a0, dx0, df0, xm0, dl0, ds0, dn0),
            [((FRONT_PAD, D), F32)],
            "front_grads_0",
        )[0]
    )
    ln1, gx, gf, ge, gs, go, ln2, gw1, gw2 = call(
        unpack_kernel,
        (fin0, fro0, fin1, fro1),
        [
            (g1.shape, F32), (wx.shape, F32), (wf.shape, F32), (en.shape, F32), (so.shape, F32),
            (wo.shape, F32), (g2.shape, F32), (w1.shape, F32), (w2.shape, F32),
        ],
        "unpack",
    )
    gq, gk, gv = (jnp.stack(p) for p in ((gq0, gq1), (gk0, gk1), (gv0, gv1)))
    return point, ln1, gx, gf, ge, gs, gq, gk, gv, go, ln2, gw1, gw2


def solution(mesh):
    split = P(("row", "col"), None)
    in_specs = (split, P(("row", "col")), split) + (P(),) * 12
    out_specs = (split,) + (P(),) * 12
    return jax.shard_map(body, mesh=mesh, in_specs=in_specs, out_specs=out_specs, check_vma=False)
```

```python
import functools
import math

import jax
import jax.numpy as jnp
from jax import lax
from jax.experimental import pallas as pl
from jax.experimental.pallas import tpu as pltpu
from jax.sharding import PartitionSpec as P

BF = jnp.bfloat16
F32 = jnp.float32
PTS = 256
D = 256
FF = 1024
HEADS = 8
WIDTH = 32
SLICES = 64
PAIRS = HEADS // 2
EPS = 1e-05


def dot(a, b, ca=1, cb=0):
    return lax.dot_general(a, b, (((ca,), (cb,)), ((), ())), preferred_element_type=F32)


def exact(a, b, ca=1, cb=0):
    return lax.dot_general(
        a,
        b,
        (((ca,), (cb,)), ((), ())),
        precision=lax.Precision.HIGH,
        preferred_element_type=F32,
    )


def head(v, h, n=WIDTH):
    return v[h * n : (h + 1) * n]


def stack(pieces):
    return jnp.concatenate(pieces, axis=0)


def iota(shape, axis):
    return lax.broadcasted_iota(jnp.int32, shape, axis)


def column(row):
    return jnp.transpose(jnp.broadcast_to(row, (PTS, D)))


def row_sum(v):
    return jnp.sum(jnp.transpose(v), axis=0, keepdims=True)


def normed(x):
    c = x - jnp.mean(x, axis=0, keepdims=True)
    r = lax.rsqrt(jnp.mean(c * c, axis=0, keepdims=True) + EPS)
    return c * r, r


def norm_back(xhat, r, gain, g):
    dh = g * gain
    return r * (
        dh
        - jnp.mean(dh, axis=0, keepdims=True)
        - xhat * jnp.mean(dh * xhat, axis=0, keepdims=True)
    )


def live_rows(n):
    keep = (iota((8, PTS), 0) == 0) & (iota((8, PTS), 1) < n)
    return jnp.where(keep, 1.0, 0.0)


def softness_rows(s):
    wide = jnp.concatenate([s] * HEADS, axis=1)
    return jnp.where((iota((HEADS, D), 1) >> 5) == iota((HEADS, D), 0), wide, 0.0)


def block_diagonal(w):
    wide = jnp.concatenate([w.reshape(D, WIDTH)] * HEADS, axis=1)
    return jnp.where((iota((D, D), 0) >> 5) == (iota((D, D), 1) >> 5), wide, 0.0)


def pair_rows(r):
    return jnp.where(iota((WIDTH, 128), 1) < SLICES, r[:WIDTH], r[WIDTH : 2 * WIDTH])


def front(x, gain, wx, wf, energy, softness, live8):
    xhat, _ = normed(x)
    a = (xhat * gain).astype(BF)
    xm = dot(wx, a, 0, 0)
    fm = dot(wf, a, 0, 0)
    s = exact(softness_rows(softness), xm)
    temp = 0.5 + jnp.maximum(s, 0.0) + jnp.log1p(jnp.exp(-jnp.abs(s)))
    es, ws = [], []
    for h in range(HEADS):
        e = exact(energy[h], head(xm, h), 0, 0) / temp[h : h + 1]
        p = jnp.exp(e - jnp.max(e, axis=0, keepdims=True))
        es.append(e)
        ws.append(p / jnp.sum(p, axis=0, keepdims=True))
    w = stack(ws)
    masked = fm * live8[:1]
    rows = []
    for j in range(PAIRS):
        r = exact(stack([head(masked, j, 64), live8]), head(w, j, 128), 1, 1)
        rows += [pair_rows(r), r[64:72]]
    return a, xm, fm, s, stack(es), w, stack(rows)


def token_mix(numer, wq, wk, wv):
    toks, invs = [], []
    for j in range(PAIRS):
        inv = 1.0 / (numer[40 * j + 32 : 40 * j + 33] + EPS)
        t = numer[40 * j : 40 * j + 32] / (numer[40 * j + 32 : 40 * j + 33] + EPS)
        inv = jnp.broadcast_to(inv, (WIDTH, 128))
        toks += [t[:, :SLICES], t[:, SLICES:]]
        invs += [inv[:, :SLICES], inv[:, SLICES:]]
    tok = stack(toks)
    q, k, v = (exact(block_diagonal(w), tok, 0, 0) for w in (wq, wk, wv))
    attns, mixes = [], []
    for h in range(HEADS):
        sc = exact(head(k, h), head(q, h), 0, 0) * (1.0 / math.sqrt(WIDTH))
        p = jnp.exp(sc - jnp.max(sc, axis=0, keepdims=True))
        attn = p / jnp.sum(p, axis=0, keepdims=True)
        attns.append(attn)
        mixes.append(exact(head(v, h), attn))
    return (tok, q, k, v, stack(invs), stack(mixes)), stack(attns)


def token_back(dmix, toks, attn, wq, wk, wv):
    tok, q, k, v, inv = (toks[i] for i in range(5))
    dqs, dks, dvs = [], [], []
    for h in range(HEADS):
        at, dm = head(attn, h, SLICES), head(dmix, h)
        dvs.append(exact(dm, at, 1, 1))
        da = exact(head(v, h), dm, 0, 0)
        ds = at * (da - jnp.sum(at * da, axis=0, keepdims=True)) * (1.0 / math.sqrt(WIDTH))
        dqs.append(exact(head(k, h), ds))
        dks.append(exact(head(q, h), ds, 1, 1))
    dq, dk, dv = stack(dqs), stack(dks), stack(dvs)
    dtok = exact(block_diagonal(wq), dq) + exact(block_diagonal(wk), dk)
    dtok = dtok + exact(block_diagonal(wv), dv)
    dnumer = dtok * inv
    return dnumer, dnumer * tok, (dq, dk, dv)


def finish(x, w, mixed, wo, gain, w1):
    y = stack([exact(head(mixed, h), head(w, h, SLICES)) for h in range(HEADS)]).astype(BF)
    x1 = x + dot(wo, y, 0, 0)
    xhat, _ = normed(x1)
    b = (xhat * gain).astype(BF)
    return y, x1, b, dot(w1, b, 0, 0)


C0 = math.sqrt(2.0 / math.pi)
C1 = 0.044715


def gelu(u):
    return 0.5 * u * (1.0 + jnp.tanh(C0 * (u + C1 * (u * u * u))))


def gelu_slope(u):
    t = jnp.tanh(C0 * (u + C1 * (u * u * u)))
    return 0.5 * (1.0 + t) + 0.5 * u * (1.0 - t * t) * (C0 * (1.0 + 3.0 * C1 * (u * u)))


def finish_back(up, x1, u, w, mixed, wo, gain, w1, w2):
    low = up.astype(BF)
    du = (dot(w2, low) * gelu_slope(u)).astype(BF)
    db = dot(w1, du)
    xhat, r = normed(x1)
    dgain = row_sum(db * xhat)
    after = norm_back(xhat, r, gain, db) + up
    after_low = after.astype(BF)
    dy = dot(wo, after_low)
    dmix = stack(
        [
            pair_rows(exact(head(dy, j, 64), head(w, j, 128), 1, 1))
            for j in range(PAIRS)
        ]
    )
    dw = stack([exact(head(mixed, h), head(dy, h), 0, 0) for h in range(HEADS)])
    return low, du, after, after_low, dgain, dw, dmix


def unpair(v):
    out = []
    for j in range(PAIRS):
        blk = head(v, j)
        out += [blk[:, :SLICES], blk[:, SLICES:]]
    return stack(out)


def front_back(dnumer, share, dw, x, gain, fm, s, e, w, wx, wf, energy, softness, live8):
    live = live8[:1]
    masked = fm * live
    temp = 0.5 + jnp.maximum(s, 0.0) + jnp.log1p(jnp.exp(-jnp.abs(s)))
    inv_temp = 1.0 / temp
    first = iota((8, SLICES), 0) == 0
    dls, dts, dfs, dxs = [], [], [], []
    for h in range(HEADS):
        dn, wh = head(dnumer, h), head(w, h, SLICES)
        dtot = jnp.where(first, -jnp.sum(head(share, h), axis=0, keepdims=True), 0.0)
        dwh = head(dw, h, SLICES) + exact(
            stack([dn, dtot]), stack([head(masked, h), live8]), 0, 0
        )
        de = wh * (dwh - jnp.sum(wh * dwh, axis=0, keepdims=True))
        dl = de * inv_temp[h : h + 1]
        dts.append(-jnp.sum(dl * head(e, h, SLICES), axis=0, keepdims=True))
        dls.append(dl)
        dfs.append(exact(dn, wh))
        dxs.append(exact(energy[h], dl))
    ds = stack(dts) / (1.0 + jnp.exp(-s))
    dx = (stack(dxs) + exact(softness_rows(softness), ds, 0, 0)).astype(BF)
    df = (stack(dfs) * live).astype(BF)
    da = dot(wx, dx) + dot(wf, df)
    xhat, r = normed(x)
    return dx, df, stack(dls), ds, norm_back(xhat, r, gain, da), row_sum(da * xhat)


def core_index():
    return lax.rem(lax.axis_index("row"), 2)


def put_halves(v, mine, other):
    h = v.shape[0] // 2
    zero = core_index() == 0
    mine[...] = jnp.where(zero, v[:h], v[h:])
    other[...] = jnp.where(zero, v[h:], v[:h])


def join_halves(mine, other):
    zero = core_index() == 0
    return stack([jnp.where(zero, mine, other), jnp.where(zero, other, mine)])


def put(refs, values):
    for ref, value in zip(refs, values):
        ref[...] = value


def first_kernel(n, x, g1, wx, wf, en, so, xt, *out):
    v = jnp.transpose(x[...].astype(F32))
    xt[...] = v
    r = front(v, column(g1[0:1]), wx[...], wf[...], en[...], so[0], live_rows(n[0]))
    put(out, r[:6])
    put_halves(r[6], *out[6:])


def save_tokens(toks, attn, tok_ref, attn_ref):
    for i, t in enumerate(toks):
        tok_ref[i] = t
    attn_ref[...] = attn


def middle_kernel(
    n, numer, numer_o, x, w, wq, wk, wv, wo, g2, w1, w2, g1, wx, wf, en, so,
    tok_ref, attn_ref, y_ref, x1_ref, b_ref, u_ref, hid_ref, xt, *out
):
    toks, attn = token_mix(join_halves(numer[...], numer_o[...]), wq[...], wk[...], wv[...])
    save_tokens(toks, attn, tok_ref, attn_ref)
    y, x1, b, u = finish(x[...], w[...], toks[5], wo[...], column(g2[0:1]), w1[...])
    hid = gelu(u).astype(BF)
    put((y_ref, x1_ref, b_ref, u_ref, hid_ref), (y, x1, b, u, hid))
    v = x1 + dot(w2[...], hid, 0, 0)
    xt[...] = v
    r = front(v, column(g1[1:2]), wx[...], wf[...], en[...], so[1], live_rows(n[0]))
    put(out, r[:6])
    put_halves(r[6], *out[6:])


def turn_kernel(
    n, numer, numer_o, x, w, wq, wk, wv, wo, g2, w1, w2, up,
    tok_ref, attn_ref, y_ref, b_ref, hid_ref, *out
):
    toks, attn = token_mix(join_halves(numer[...], numer_o[...]), wq[...], wk[...], wv[...])
    save_tokens(toks, attn, tok_ref, attn_ref)
    gain = column(g2[1:2])
    y, x1, b, u = finish(x[...], w[...], toks[5], wo[...], gain, w1[...])
    put((y_ref, b_ref, hid_ref), (y, b, gelu(u).astype(BF)))
    upt = jnp.transpose(up[...].astype(F32)) * live_rows(n[0])[:1]
    r = finish_back(upt, x1, u, w[...], toks[5], wo[...], gain, w1[...], w2[...])
    put(out, r[:6])
    put_halves(r[6], *out[6:])


def token_grads(tok, dqkv, refs):
    for ref, d in zip(refs, dqkv):
        for h in range(HEADS):
            ref[h] = exact(head(tok, h), head(d, h), 1, 1)


def reverse(layer, n, dmix, dmix_o, tok_ref, attn, wq, wk, wv, dw, x, fm, s, e, w, g1, wx, wf, en, so):
    dnumer, share, dqkv = token_back(
        unpair(join_halves(dmix[...], dmix_o[...])), tok_ref, attn[...], wq[...], wk[...], wv[...]
    )
    out = front_back(
        dnumer, share, dw[...], x[...], column(g1[layer : layer + 1]), fm[...], s[...],
        e[...], w[...], wx[...], wf[...], en[...], so[layer], live_rows(n[0]),
    )
    return out, dqkv


def back_kernel(
    n, dmix, dmix_o, tok_ref, attn, wq, wk, wv, dw, x, fm, s, e, w, g1, wx, wf, en, so,
    after, x1, u, w_below, tok_below, wo, g2, w1, w2,
    dwq, dwk, dwv, dx, df, dl, ds, dg, *out
):
    r, dqkv = reverse(1, n, dmix, dmix_o, tok_ref, attn, wq, wk, wv, dw, x, fm, s, e, w, g1, wx, wf, en, so)
    put((dx, df, dl, ds), r[:4])
    dg[...] = r[5]
    up = after[...] + r[4]
    r = finish_back(
        up, x1[...], u[...], w_below[...], tok_below[5], wo[...], column(g2[0:1]),
        w1[...], w2[...],
    )
    put(out, r[:6])
    put_halves(r[6], *out[6:])
    token_grads(tok_ref[0], dqkv, (dwq, dwk, dwv))


def last_kernel(
    n, dmix, dmix_o, tok_ref, attn, wq, wk, wv, dw, x, fm, s, e, w, g1, wx, wf, en, so,
    after, a, xm, dwq, dwk, dwv, point, mine, other, dx, df, dl, ds, dg
):
    r, dqkv = reverse(
        0, n, dmix, dmix_o, tok_ref, attn, wq, wk, wv, dw, x, fm, s, e, w, g1, wx, wf, en, so
    )
    put((dx, df, dl, ds), r[:4])
    dg[...] = r[5]
    both(front_half, (a, dx, df, xm, dl, ds, dg), mine, other, 0)
    clear(FRONT_HALF, mine, other)
    point[...] = jnp.transpose(after[...] + r[4])
    token_grads(tok_ref[0], dqkv, (dwq, dwk, dwv))


def first_row(v):
    return jnp.where(iota((8, D), 0) == 0, v, 0.0)


FINISH_HALF = 1160
FRONT_HALF = 296


def finish_half(c, hid, up, b, du, y, after, dg, out, at):
    out[at : at + 512] = dot(hid[pl.ds(c * 512, 512)], up[...], 1, 1)
    for k in range(2):
        t = dot(b[...], du[pl.ds(c * 512 + 256 * k, 256)], 1, 1)
        out[at + 512 + 256 * k : at + 768 + 256 * k] = t
    out[at + 1024 : at + 1152] = dot(y[pl.ds(c * 128, 128)], after[...], 1, 1)
    out[at + 1152 : at + 1160] = first_row(dg[...])


def front_half(c, a, dx, df, xm, dl, ds, dg, out, at):
    rows = a[pl.ds(c * 128, 128)]
    out[at : at + 128] = dot(rows, dx[...], 1, 1)
    out[at + 128 : at + 256] = dot(rows, df[...], 1, 1)
    for j in range(2):
        r = exact(xm[pl.ds(c * 128 + 64 * j, 64)], dl[pl.ds(c * 256 + 128 * j, 128)], 1, 1)
        out[at + 256 : at + 288, 128 * j : 128 * (j + 1)] = pair_rows(r)
    t = exact(ds[...], xm[...], 1, 1)
    t = jnp.where((iota((HEADS, D), 1) >> 5) == iota((HEADS, D), 0), t, 0.0)
    t = jnp.sum(t, axis=0, keepdims=True)
    out[at + 288 : at + 296] = first_row(dg[...]) + jnp.where(iota((8, D), 0) == 1, t, 0.0)


def both(half, refs, mine, other, at):
    c = core_index()
    half(c, *refs, mine, at)
    half(1 - c, *refs, other, at)


def clear(rows, *outs):
    for out in outs:
        out[rows:] = jnp.zeros((out.shape[0] - rows, D), F32)


def finish_grads_kernel(*refs):
    both(finish_half, refs[:7], *refs[7:], 0)
    clear(FINISH_HALF, *refs[7:])


def second_grads_kernel(*refs):
    both(finish_half, refs[:7], *refs[14:], 0)
    both(front_half, refs[7:14], *refs[14:], FINISH_HALF)
    clear(FINISH_HALF + FRONT_HALF, *refs[14:])


def ordered(mine, other, out):
    r, h = mine.shape[1], out.shape[1]
    zero = core_index() == 0
    for q in range(16):
        at = place(q, h)
        m, o = mine[q], other[q]
        out[0, at : at + r] = jnp.where(zero, m, o)
        out[1, at : at + r] = jnp.where(zero, o, m)


def unpack_kernel(
    fin, fin_o, sec, sec_o, fro, fro_o,
    ln1, gx, gf, ge, gs, go, ln2, g1, g2, one, two, three
):
    ordered(fin, fin_o, one)
    ordered(sec, sec_o, two)
    zero = core_index() == 0
    m, o = fro[...], fro_o[...]
    three[0] = jnp.where(zero, m, o)
    three[1] = jnp.where(zero, o, m)
    for l, (fin, fro, at) in enumerate(((two, three, 0), (one, two, FINISH_HALF))):
        for c in range(2):
            g2[l, 512 * c : 512 * (c + 1)] = fin[c, 0:512]
            for k in range(2):
                lane = 512 * c + 256 * k
                g1[l, :, lane : lane + 256] = fin[c, 512 + 256 * k : 768 + 256 * k]
            go[l, 128 * c : 128 * (c + 1)] = fin[c, 1024:1152]
            gx[l, 128 * c : 128 * (c + 1)] = fro[c, at : at + 128]
            gf[l, 128 * c : 128 * (c + 1)] = fro[c, at + 128 : at + 256]
            for h in range(4):
                t = fro[c, at + 256 : at + 288, 128 * (h // 2) : 128 * (h // 2 + 1)]
                ge[l, 4 * c + h] = t[:, 64 * (h % 2) : 64 * (h % 2 + 1)]
        ln2[l : l + 1] = fin[0, 1152:1153]
        ln1[l : l + 1] = fro[0, at + 288 : at + 289]
        for h in range(HEADS):
            gs[l, h : h + 1] = fro[0, at + 289 : at + 290, 32 * h : 32 * (h + 1)]


AXES = ("row", "col")


def linear(z, c, y, x):
    return (z * 2 + c) * 16 + y * 4 + x


def swap(v, zm=0, cm=0, ym=0, xm=0):
    pairs = [
        (linear(z, c, y, x), linear(z ^ zm, c ^ cm, y ^ ym, x ^ xm))
        for z in range(8)
        for c in range(2)
        for y in range(4)
        for x in range(4)
    ]
    return lax.ppermute(v, AXES, pairs)


def coords():
    r = lax.axis_index("row")
    q = lax.axis_index("col")
    return r // 2, r % 2, q // 4, q % 4


def gray(v):
    return ((v ^ (v >> 1)) & 1, v >> 1)


def halves(v, b):
    h = v.shape[0] // 2
    return (
        lax.dynamic_slice_in_dim(v, b * h, h, 0),
        lax.dynamic_slice_in_dim(v, (1 - b) * h, h, 0),
    )


CORE = dict(cm=1)
ALONG_X = (dict(xm=1), dict(xm=2), dict(xm=3))
ALONG_Y = (dict(ym=1), dict(ym=2), dict(ym=3))
NEAR_Z = (dict(zm=1), dict(zm=7), dict(zm=6))


def all_to(v, partners):
    return [(v, k) for k in partners]


def four(v, got):
    return (v + got[0]) + (got[1] + got[2])


def small_sum(mine, other):
    m = mine + (yield [(other, CORE)])[0]
    m = four(m, (yield all_to(m, ALONG_X)))
    m = four(m, (yield all_to(m, ALONG_Y)))
    m = four(m, (yield all_to(m, NEAR_Z)))
    m = m + (yield [(m, dict(zm=2))])[0]
    return m, (yield [(m, CORE)])[0]


def place(q, rows):
    (x0, x1), (y0, y1) = gray(q % 4), gray(q // 4)
    index = x0 * 2 + x1 if y0 == 0 else x1 * 2 + x0
    return y0 * rows // 2 + index * rows // 8 + y1 * rows // 16


def scatter_sum(mine, other):
    z, c, y, x = coords()
    (x0, x1), (y0, y1) = gray(x), gray(y)
    m = mine + (yield [(other, CORE)])[0]
    h = m.shape[0] // 2
    parts = [m[:h], m[h:]]
    for first, second in (((x0, 1), (x1, 3)), ((x1, 3), (x0, 1))):
        cut = [halves(parts[0], first[0]), halves(parts[1], second[0])]
        got = yield [(cut[0][1], dict(xm=first[1])), (cut[1][1], dict(xm=second[1]))]
        parts = [keep + g for (keep, _), g in zip(cut, got)]
    m = jnp.concatenate(parts)
    for bit, ym in ((y0, 1), (y1, 3)):
        keep, o = halves(m, bit)
        m = keep + (yield [(o, dict(ym=ym))])[0]
    for zm in (1, 2, 7):
        m = m + (yield [(m, dict(zm=zm))])[0]
    return m


def gather(m):
    return lax.all_gather(m, "col")


def take(v, i):
    return lax.dynamic_index_in_dim(v, i, 0, keepdims=False)


def in_order(v, got, i):
    t = [v] + list(got)
    odd = [t[1], t[0], t[3], t[2]]
    t = [jnp.where(i & 1 == 1, b, a) for a, b in zip(t, odd)]
    return jnp.concatenate(
        [jnp.where(i & 2 == 2, b, a) for a, b in zip(t, (t[2], t[3], t[0], t[1]))]
    )


def mid_sum(mine, other):
    z, c, y, x = coords()
    m = mine + (yield [(other, CORE)])[0]
    for i, along in ((x, ALONG_X), (y, ALONG_Y)):
        t = m.reshape(4, -1, m.shape[-1])
        got = yield [(take(t, i ^ (k + 1)), partner) for k, partner in enumerate(along)]
        m = four(take(t, i), got)
    m = four(m, (yield all_to(m, NEAR_Z)))
    m = m + (yield [(m, dict(zm=2))])[0]
    for i, along in ((y, ALONG_Y), (x, ALONG_X)):
        m = in_order(m, (yield all_to(m, along)), i)
    return m, (yield [(m, CORE)])[0]


class Sum:
    def __init__(self, steps_of):
        self.steps_of = steps_of
        self.wanted = next(steps_of)
        self.value = None
        self.done = False

    def send(self, got):
        try:
            self.wanted = self.steps_of.send(got)
        except StopIteration as end:
            self.value, self.done = end.value, True


def phase(sums, *beside):
    sums = [s for s in sums if not s.done]
    moved = [[swap(v, **k) for v, k in s.wanted] for s in sums]
    moved, beside = lax.optimization_barrier((moved, beside))
    for s, got in zip(sums, moved):
        s.send(got)
    return beside


def call(kernel, args, outs, name, scratch=(), cost=None):
    specs, values = [], []
    for a in args:
        if isinstance(a, tuple):
            v, layer = a
            block = (None,) + v.shape[1:]
            zeros = (0,) * (v.ndim - 1)
            specs.append(pl.BlockSpec(block, functools.partial(lambda t, i: t, (layer,) + zeros)))
        else:
            v = a
            if v.dtype == jnp.int32:
                specs.append(pl.BlockSpec(memory_space=pltpu.SMEM))
            else:
                specs.append(
                    pl.BlockSpec(v.shape, functools.partial(lambda t, i: t, (0,) * v.ndim))
                )
        values.append(v)
    out_shape = [jax.ShapeDtypeStruct(s, t) for s, t in outs]
    out_specs = [
        pl.BlockSpec(s, functools.partial(lambda t, i: t, (0,) * len(s))) for s, t in outs
    ]
    return pl.pallas_call(
        kernel,
        grid=(1,),
        in_specs=specs,
        out_specs=out_specs,
        out_shape=out_shape,
        scratch_shapes=list(scratch),
        cost_estimate=cost,
        name=name,
        compiler_params=pltpu.CompilerParams(vmem_limit_bytes=63 * 1024 * 1024),
    )(*values)


WIDE = ((D, PTS), F32)
LOW = ((D, PTS), BF)
BY_SLICE = ((HEADS * SLICES, PTS), F32)
BY_HEAD = ((HEADS, PTS), F32)
HIDDEN = ((FF, PTS), BF)
ROW = ((1, D), F32)
FRONT_OUTS = [LOW, WIDE, WIDE, BY_HEAD, BY_SLICE, BY_SLICE] + [((80, 128), F32)] * 2
TOKEN_OUTS = [((6, D, SLICES), F32), ((HEADS * SLICES, SLICES), F32)]
BACK_OUTS = [LOW, HIDDEN, WIDE, LOW, ROW, BY_SLICE] + [((64, 128), F32)] * 2
TOKEN_GRADS = [((HEADS, WIDTH, WIDTH), F32)] * 3
REVERSE_OUTS = TOKEN_GRADS + [LOW, LOW, BY_SLICE, BY_HEAD, ROW]


FINISH_PAD = 1280
SECOND_PAD = 1536
FRONT_PAD = 384


def cost(flops, nbytes):
    return pl.CostEstimate(flops=flops, bytes_accessed=nbytes, transcendentals=0)


def body(x, n, up, g1, wx, wf, en, so, wq, wk, wv, wo, g2, w1, w2):
    def lead(l):
        return (g1, (wx, l), (wf, l), (en, l), so)

    def mix(l):
        return ((wq, l), (wk, l), (wv, l))

    def total(*part):
        s = Sum(small_sum(*part))
        while not s.done:
            phase([s])
        return s.value

    x0, a0, xm0, fm0, s0, e0, p0, mine, other = call(
        first_kernel, (n, x, *lead(0)), [WIDE] + FRONT_OUTS, "first"
    )
    numer = total(mine, other)
    tok0, attn0, y0, mid0, b0, u0, hid0, x1, a1, xm1, fm1, s1, e1, p1, mine, other = call(
        middle_kernel,
        (n, *numer, x0, p0, *mix(0), (wo, 0), g2, (w1, 0), (w2, 0), *lead(1)),
        TOKEN_OUTS + [LOW, WIDE, LOW, ((FF, PTS), F32), HIDDEN, WIDE] + FRONT_OUTS,
        "middle",
    )
    numer = total(mine, other)
    tok1, attn1, y1, b1, hid1, low1, du1, after1, alow1, dg1, dw1, mine, other = call(
        turn_kernel,
        (n, *numer, x1, p1, *mix(1), (wo, 1), g2, (w1, 1), (w2, 1), up),
        TOKEN_OUTS + [LOW, LOW, HIDDEN] + BACK_OUTS,
        "turn",
    )
    small = Sum(small_sum(mine, other))
    held = phase([small], hid1, low1, b1, du1, y1, alow1, dg1)
    halves1 = call(
        finish_grads_kernel, held, [((FINISH_PAD, D), F32)] * 2, "finish_grads",
        cost=cost(310000000, 4500000),
    )
    halves1 = phase([small], *halves1)
    finish1 = Sum(scatter_sum(*halves1))
    for _ in range(3):
        phase([small, finish1])
    phase([small])
    dmix = small.value
    (gq1, gk1, gv1, dx1, df1, dl1, ds1, dn1, low0, du0, after0, alow0, dg0, dw0, mine, other) = call(
        back_kernel,
        (n, *dmix, tok1, attn1, *mix(1), dw1, x1, fm1, s1, e1, p1, *lead(1))
        + (after1, mid0, u0, p0, tok0, (wo, 0), g2, (w1, 0), (w2, 0)),
        REVERSE_OUTS + BACK_OUTS,
        "back",
        cost=cost(2000000000, 8000000),
    )
    mine, other = phase([finish1], mine, other)
    small = Sum(small_sum(mine, other))
    held = phase(
        [small], hid0, low0, b0, du0, y0, alow0, dg0, a1, dx1, df1, xm1, dl1, ds1, dn1
    )
    halves0 = call(
        second_grads_kernel, held, [((SECOND_PAD, D), F32)] * 2, "second_grads",
        cost=cost(600000000, 6000000),
    )
    halves0 = phase([small, finish1], *halves0)
    second = Sum(scatter_sum(*halves0))
    for _ in range(3):
        phase([small, second, finish1])
    fin1 = gather(finish1.value)
    phase([small])
    dmix = small.value
    gq0, gk0, gv0, point, mine, other = call(
        last_kernel,
        (n, *dmix, tok0, attn0, *mix(0), dw0, x0, fm0, s0, e0, p0, *lead(0), after0, a0, xm0),
        TOKEN_GRADS + [((PTS, D), F32)] + [((FRONT_PAD, D), F32)] * 2,
        "last",
        scratch=[pltpu.VMEM(s, t) for s, t in (LOW, LOW, BY_SLICE, BY_HEAD, ROW)],
        cost=cost(2000000000, 6000000),
    )
    mine, other = phase([second], mine, other)
    front0 = Sum(mid_sum(mine, other))
    for _ in range(4):
        phase([front0, second])
    sec = gather(second.value)
    phase([front0])
    (fin1,) = phase([front0], fin1)
    fin1_o = swap(fin1, **CORE)
    fin1_o, sec = phase([front0], fin1_o, sec)
    phase([front0])
    sec_o = swap(sec, **CORE)
    ln1, gx, gf, ge, gs, go, ln2, gw1, gw2 = call(
        unpack_kernel,
        (fin1, fin1_o, sec, sec_o, *front0.value),
        [
            (g1.shape, F32), (wx.shape, F32), (wf.shape, F32), (en.shape, F32), (so.shape, F32),
            (wo.shape, F32), (g2.shape, F32), (w1.shape, F32), (w2.shape, F32),
        ],
        "unpack",
        scratch=[pltpu.VMEM((2, r, D), F32) for r in (FINISH_PAD, SECOND_PAD, FRONT_PAD)],
    )
    gq, gk, gv = (jnp.stack(p) for p in ((gq0, gq1), (gk0, gk1), (gv0, gv1)))
    return point, ln1, gx, gf, ge, gs, gq, gk, gv, go, ln2, gw1, gw2


def solution(mesh):
    split = P(("row", "col"), None)
    in_specs = (split, P(("row", "col")), split) + (P(),) * 12
    out_specs = (split,) + (P(),) * 12
    return jax.shard_map(body, mesh=mesh, in_specs=in_specs, out_specs=out_specs, check_vma=False)
```

```python
import functools
import math

import jax
import jax.numpy as jnp
from jax import lax
from jax.experimental import pallas as pl
from jax.experimental.pallas import tpu as pltpu
from jax.sharding import PartitionSpec as P

BF = jnp.bfloat16
F32 = jnp.float32
PTS = 256
D = 256
FF = 1024
HEADS = 8
WIDTH = 32
SLICES = 64
PAIRS = HEADS // 2
EPS = 1e-05


def dot(a, b, ca=1, cb=0):
    return lax.dot_general(a, b, (((ca,), (cb,)), ((), ())), preferred_element_type=F32)


def exact(a, b, ca=1, cb=0):
    return lax.dot_general(
        a,
        b,
        (((ca,), (cb,)), ((), ())),
        precision=lax.Precision.HIGH,
        preferred_element_type=F32,
    )


def head(v, h, n=WIDTH):
    return v[h * n : (h + 1) * n]


def stack(pieces):
    return jnp.concatenate(pieces, axis=0)


def iota(shape, axis):
    return lax.broadcasted_iota(jnp.int32, shape, axis)


def column(row):
    return jnp.transpose(jnp.broadcast_to(row, (PTS, D)))


def row_sum(v):
    return jnp.sum(jnp.transpose(v), axis=0, keepdims=True)


def normed(x):
    c = x - jnp.mean(x, axis=0, keepdims=True)
    r = lax.rsqrt(jnp.mean(c * c, axis=0, keepdims=True) + EPS)
    return c * r, r


def norm_back(xhat, r, gain, g):
    dh = g * gain
    return r * (
        dh
        - jnp.mean(dh, axis=0, keepdims=True)
        - xhat * jnp.mean(dh * xhat, axis=0, keepdims=True)
    )


def live_rows(n):
    keep = (iota((8, PTS), 0) == 0) & (iota((8, PTS), 1) < n)
    return jnp.where(keep, 1.0, 0.0)


def softness_rows(s):
    wide = jnp.concatenate([s] * HEADS, axis=1)
    return jnp.where((iota((HEADS, D), 1) >> 5) == iota((HEADS, D), 0), wide, 0.0)


def block_diagonal(w):
    wide = jnp.concatenate([w.reshape(D, WIDTH)] * HEADS, axis=1)
    return jnp.where((iota((D, D), 0) >> 5) == (iota((D, D), 1) >> 5), wide, 0.0)


def pair_rows(r):
    return jnp.where(iota((WIDTH, 128), 1) < SLICES, r[:WIDTH], r[WIDTH : 2 * WIDTH])


def front(x, gain, wx, wf, energy, softness, live8):
    xhat, _ = normed(x)
    a = (xhat * gain).astype(BF)
    xm = dot(wx, a, 0, 0)
    fm = dot(wf, a, 0, 0)
    s = exact(softness_rows(softness), xm)
    temp = 0.5 + jnp.maximum(s, 0.0) + jnp.log1p(jnp.exp(-jnp.abs(s)))
    es, ws = [], []
    for h in range(HEADS):
        e = exact(energy[h], head(xm, h), 0, 0) / temp[h : h + 1]
        p = jnp.exp(e - jnp.max(e, axis=0, keepdims=True))
        es.append(e)
        ws.append(p / jnp.sum(p, axis=0, keepdims=True))
    w = stack(ws)
    masked = fm * live8[:1]
    rows = []
    for j in range(PAIRS):
        r = exact(stack([head(masked, j, 64), live8]), head(w, j, 128), 1, 1)
        rows += [pair_rows(r), r[64:72]]
    return a, xm, fm, s, stack(es), w, stack(rows)


def token_mix(numer, wq, wk, wv):
    toks, invs = [], []
    for j in range(PAIRS):
        inv = 1.0 / (numer[40 * j + 32 : 40 * j + 33] + EPS)
        t = numer[40 * j : 40 * j + 32] / (numer[40 * j + 32 : 40 * j + 33] + EPS)
        inv = jnp.broadcast_to(inv, (WIDTH, 128))
        toks += [t[:, :SLICES], t[:, SLICES:]]
        invs += [inv[:, :SLICES], inv[:, SLICES:]]
    tok = stack(toks)
    q, k, v = (exact(block_diagonal(w), tok, 0, 0) for w in (wq, wk, wv))
    attns, mixes = [], []
    for h in range(HEADS):
        sc = exact(head(k, h), head(q, h), 0, 0) * (1.0 / math.sqrt(WIDTH))
        p = jnp.exp(sc - jnp.max(sc, axis=0, keepdims=True))
        attn = p / jnp.sum(p, axis=0, keepdims=True)
        attns.append(attn)
        mixes.append(exact(head(v, h), attn))
    return (tok, q, k, v, stack(invs), stack(mixes)), stack(attns)


def token_back(dmix, toks, attn, wq, wk, wv):
    tok, q, k, v, inv = (toks[i] for i in range(5))
    dqs, dks, dvs = [], [], []
    for h in range(HEADS):
        at, dm = head(attn, h, SLICES), head(dmix, h)
        dvs.append(exact(dm, at, 1, 1))
        da = exact(head(v, h), dm, 0, 0)
        ds = at * (da - jnp.sum(at * da, axis=0, keepdims=True)) * (1.0 / math.sqrt(WIDTH))
        dqs.append(exact(head(k, h), ds))
        dks.append(exact(head(q, h), ds, 1, 1))
    dq, dk, dv = stack(dqs), stack(dks), stack(dvs)
    dtok = exact(block_diagonal(wq), dq) + exact(block_diagonal(wk), dk)
    dtok = dtok + exact(block_diagonal(wv), dv)
    dnumer = dtok * inv
    return dnumer, dnumer * tok, (dq, dk, dv)


def finish(x, w, mixed, wo, gain, w1):
    y = stack([exact(head(mixed, h), head(w, h, SLICES)) for h in range(HEADS)]).astype(BF)
    x1 = x + dot(wo, y, 0, 0)
    xhat, _ = normed(x1)
    b = (xhat * gain).astype(BF)
    return y, x1, b, dot(w1, b, 0, 0)


C0 = math.sqrt(2.0 / math.pi)
C1 = 0.044715


def gelu(u):
    return 0.5 * u * (1.0 + jnp.tanh(C0 * (u + C1 * (u * u * u))))


def gelu_slope(u):
    t = jnp.tanh(C0 * (u + C1 * (u * u * u)))
    return 0.5 * (1.0 + t) + 0.5 * u * (1.0 - t * t) * (C0 * (1.0 + 3.0 * C1 * (u * u)))


def finish_back(up, x1, u, w, mixed, wo, gain, w1, w2):
    low = up.astype(BF)
    du = (dot(w2, low) * gelu_slope(u)).astype(BF)
    db = dot(w1, du)
    xhat, r = normed(x1)
    dgain = row_sum(db * xhat)
    after = norm_back(xhat, r, gain, db) + up
    after_low = after.astype(BF)
    dy = dot(wo, after_low)
    dmix = stack(
        [
            pair_rows(exact(head(dy, j, 64), head(w, j, 128), 1, 1))
            for j in range(PAIRS)
        ]
    )
    dw = stack([exact(head(mixed, h), head(dy, h), 0, 0) for h in range(HEADS)])
    return low, du, after, after_low, dgain, dw, dmix


def unpair(v):
    out = []
    for j in range(PAIRS):
        blk = head(v, j)
        out += [blk[:, :SLICES], blk[:, SLICES:]]
    return stack(out)


def front_back(dnumer, share, dw, x, gain, fm, s, e, w, wx, wf, energy, softness, live8):
    live = live8[:1]
    masked = fm * live
    temp = 0.5 + jnp.maximum(s, 0.0) + jnp.log1p(jnp.exp(-jnp.abs(s)))
    inv_temp = 1.0 / temp
    first = iota((8, SLICES), 0) == 0
    dls, dts, dfs, dxs = [], [], [], []
    for h in range(HEADS):
        dn, wh = head(dnumer, h), head(w, h, SLICES)
        dtot = jnp.where(first, -jnp.sum(head(share, h), axis=0, keepdims=True), 0.0)
        dwh = head(dw, h, SLICES) + exact(
            stack([dn, dtot]), stack([head(masked, h), live8]), 0, 0
        )
        de = wh * (dwh - jnp.sum(wh * dwh, axis=0, keepdims=True))
        dl = de * inv_temp[h : h + 1]
        dts.append(-jnp.sum(dl * head(e, h, SLICES), axis=0, keepdims=True))
        dls.append(dl)
        dfs.append(exact(dn, wh))
        dxs.append(exact(energy[h], dl))
    ds = stack(dts) / (1.0 + jnp.exp(-s))
    dx = (stack(dxs) + exact(softness_rows(softness), ds, 0, 0)).astype(BF)
    df = (stack(dfs) * live).astype(BF)
    da = dot(wx, dx) + dot(wf, df)
    xhat, r = normed(x)
    return dx, df, stack(dls), ds, norm_back(xhat, r, gain, da), row_sum(da * xhat)


def core_index():
    return lax.rem(lax.axis_index("row"), 2)


def put_halves(v, mine, other):
    h = v.shape[0] // 2
    zero = core_index() == 0
    mine[...] = jnp.where(zero, v[:h], v[h:])
    other[...] = jnp.where(zero, v[h:], v[:h])


def join_halves(mine, other):
    zero = core_index() == 0
    return stack([jnp.where(zero, mine, other), jnp.where(zero, other, mine)])


def put(refs, values):
    for ref, value in zip(refs, values):
        ref[...] = value


def first_kernel(n, x, g1, wx, wf, en, so, xt, *out):
    v = jnp.transpose(x[...].astype(F32))
    xt[...] = v
    r = front(v, column(g1[0:1]), wx[...], wf[...], en[...], so[0], live_rows(n[0]))
    put(out, r[:6])
    put_halves(r[6], *out[6:])


def save_tokens(toks, attn, tok_ref, attn_ref):
    for i, t in enumerate(toks):
        tok_ref[i] = t
    attn_ref[...] = attn


def middle_kernel(
    n, numer, numer_o, x, w, wq, wk, wv, wo, g2, w1, w2, g1, wx, wf, en, so,
    tok_ref, attn_ref, y_ref, x1_ref, b_ref, u_ref, hid_ref, xt, *out
):
    toks, attn = token_mix(join_halves(numer[...], numer_o[...]), wq[...], wk[...], wv[...])
    save_tokens(toks, attn, tok_ref, attn_ref)
    y, x1, b, u = finish(x[...], w[...], toks[5], wo[...], column(g2[0:1]), w1[...])
    hid = gelu(u).astype(BF)
    put((y_ref, x1_ref, b_ref, u_ref, hid_ref), (y, x1, b, u, hid))
    v = x1 + dot(w2[...], hid, 0, 0)
    xt[...] = v
    r = front(v, column(g1[1:2]), wx[...], wf[...], en[...], so[1], live_rows(n[0]))
    put(out, r[:6])
    put_halves(r[6], *out[6:])


def turn_kernel(
    n, numer, numer_o, x, w, wq, wk, wv, wo, g2, w1, w2, up,
    tok_ref, attn_ref, y_ref, b_ref, hid_ref, *out
):
    toks, attn = token_mix(join_halves(numer[...], numer_o[...]), wq[...], wk[...], wv[...])
    save_tokens(toks, attn, tok_ref, attn_ref)
    gain = column(g2[1:2])
    y, x1, b, u = finish(x[...], w[...], toks[5], wo[...], gain, w1[...])
    put((y_ref, b_ref, hid_ref), (y, b, gelu(u).astype(BF)))
    upt = jnp.transpose(up[...].astype(F32)) * live_rows(n[0])[:1]
    r = finish_back(upt, x1, u, w[...], toks[5], wo[...], gain, w1[...], w2[...])
    put(out, r[:6])
    put_halves(r[6], *out[6:])


def token_grads(tok, dqkv, refs):
    for ref, d in zip(refs, dqkv):
        for h in range(HEADS):
            ref[h] = exact(head(tok, h), head(d, h), 1, 1)


def reverse(layer, n, dmix, dmix_o, tok_ref, attn, wq, wk, wv, dw, x, fm, s, e, w, g1, wx, wf, en, so):
    dnumer, share, dqkv = token_back(
        unpair(join_halves(dmix[...], dmix_o[...])), tok_ref, attn[...], wq[...], wk[...], wv[...]
    )
    out = front_back(
        dnumer, share, dw[...], x[...], column(g1[layer : layer + 1]), fm[...], s[...],
        e[...], w[...], wx[...], wf[...], en[...], so[layer], live_rows(n[0]),
    )
    return out, dqkv


def back_kernel(
    n, dmix, dmix_o, tok_ref, attn, wq, wk, wv, dw, x, fm, s, e, w, g1, wx, wf, en, so,
    after, x1, u, w_below, tok_below, wo, g2, w1, w2,
    dwq, dwk, dwv, dx, df, dl, ds, dg, *out
):
    r, dqkv = reverse(1, n, dmix, dmix_o, tok_ref, attn, wq, wk, wv, dw, x, fm, s, e, w, g1, wx, wf, en, so)
    put((dx, df, dl, ds), r[:4])
    dg[...] = r[5]
    up = after[...] + r[4]
    r = finish_back(
        up, x1[...], u[...], w_below[...], tok_below[5], wo[...], column(g2[0:1]),
        w1[...], w2[...],
    )
    put(out, r[:6])
    put_halves(r[6], *out[6:])
    token_grads(tok_ref[0], dqkv, (dwq, dwk, dwv))


def last_kernel(
    n, dmix, dmix_o, tok_ref, attn, wq, wk, wv, dw, x, fm, s, e, w, g1, wx, wf, en, so,
    after, a, xm, dwq, dwk, dwv, point, mine, other, dx, df, dl, ds, dg
):
    r, dqkv = reverse(
        0, n, dmix, dmix_o, tok_ref, attn, wq, wk, wv, dw, x, fm, s, e, w, g1, wx, wf, en, so
    )
    put((dx, df, dl, ds), r[:4])
    dg[...] = r[5]
    both(front_half, (a, dx, df, xm, dl, ds, dg), mine, other, 0)
    clear(FRONT_HALF, mine, other)
    point[...] = jnp.transpose(after[...] + r[4])
    token_grads(tok_ref[0], dqkv, (dwq, dwk, dwv))


def first_row(v):
    return jnp.where(iota((8, D), 0) == 0, v, 0.0)


FINISH_HALF = 1160
FRONT_HALF = 296


def finish_half(c, hid, up, b, du, y, after, dg, out, at):
    out[at : at + 512] = dot(hid[pl.ds(c * 512, 512)], up[...], 1, 1)
    for k in range(2):
        t = dot(b[...], du[pl.ds(c * 512 + 256 * k, 256)], 1, 1)
        out[at + 512 + 256 * k : at + 768 + 256 * k] = t
    out[at + 1024 : at + 1152] = dot(y[pl.ds(c * 128, 128)], after[...], 1, 1)
    out[at + 1152 : at + 1160] = first_row(dg[...])


def front_half(c, a, dx, df, xm, dl, ds, dg, out, at):
    rows = a[pl.ds(c * 128, 128)]
    out[at : at + 128] = dot(rows, dx[...], 1, 1)
    out[at + 128 : at + 256] = dot(rows, df[...], 1, 1)
    for j in range(2):
        r = exact(xm[pl.ds(c * 128 + 64 * j, 64)], dl[pl.ds(c * 256 + 128 * j, 128)], 1, 1)
        out[at + 256 : at + 288, 128 * j : 128 * (j + 1)] = pair_rows(r)
    t = exact(ds[...], xm[...], 1, 1)
    t = jnp.where((iota((HEADS, D), 1) >> 5) == iota((HEADS, D), 0), t, 0.0)
    t = jnp.sum(t, axis=0, keepdims=True)
    out[at + 288 : at + 296] = first_row(dg[...]) + jnp.where(iota((8, D), 0) == 1, t, 0.0)


def both(half, refs, mine, other, at):
    c = core_index()
    half(c, *refs, mine, at)
    half(1 - c, *refs, other, at)


def clear(rows, *outs):
    for out in outs:
        out[rows:] = jnp.zeros((out.shape[0] - rows, D), F32)


def finish_grads_kernel(*refs):
    both(finish_half, refs[:7], *refs[7:], 0)
    clear(FINISH_HALF, *refs[7:])


def second_grads_kernel(*refs):
    both(finish_half, refs[:7], *refs[14:], 0)
    both(front_half, refs[7:14], *refs[14:], FINISH_HALF)
    clear(FINISH_HALF + FRONT_HALF, *refs[14:])


def ordered(mine, other, first, out):
    h = out.shape[1]
    r = h // 16
    zero = core_index() == 0
    for q in range(16):
        at = place(q, h)
        m, o = mine[q, first : first + r], other[q, first : first + r]
        out[0, at : at + r] = jnp.where(zero, m, o)
        out[1, at : at + r] = jnp.where(zero, o, m)


def unpack_kernel(
    got, got_o, fro, fro_o, q0, q1, k0, k1, v0, v1,
    ln1, gx, gf, ge, gs, gq, gk, gv, go, ln2, g1, g2, one, two, three
):
    for ref, below, above in ((gq, q0, q1), (gk, k0, k1), (gv, v0, v1)):
        ref[0] = below[...]
        ref[1] = above[...]
    ordered(got, got_o, 0, one)
    ordered(got, got_o, one.shape[1] // 16, two)
    zero = core_index() == 0
    m, o = fro[...], fro_o[...]
    three[0] = jnp.where(zero, m, o)
    three[1] = jnp.where(zero, o, m)
    for l, (fin, fro, at) in enumerate(((two, three, 0), (one, two, FINISH_HALF))):
        for c in range(2):
            g2[l, 512 * c : 512 * (c + 1)] = fin[c, 0:512]
            for k in range(2):
                lane = 512 * c + 256 * k
                g1[l, :, lane : lane + 256] = fin[c, 512 + 256 * k : 768 + 256 * k]
            go[l, 128 * c : 128 * (c + 1)] = fin[c, 1024:1152]
            gx[l, 128 * c : 128 * (c + 1)] = fro[c, at : at + 128]
            gf[l, 128 * c : 128 * (c + 1)] = fro[c, at + 128 : at + 256]
            for h in range(4):
                t = fro[c, at + 256 : at + 288, 128 * (h // 2) : 128 * (h // 2 + 1)]
                ge[l, 4 * c + h] = t[:, 64 * (h % 2) : 64 * (h % 2 + 1)]
        ln2[l : l + 1] = fin[0, 1152:1153]
        ln1[l : l + 1] = fro[0, at + 288 : at + 289]
        for h in range(HEADS):
            gs[l, h : h + 1] = fro[0, at + 289 : at + 290, 32 * h : 32 * (h + 1)]


AXES = ("row", "col")


def linear(z, c, y, x):
    return (z * 2 + c) * 16 + y * 4 + x


def swap(v, zm=0, cm=0, ym=0, xm=0):
    pairs = [
        (linear(z, c, y, x), linear(z ^ zm, c ^ cm, y ^ ym, x ^ xm))
        for z in range(8)
        for c in range(2)
        for y in range(4)
        for x in range(4)
    ]
    return lax.ppermute(v, AXES, pairs)


def coords():
    r = lax.axis_index("row")
    q = lax.axis_index("col")
    return r // 2, r % 2, q // 4, q % 4


def gray(v):
    return ((v ^ (v >> 1)) & 1, v >> 1)


def halves(v, b):
    h = v.shape[0] // 2
    return (
        lax.dynamic_slice_in_dim(v, b * h, h, 0),
        lax.dynamic_slice_in_dim(v, (1 - b) * h, h, 0),
    )


CORE = dict(cm=1)
ALONG_X = (dict(xm=1), dict(xm=2), dict(xm=3))
ALONG_Y = (dict(ym=1), dict(ym=2), dict(ym=3))
NEAR_Z = (dict(zm=1), dict(zm=7), dict(zm=6))


def all_to(v, partners):
    return [(v, k) for k in partners]


def four(v, got):
    return (v + got[0]) + (got[1] + got[2])


def small_sum(mine, other):
    m = mine + (yield [(other, CORE)])[0]
    m = four(m, (yield all_to(m, ALONG_X)))
    m = four(m, (yield all_to(m, ALONG_Y)))
    m = four(m, (yield all_to(m, NEAR_Z)))
    m = m + (yield [(m, dict(zm=2))])[0]
    return m, (yield [(m, CORE)])[0]


PAIRWISE = (
    dict(xm=1), dict(xm=3), dict(ym=1), dict(ym=3), dict(zm=1), dict(zm=2), dict(zm=7)
)


def pair_sum(mine, other):
    m = mine + (yield [(other, CORE)])[0]
    for partner in PAIRWISE:
        m = m + (yield [(m, partner)])[0]
    return m, (yield [(m, CORE)])[0]


def place(q, rows):
    (x0, x1), (y0, y1) = gray(q % 4), gray(q // 4)
    index = x0 * 2 + x1 if y0 == 0 else x1 * 2 + x0
    return y0 * rows // 2 + index * rows // 8 + y1 * rows // 16


def scatter_sum(mine, other):
    z, c, y, x = coords()
    (x0, x1), (y0, y1) = gray(x), gray(y)
    m = mine + (yield [(other, CORE)])[0]
    h = m.shape[0] // 2
    parts = [m[:h], m[h:]]
    for first, second in (((x0, 1), (x1, 3)), ((x1, 3), (x0, 1))):
        cut = [halves(parts[0], first[0]), halves(parts[1], second[0])]
        got = yield [(cut[0][1], dict(xm=first[1])), (cut[1][1], dict(xm=second[1]))]
        parts = [keep + g for (keep, _), g in zip(cut, got)]
    m = jnp.concatenate(parts)
    for bit, ym in ((y0, 1), (y1, 3)):
        keep, o = halves(m, bit)
        m = keep + (yield [(o, dict(ym=ym))])[0]
    return m


def across_z(m):
    for zm in (1, 2, 7):
        m = m + (yield [(m, dict(zm=zm))])[0]
    return m


def gather(m):
    return lax.all_gather(m, "col")


def take(v, i):
    return lax.dynamic_index_in_dim(v, i, 0, keepdims=False)


def in_order(v, got, i):
    t = [v] + list(got)
    odd = [t[1], t[0], t[3], t[2]]
    t = [jnp.where(i & 1 == 1, b, a) for a, b in zip(t, odd)]
    return jnp.concatenate(
        [jnp.where(i & 2 == 2, b, a) for a, b in zip(t, (t[2], t[3], t[0], t[1]))]
    )


def mid_sum(mine, other):
    z, c, y, x = coords()
    m = mine + (yield [(other, CORE)])[0]
    for i, along in ((x, ALONG_X), (y, ALONG_Y)):
        t = m.reshape(4, -1, m.shape[-1])
        got = yield [(take(t, i ^ (k + 1)), partner) for k, partner in enumerate(along)]
        m = four(take(t, i), got)
    m = four(m, (yield all_to(m, NEAR_Z)))
    m = m + (yield [(m, dict(zm=2))])[0]
    for i, along in ((y, ALONG_Y), (x, ALONG_X)):
        m = in_order(m, (yield all_to(m, along)), i)
    return m, (yield [(m, CORE)])[0]


class Sum:
    def __init__(self, steps_of):
        self.steps_of = steps_of
        self.wanted = next(steps_of)
        self.value = None
        self.done = False

    def send(self, got):
        try:
            self.wanted = self.steps_of.send(got)
        except StopIteration as end:
            self.value, self.done = end.value, True


def phase(sums, *beside):
    sums = [s for s in sums if not s.done]
    moved = [[swap(v, **k) for v, k in s.wanted] for s in sums]
    moved, beside = lax.optimization_barrier((moved, beside))
    for s, got in zip(sums, moved):
        s.send(got)
    return beside


def call(kernel, args, outs, name, scratch=(), cost=None):
    specs, values = [], []
    for a in args:
        if isinstance(a, tuple):
            v, layer = a
            block = (None,) + v.shape[1:]
            zeros = (0,) * (v.ndim - 1)
            specs.append(pl.BlockSpec(block, functools.partial(lambda t, i: t, (layer,) + zeros)))
        else:
            v = a
            if v.dtype == jnp.int32:
                specs.append(pl.BlockSpec(memory_space=pltpu.SMEM))
            else:
                specs.append(
                    pl.BlockSpec(v.shape, functools.partial(lambda t, i: t, (0,) * v.ndim))
                )
        values.append(v)
    out_shape = [jax.ShapeDtypeStruct(s, t) for s, t in outs]
    out_specs = [
        pl.BlockSpec(s, functools.partial(lambda t, i: t, (0,) * len(s))) for s, t in outs
    ]
    return pl.pallas_call(
        kernel,
        grid=(1,),
        in_specs=specs,
        out_specs=out_specs,
        out_shape=out_shape,
        scratch_shapes=list(scratch),
        cost_estimate=cost,
        name=name,
        compiler_params=pltpu.CompilerParams(vmem_limit_bytes=63 * 1024 * 1024),
    )(*values)


WIDE = ((D, PTS), F32)
LOW = ((D, PTS), BF)
BY_SLICE = ((HEADS * SLICES, PTS), F32)
BY_HEAD = ((HEADS, PTS), F32)
HIDDEN = ((FF, PTS), BF)
ROW = ((1, D), F32)
FRONT_OUTS = [LOW, WIDE, WIDE, BY_HEAD, BY_SLICE, BY_SLICE] + [((80, 128), F32)] * 2
TOKEN_OUTS = [((6, D, SLICES), F32), ((HEADS * SLICES, SLICES), F32)]
BACK_OUTS = [LOW, HIDDEN, WIDE, LOW, ROW, BY_SLICE] + [((64, 128), F32)] * 2
TOKEN_GRADS = [((HEADS, WIDTH, WIDTH), F32)] * 3
REVERSE_OUTS = TOKEN_GRADS + [LOW, LOW, BY_SLICE, BY_HEAD, ROW]


FINISH_PAD = 1280
SECOND_PAD = 1536
FRONT_PAD = 384


def cost(flops, nbytes):
    return pl.CostEstimate(flops=flops, bytes_accessed=nbytes, transcendentals=0)


def body(x, n, up, g1, wx, wf, en, so, wq, wk, wv, wo, g2, w1, w2):
    def lead(l):
        return (g1, (wx, l), (wf, l), (en, l), so)

    def mix(l):
        return ((wq, l), (wk, l), (wv, l))

    def total(*part):
        s = Sum(small_sum(*part))
        while not s.done:
            phase([s])
        return s.value

    x0, a0, xm0, fm0, s0, e0, p0, mine, other = call(
        first_kernel, (n, x, *lead(0)), [WIDE] + FRONT_OUTS, "first"
    )
    numer = total(mine, other)
    tok0, attn0, y0, mid0, b0, u0, hid0, x1, a1, xm1, fm1, s1, e1, p1, mine, other = call(
        middle_kernel,
        (n, *numer, x0, p0, *mix(0), (wo, 0), g2, (w1, 0), (w2, 0), *lead(1)),
        TOKEN_OUTS + [LOW, WIDE, LOW, ((FF, PTS), F32), HIDDEN, WIDE] + FRONT_OUTS,
        "middle",
    )
    numer = total(mine, other)
    tok1, attn1, y1, b1, hid1, low1, du1, after1, alow1, dg1, dw1, mine, other = call(
        turn_kernel,
        (n, *numer, x1, p1, *mix(1), (wo, 1), g2, (w1, 1), (w2, 1), up),
        TOKEN_OUTS + [LOW, LOW, HIDDEN] + BACK_OUTS,
        "turn",
    )
    small = Sum(pair_sum(mine, other))
    held = phase([small], hid1, low1, b1, du1, y1, alow1, dg1)
    halves1 = call(
        finish_grads_kernel, held, [((FINISH_PAD, D), F32)] * 2, "finish_grads",
        cost=cost(310000000, 4500000),
    )
    halves1 = phase([small], *halves1)
    finish1 = Sum(scatter_sum(*halves1))
    for _ in range(5):
        phase([small, finish1])
    phase([small])
    phase([small])
    dmix = small.value
    (gq1, gk1, gv1, dx1, df1, dl1, ds1, dn1, low0, du0, after0, alow0, dg0, dw0, mine, other) = call(
        back_kernel,
        (n, *dmix, tok1, attn1, *mix(1), dw1, x1, fm1, s1, e1, p1, *lead(1))
        + (after1, mid0, u0, p0, tok0, (wo, 0), g2, (w1, 0), (w2, 0)),
        REVERSE_OUTS + BACK_OUTS,
        "back",
        cost=cost(2000000000, 8000000),
    )
    small = Sum(pair_sum(mine, other))
    held = phase(
        [small], hid0, low0, b0, du0, y0, alow0, dg0, a1, dx1, df1, xm1, dl1, ds1, dn1
    )
    halves0 = call(
        second_grads_kernel, held, [((SECOND_PAD, D), F32)] * 2, "second_grads",
        cost=cost(600000000, 6000000),
    )
    halves0 = phase([small], *halves0)
    second = Sum(scatter_sum(*halves0))
    for _ in range(5):
        phase([small, second])
    early = Sum(across_z(jnp.concatenate([finish1.value, second.value])))
    phase([small, early])
    phase([small])
    dmix = small.value
    gq0, gk0, gv0, point, mine, other = call(
        last_kernel,
        (n, *dmix, tok0, attn0, *mix(0), dw0, x0, fm0, s0, e0, p0, *lead(0), after0, a0, xm0),
        TOKEN_GRADS + [((PTS, D), F32)] + [((FRONT_PAD, D), F32)] * 2,
        "last",
        scratch=[pltpu.VMEM(s, t) for s, t in (LOW, LOW, BY_SLICE, BY_HEAD, ROW)],
        cost=cost(2000000000, 6000000),
    )
    mine, other = phase([early], mine, other)
    front0 = Sum(mid_sum(mine, other))
    phase([front0])
    phase([front0, early])
    got = gather(early.value)
    for _ in range(4):
        phase([front0])
    (got,) = phase([front0], got)
    phase([front0])
    got_o = swap(got, **CORE)
    grads = call(
        unpack_kernel,
        (got, got_o, *front0.value, gq0, gq1, gk0, gk1, gv0, gv1),
        [(v.shape, F32) for v in (g1, wx, wf, en, so, wq, wk, wv, wo, g2, w1, w2)],
        "unpack",
        scratch=[pltpu.VMEM((2, r, D), F32) for r in (FINISH_PAD, SECOND_PAD, FRONT_PAD)],
    )
    return point, *grads


def solution(mesh):
    split = P(("row", "col"), None)
    in_specs = (split, P(("row", "col")), split) + (P(),) * 12
    out_specs = (split,) + (P(),) * 12
    return jax.shard_map(body, mesh=mesh, in_specs=in_specs, out_specs=out_specs, check_vma=False)
```

```python
import functools
import math

import jax
import jax.numpy as jnp
from jax import lax
from jax.experimental import pallas as pl
from jax.experimental.pallas import tpu as pltpu
from jax.sharding import PartitionSpec as P

BF = jnp.bfloat16
F32 = jnp.float32
PTS = 256
D = 256
FF = 1024
HEADS = 8
WIDTH = 32
SLICES = 64
PAIRS = HEADS // 2
EPS = 1e-05


def dot(a, b, ca=1, cb=0):
    return lax.dot_general(a, b, (((ca,), (cb,)), ((), ())), preferred_element_type=F32)


def exact(a, b, ca=1, cb=0):
    return lax.dot_general(
        a,
        b,
        (((ca,), (cb,)), ((), ())),
        precision=lax.Precision.HIGH,
        preferred_element_type=F32,
    )


def head(v, h, n=WIDTH):
    return v[h * n : (h + 1) * n]


def stack(pieces):
    return jnp.concatenate(pieces, axis=0)


def iota(shape, axis):
    return lax.broadcasted_iota(jnp.int32, shape, axis)


def column(row):
    return jnp.transpose(jnp.broadcast_to(row, (PTS, D)))


def row_sum(v):
    return jnp.sum(jnp.transpose(v), axis=0, keepdims=True)


def normed(x):
    c = x - jnp.mean(x, axis=0, keepdims=True)
    r = lax.rsqrt(jnp.mean(c * c, axis=0, keepdims=True) + EPS)
    return c * r, r


def norm_back(xhat, r, gain, g):
    dh = g * gain
    return r * (
        dh
        - jnp.mean(dh, axis=0, keepdims=True)
        - xhat * jnp.mean(dh * xhat, axis=0, keepdims=True)
    )


def live_rows(n):
    keep = (iota((8, PTS), 0) == 0) & (iota((8, PTS), 1) < n)
    return jnp.where(keep, 1.0, 0.0)


def softness_rows(s):
    wide = jnp.concatenate([s] * HEADS, axis=1)
    return jnp.where((iota((HEADS, D), 1) >> 5) == iota((HEADS, D), 0), wide, 0.0)


def block_diagonal(w):
    wide = jnp.concatenate([w.reshape(D, WIDTH)] * HEADS, axis=1)
    return jnp.where((iota((D, D), 0) >> 5) == (iota((D, D), 1) >> 5), wide, 0.0)


def pair_rows(r):
    return jnp.where(iota((WIDTH, 128), 1) < SLICES, r[:WIDTH], r[WIDTH : 2 * WIDTH])


def front(x, gain, wx, wf, energy, softness, live8):
    xhat, _ = normed(x)
    a = (xhat * gain).astype(BF)
    xm = dot(wx, a, 0, 0)
    fm = dot(wf, a, 0, 0)
    s = exact(softness_rows(softness), xm)
    temp = 0.5 + jnp.maximum(s, 0.0) + jnp.log1p(jnp.exp(-jnp.abs(s)))
    es, ws = [], []
    for h in range(HEADS):
        e = exact(energy[h], head(xm, h), 0, 0) / temp[h : h + 1]
        p = jnp.exp(e - jnp.max(e, axis=0, keepdims=True))
        es.append(e)
        ws.append(p / jnp.sum(p, axis=0, keepdims=True))
    w = stack(ws)
    masked = fm * live8[:1]
    rows = []
    for j in range(PAIRS):
        r = exact(stack([head(masked, j, 64), live8]), head(w, j, 128), 1, 1)
        rows += [pair_rows(r), r[64:72]]
    return a, xm, fm, s, stack(es), w, stack(rows)


def token_mix(numer, wq, wk, wv):
    toks, invs = [], []
    for j in range(PAIRS):
        inv = 1.0 / (numer[40 * j + 32 : 40 * j + 33] + EPS)
        t = numer[40 * j : 40 * j + 32] / (numer[40 * j + 32 : 40 * j + 33] + EPS)
        inv = jnp.broadcast_to(inv, (WIDTH, 128))
        toks += [t[:, :SLICES], t[:, SLICES:]]
        invs += [inv[:, :SLICES], inv[:, SLICES:]]
    tok = stack(toks)
    q, k, v = (exact(block_diagonal(w), tok, 0, 0) for w in (wq, wk, wv))
    attns, mixes = [], []
    for h in range(HEADS):
        sc = exact(head(k, h), head(q, h), 0, 0) * (1.0 / math.sqrt(WIDTH))
        p = jnp.exp(sc - jnp.max(sc, axis=0, keepdims=True))
        attn = p / jnp.sum(p, axis=0, keepdims=True)
        attns.append(attn)
        mixes.append(exact(head(v, h), attn))
    return (tok, q, k, v, stack(invs), stack(mixes)), stack(attns)


def token_back(dmix, toks, attn, wq, wk, wv):
    tok, q, k, v, inv = (toks[i] for i in range(5))
    dqs, dks, dvs = [], [], []
    for h in range(HEADS):
        at, dm = head(attn, h, SLICES), head(dmix, h)
        dvs.append(exact(dm, at, 1, 1))
        da = exact(head(v, h), dm, 0, 0)
        ds = at * (da - jnp.sum(at * da, axis=0, keepdims=True)) * (1.0 / math.sqrt(WIDTH))
        dqs.append(exact(head(k, h), ds))
        dks.append(exact(head(q, h), ds, 1, 1))
    dq, dk, dv = stack(dqs), stack(dks), stack(dvs)
    dtok = exact(block_diagonal(wq), dq) + exact(block_diagonal(wk), dk)
    dtok = dtok + exact(block_diagonal(wv), dv)
    dnumer = dtok * inv
    return dnumer, dnumer * tok, (dq, dk, dv)


def finish(x, w, mixed, wo, gain, w1):
    y = stack([exact(head(mixed, h), head(w, h, SLICES)) for h in range(HEADS)]).astype(BF)
    x1 = x + dot(wo, y, 0, 0)
    xhat, _ = normed(x1)
    b = (xhat * gain).astype(BF)
    return y, x1, b, dot(w1, b, 0, 0)


C0 = math.sqrt(2.0 / math.pi)
C1 = 0.044715


def gelu(u):
    return 0.5 * u * (1.0 + jnp.tanh(C0 * (u + C1 * (u * u * u))))


def gelu_slope(u):
    t = jnp.tanh(C0 * (u + C1 * (u * u * u)))
    return 0.5 * (1.0 + t) + 0.5 * u * (1.0 - t * t) * (C0 * (1.0 + 3.0 * C1 * (u * u)))


def finish_back(up, x1, u, w, mixed, wo, gain, w1, w2):
    low = up.astype(BF)
    du = (dot(w2, low) * gelu_slope(u)).astype(BF)
    db = dot(w1, du)
    xhat, r = normed(x1)
    dgain = row_sum(db * xhat)
    after = norm_back(xhat, r, gain, db) + up
    after_low = after.astype(BF)
    dy = dot(wo, after_low)
    dmix = stack(
        [
            pair_rows(exact(head(dy, j, 64), head(w, j, 128), 1, 1))
            for j in range(PAIRS)
        ]
    )
    dw = stack([exact(head(mixed, h), head(dy, h), 0, 0) for h in range(HEADS)])
    return low, du, after, after_low, dgain, dw, dmix


def unpair(v):
    out = []
    for j in range(PAIRS):
        blk = head(v, j)
        out += [blk[:, :SLICES], blk[:, SLICES:]]
    return stack(out)


def front_back(dnumer, share, dw, x, gain, fm, s, e, w, wx, wf, energy, softness, live8):
    live = live8[:1]
    masked = fm * live
    temp = 0.5 + jnp.maximum(s, 0.0) + jnp.log1p(jnp.exp(-jnp.abs(s)))
    inv_temp = 1.0 / temp
    first = iota((8, SLICES), 0) == 0
    dls, dts, dfs, dxs = [], [], [], []
    for h in range(HEADS):
        dn, wh = head(dnumer, h), head(w, h, SLICES)
        dtot = jnp.where(first, -jnp.sum(head(share, h), axis=0, keepdims=True), 0.0)
        dwh = head(dw, h, SLICES) + exact(
            stack([dn, dtot]), stack([head(masked, h), live8]), 0, 0
        )
        de = wh * (dwh - jnp.sum(wh * dwh, axis=0, keepdims=True))
        dl = de * inv_temp[h : h + 1]
        dts.append(-jnp.sum(dl * head(e, h, SLICES), axis=0, keepdims=True))
        dls.append(dl)
        dfs.append(exact(dn, wh))
        dxs.append(exact(energy[h], dl))
    ds = stack(dts) / (1.0 + jnp.exp(-s))
    dx = (stack(dxs) + exact(softness_rows(softness), ds, 0, 0)).astype(BF)
    df = (stack(dfs) * live).astype(BF)
    da = dot(wx, dx) + dot(wf, df)
    xhat, r = normed(x)
    return dx, df, stack(dls), ds, norm_back(xhat, r, gain, da), row_sum(da * xhat)


def core_index():
    return lax.rem(lax.axis_index("row"), 2)


def put_halves(v, mine, other):
    h = v.shape[0] // 2
    zero = core_index() == 0
    mine[...] = jnp.where(zero, v[:h], v[h:])
    other[...] = jnp.where(zero, v[h:], v[:h])


def join_halves(mine, other):
    zero = core_index() == 0
    return stack([jnp.where(zero, mine, other), jnp.where(zero, other, mine)])


def put(refs, values):
    for ref, value in zip(refs, values):
        ref[...] = value


def first_kernel(n, x, g1, wx, wf, en, so, xt, *out):
    v = jnp.transpose(x[...].astype(F32))
    xt[...] = v
    r = front(v, column(g1[0:1]), wx[...], wf[...], en[...], so[0], live_rows(n[0]))
    put(out, r[:6])
    put_halves(r[6], *out[6:])


def save_tokens(toks, attn, tok_ref, attn_ref):
    for i, t in enumerate(toks):
        tok_ref[i] = t
    attn_ref[...] = attn


def middle_kernel(
    n, numer, numer_o, x, w, wq, wk, wv, wo, g2, w1, w2, g1, wx, wf, en, so,
    tok_ref, attn_ref, y_ref, x1_ref, b_ref, u_ref, hid_ref, xt, *out
):
    toks, attn = token_mix(join_halves(numer[...], numer_o[...]), wq[...], wk[...], wv[...])
    save_tokens(toks, attn, tok_ref, attn_ref)
    y, x1, b, u = finish(x[...], w[...], toks[5], wo[...], column(g2[0:1]), w1[...])
    hid = gelu(u).astype(BF)
    put((y_ref, x1_ref, b_ref, u_ref, hid_ref), (y, x1, b, u, hid))
    v = x1 + dot(w2[...], hid, 0, 0)
    xt[...] = v
    r = front(v, column(g1[1:2]), wx[...], wf[...], en[...], so[1], live_rows(n[0]))
    put(out, r[:6])
    put_halves(r[6], *out[6:])


def turn_kernel(
    n, numer, numer_o, x, w, wq, wk, wv, wo, g2, w1, w2, up,
    tok_ref, attn_ref, y_ref, b_ref, hid_ref, *out
):
    toks, attn = token_mix(join_halves(numer[...], numer_o[...]), wq[...], wk[...], wv[...])
    save_tokens(toks, attn, tok_ref, attn_ref)
    gain = column(g2[1:2])
    y, x1, b, u = finish(x[...], w[...], toks[5], wo[...], gain, w1[...])
    put((y_ref, b_ref, hid_ref), (y, b, gelu(u).astype(BF)))
    upt = jnp.transpose(up[...].astype(F32)) * live_rows(n[0])[:1]
    r = finish_back(upt, x1, u, w[...], toks[5], wo[...], gain, w1[...], w2[...])
    put(out, r[:6])
    put_halves(r[6], *out[6:])


def token_grads(tok, dqkv, refs):
    for ref, d in zip(refs, dqkv):
        for h in range(HEADS):
            ref[h] = exact(head(tok, h), head(d, h), 1, 1)


def reverse(layer, n, dmix, dmix_o, tok_ref, attn, wq, wk, wv, dw, x, fm, s, e, w, g1, wx, wf, en, so):
    dnumer, share, dqkv = token_back(
        unpair(join_halves(dmix[...], dmix_o[...])), tok_ref, attn[...], wq[...], wk[...], wv[...]
    )
    out = front_back(
        dnumer, share, dw[...], x[...], column(g1[layer : layer + 1]), fm[...], s[...],
        e[...], w[...], wx[...], wf[...], en[...], so[layer], live_rows(n[0]),
    )
    return out, dqkv


def back_kernel(
    n, dmix, dmix_o, tok_ref, attn, wq, wk, wv, dw, x, fm, s, e, w, g1, wx, wf, en, so,
    after, x1, u, w_below, tok_below, wo, g2, w1, w2,
    dwq, dwk, dwv, dx, df, dl, ds, dg, *out
):
    r, dqkv = reverse(1, n, dmix, dmix_o, tok_ref, attn, wq, wk, wv, dw, x, fm, s, e, w, g1, wx, wf, en, so)
    put((dx, df, dl, ds), r[:4])
    dg[...] = r[5]
    up = after[...] + r[4]
    r = finish_back(
        up, x1[...], u[...], w_below[...], tok_below[5], wo[...], column(g2[0:1]),
        w1[...], w2[...],
    )
    put(out, r[:6])
    put_halves(r[6], *out[6:])
    token_grads(tok_ref[0], dqkv, (dwq, dwk, dwv))


def last_kernel(
    n, dmix, dmix_o, tok_ref, attn, wq, wk, wv, dw, x, fm, s, e, w, g1, wx, wf, en, so,
    after, a, xm, dwq, dwk, dwv, point, mine, other, dx, df, dl, ds, dg
):
    r, dqkv = reverse(
        0, n, dmix, dmix_o, tok_ref, attn, wq, wk, wv, dw, x, fm, s, e, w, g1, wx, wf, en, so
    )
    put((dx, df, dl, ds), r[:4])
    dg[...] = r[5]
    both(front_half, (a, dx, df, xm, dl, ds, dg), mine, other, 0)
    clear(FRONT_HALF, mine, other)
    point[...] = jnp.transpose(after[...] + r[4])
    token_grads(tok_ref[0], dqkv, (dwq, dwk, dwv))


def first_row(v):
    return jnp.where(iota((8, D), 0) == 0, v, 0.0)


FINISH_HALF = 1160
FRONT_HALF = 296


def finish_half(c, hid, up, b, du, y, after, dg, out, at):
    out[at : at + 512] = dot(hid[pl.ds(c * 512, 512)], up[...], 1, 1)
    for k in range(2):
        t = dot(b[...], du[pl.ds(c * 512 + 256 * k, 256)], 1, 1)
        out[at + 512 + 256 * k : at + 768 + 256 * k] = t
    out[at + 1024 : at + 1152] = dot(y[pl.ds(c * 128, 128)], after[...], 1, 1)
    out[at + 1152 : at + 1160] = first_row(dg[...])


def front_half(c, a, dx, df, xm, dl, ds, dg, out, at):
    rows = a[pl.ds(c * 128, 128)]
    out[at : at + 128] = dot(rows, dx[...], 1, 1)
    out[at + 128 : at + 256] = dot(rows, df[...], 1, 1)
    for j in range(2):
        r = exact(xm[pl.ds(c * 128 + 64 * j, 64)], dl[pl.ds(c * 256 + 128 * j, 128)], 1, 1)
        out[at + 256 : at + 288, 128 * j : 128 * (j + 1)] = pair_rows(r)
    t = exact(ds[...], xm[...], 1, 1)
    t = jnp.where((iota((HEADS, D), 1) >> 5) == iota((HEADS, D), 0), t, 0.0)
    t = jnp.sum(t, axis=0, keepdims=True)
    out[at + 288 : at + 296] = first_row(dg[...]) + jnp.where(iota((8, D), 0) == 1, t, 0.0)


def both(half, refs, mine, other, at):
    c = core_index()
    half(c, *refs, mine, at)
    half(1 - c, *refs, other, at)


def clear(rows, *outs):
    for out in outs:
        out[rows:] = jnp.zeros((out.shape[0] - rows, D), F32)


def finish_grads_kernel(*refs):
    both(finish_half, refs[:7], *refs[7:], 0)
    clear(FINISH_HALF, *refs[7:])


def second_grads_kernel(*refs):
    both(finish_half, refs[:7], *refs[14:], 0)
    both(front_half, refs[7:14], *refs[14:], FINISH_HALF)
    clear(FINISH_HALF + FRONT_HALF, *refs[14:])


def ordered(mine, other, first, out):
    h = out.shape[1]
    r = h // 16
    zero = core_index() == 0
    for q in range(16):
        at = place(q, h)
        i = q % 4 * 4 + q // 4
        m, o = mine[i, first : first + r], other[i, first : first + r]
        out[0, at : at + r] = jnp.where(zero, m, o)
        out[1, at : at + r] = jnp.where(zero, o, m)


def unpack_kernel(
    got, got_o, fro, fro_o, q0, q1, k0, k1, v0, v1,
    ln1, gx, gf, ge, gs, gq, gk, gv, go, ln2, g1, g2, one, two, three
):
    for ref, below, above in ((gq, q0, q1), (gk, k0, k1), (gv, v0, v1)):
        ref[0] = below[...]
        ref[1] = above[...]
    ordered(got, got_o, 0, one)
    ordered(got, got_o, one.shape[1] // 16, two)
    zero = core_index() == 0
    m, o = fro[...], fro_o[...]
    three[0] = jnp.where(zero, m, o)
    three[1] = jnp.where(zero, o, m)
    for l, (fin, fro, at) in enumerate(((two, three, 0), (one, two, FINISH_HALF))):
        for c in range(2):
            g2[l, 512 * c : 512 * (c + 1)] = fin[c, 0:512]
            for k in range(2):
                lane = 512 * c + 256 * k
                g1[l, :, lane : lane + 256] = fin[c, 512 + 256 * k : 768 + 256 * k]
            go[l, 128 * c : 128 * (c + 1)] = fin[c, 1024:1152]
            gx[l, 128 * c : 128 * (c + 1)] = fro[c, at : at + 128]
            gf[l, 128 * c : 128 * (c + 1)] = fro[c, at + 128 : at + 256]
            for h in range(4):
                t = fro[c, at + 256 : at + 288, 128 * (h // 2) : 128 * (h // 2 + 1)]
                ge[l, 4 * c + h] = t[:, 64 * (h % 2) : 64 * (h % 2 + 1)]
        ln2[l : l + 1] = fin[0, 1152:1153]
        ln1[l : l + 1] = fro[0, at + 288 : at + 289]
        for h in range(HEADS):
            gs[l, h : h + 1] = fro[0, at + 289 : at + 290, 32 * h : 32 * (h + 1)]


AXES = ("row", "col")


def linear(z, c, y, x):
    return (z * 2 + c) * 16 + y * 4 + x


def swap(v, zm=0, cm=0, ym=0, xm=0):
    pairs = [
        (linear(z, c, y, x), linear(z ^ zm, c ^ cm, y ^ ym, x ^ xm))
        for z in range(8)
        for c in range(2)
        for y in range(4)
        for x in range(4)
    ]
    return lax.ppermute(v, AXES, pairs)


def coords():
    r = lax.axis_index("row")
    q = lax.axis_index("col")
    return r // 2, r % 2, q // 4, q % 4


def gray(v):
    return ((v ^ (v >> 1)) & 1, v >> 1)


def halves(v, b):
    h = v.shape[0] // 2
    return (
        lax.dynamic_slice_in_dim(v, b * h, h, 0),
        lax.dynamic_slice_in_dim(v, (1 - b) * h, h, 0),
    )


CORE = dict(cm=1)
ALONG_X = (dict(xm=1), dict(xm=2), dict(xm=3))
ALONG_Y = (dict(ym=1), dict(ym=2), dict(ym=3))
NEAR_Z = (dict(zm=1), dict(zm=7), dict(zm=6))


def all_to(v, partners):
    return [(v, k) for k in partners]


def four(v, got):
    return (v + got[0]) + (got[1] + got[2])


def small_sum(mine, other):
    m = mine + (yield [(other, CORE)])[0]
    m = four(m, (yield all_to(m, ALONG_X)))
    m = four(m, (yield all_to(m, ALONG_Y)))
    m = four(m, (yield all_to(m, NEAR_Z)))
    m = m + (yield [(m, dict(zm=2))])[0]
    return m, (yield [(m, CORE)])[0]


def place(q, rows):
    (x0, x1), (y0, y1) = gray(q % 4), gray(q // 4)
    index = x0 * 2 + x1 if y0 == 0 else x1 * 2 + x0
    return y0 * rows // 2 + index * rows // 8 + y1 * rows // 16


def scatter_sum(mine, other):
    z, c, y, x = coords()
    (x0, x1), (y0, y1) = gray(x), gray(y)
    m = mine + (yield [(other, CORE)])[0]
    h = m.shape[0] // 2
    parts = [m[:h], m[h:]]
    for first, second in (((x0, 1), (x1, 3)), ((x1, 3), (x0, 1))):
        cut = [halves(parts[0], first[0]), halves(parts[1], second[0])]
        got = yield [(cut[0][1], dict(xm=first[1])), (cut[1][1], dict(xm=second[1]))]
        parts = [keep + g for (keep, _), g in zip(cut, got)]
    m = jnp.concatenate(parts)
    for bit, ym in ((y0, 1), (y1, 3)):
        keep, o = halves(m, bit)
        m = keep + (yield [(o, dict(ym=ym))])[0]
    return m


def across_z(m):
    m = four(m, (yield all_to(m, NEAR_Z)))
    return m + (yield [(m, dict(zm=2))])[0]


SAME_X = [[y * 4 + x for y in range(4)] for x in range(4)]
SAME_Y = [[y * 4 + x for x in range(4)] for y in range(4)]


def gather(m, groups):
    return lax.all_gather(m, "col", axis_index_groups=groups)


def take(v, i):
    return lax.dynamic_index_in_dim(v, i, 0, keepdims=False)


def in_order(v, got, i):
    t = [v] + list(got)
    odd = [t[1], t[0], t[3], t[2]]
    t = [jnp.where(i & 1 == 1, b, a) for a, b in zip(t, odd)]
    return jnp.concatenate(
        [jnp.where(i & 2 == 2, b, a) for a, b in zip(t, (t[2], t[3], t[0], t[1]))]
    )


def mid_sum(mine, other):
    z, c, y, x = coords()
    m = mine + (yield [(other, CORE)])[0]
    for i, along in ((x, ALONG_X), (y, ALONG_Y)):
        t = m.reshape(4, -1, m.shape[-1])
        got = yield [(take(t, i ^ (k + 1)), partner) for k, partner in enumerate(along)]
        m = four(take(t, i), got)
    m = four(m, (yield all_to(m, NEAR_Z)))
    m = m + (yield [(m, dict(zm=2))])[0]
    for i, along in ((y, ALONG_Y), (x, ALONG_X)):
        m = in_order(m, (yield all_to(m, along)), i)
    return m, (yield [(m, CORE)])[0]


class Sum:
    def __init__(self, steps_of):
        self.steps_of = steps_of
        self.wanted = next(steps_of)
        self.value = None
        self.done = False

    def send(self, got):
        try:
            self.wanted = self.steps_of.send(got)
        except StopIteration as end:
            self.value, self.done = end.value, True


def phase(sums, *beside):
    sums = [s for s in sums if not s.done]
    moved = [[swap(v, **k) for v, k in s.wanted] for s in sums]
    moved, beside = lax.optimization_barrier((moved, beside))
    for s, got in zip(sums, moved):
        s.send(got)
    return beside


def call(kernel, args, outs, name, scratch=(), cost=None):
    specs, values = [], []
    for a in args:
        if isinstance(a, tuple):
            v, layer = a
            block = (None,) + v.shape[1:]
            zeros = (0,) * (v.ndim - 1)
            specs.append(pl.BlockSpec(block, functools.partial(lambda t, i: t, (layer,) + zeros)))
        else:
            v = a
            if v.dtype == jnp.int32:
                specs.append(pl.BlockSpec(memory_space=pltpu.SMEM))
            else:
                specs.append(
                    pl.BlockSpec(v.shape, functools.partial(lambda t, i: t, (0,) * v.ndim))
                )
        values.append(v)
    out_shape = [jax.ShapeDtypeStruct(s, t) for s, t in outs]
    out_specs = [
        pl.BlockSpec(s, functools.partial(lambda t, i: t, (0,) * len(s))) for s, t in outs
    ]
    return pl.pallas_call(
        kernel,
        grid=(1,),
        in_specs=specs,
        out_specs=out_specs,
        out_shape=out_shape,
        scratch_shapes=list(scratch),
        cost_estimate=cost,
        name=name,
        compiler_params=pltpu.CompilerParams(vmem_limit_bytes=63 * 1024 * 1024),
    )(*values)


WIDE = ((D, PTS), F32)
LOW = ((D, PTS), BF)
BY_SLICE = ((HEADS * SLICES, PTS), F32)
BY_HEAD = ((HEADS, PTS), F32)
HIDDEN = ((FF, PTS), BF)
ROW = ((1, D), F32)
FRONT_OUTS = [LOW, WIDE, WIDE, BY_HEAD, BY_SLICE, BY_SLICE] + [((80, 128), F32)] * 2
TOKEN_OUTS = [((6, D, SLICES), F32), ((HEADS * SLICES, SLICES), F32)]
BACK_OUTS = [LOW, HIDDEN, WIDE, LOW, ROW, BY_SLICE] + [((64, 128), F32)] * 2
TOKEN_GRADS = [((HEADS, WIDTH, WIDTH), F32)] * 3
REVERSE_OUTS = TOKEN_GRADS + [LOW, LOW, BY_SLICE, BY_HEAD, ROW]


FINISH_PAD = 1280
SECOND_PAD = 1536
FRONT_PAD = 384


def cost(flops, nbytes):
    return pl.CostEstimate(flops=flops, bytes_accessed=nbytes, transcendentals=0)


def body(x, n, up, g1, wx, wf, en, so, wq, wk, wv, wo, g2, w1, w2):
    def lead(l):
        return (g1, (wx, l), (wf, l), (en, l), so)

    def mix(l):
        return ((wq, l), (wk, l), (wv, l))

    def total(*part):
        s = Sum(small_sum(*part))
        while not s.done:
            phase([s])
        return s.value

    x0, a0, xm0, fm0, s0, e0, p0, mine, other = call(
        first_kernel, (n, x, *lead(0)), [WIDE] + FRONT_OUTS, "first"
    )
    numer = total(mine, other)
    tok0, attn0, y0, mid0, b0, u0, hid0, x1, a1, xm1, fm1, s1, e1, p1, mine, other = call(
        middle_kernel,
        (n, *numer, x0, p0, *mix(0), (wo, 0), g2, (w1, 0), (w2, 0), *lead(1)),
        TOKEN_OUTS + [LOW, WIDE, LOW, ((FF, PTS), F32), HIDDEN, WIDE] + FRONT_OUTS,
        "middle",
    )
    numer = total(mine, other)
    tok1, attn1, y1, b1, hid1, low1, du1, after1, alow1, dg1, dw1, mine, other = call(
        turn_kernel,
        (n, *numer, x1, p1, *mix(1), (wo, 1), g2, (w1, 1), (w2, 1), up),
        TOKEN_OUTS + [LOW, LOW, HIDDEN] + BACK_OUTS,
        "turn",
    )
    small = Sum(small_sum(mine, other))
    held = phase([small], hid1, low1, b1, du1, y1, alow1, dg1)
    halves1 = call(
        finish_grads_kernel, held, [((FINISH_PAD, D), F32)] * 2, "finish_grads",
        cost=cost(310000000, 4500000),
    )
    halves1 = phase([small], *halves1)
    finish1 = Sum(scatter_sum(*halves1))
    for _ in range(3):
        phase([small, finish1])
    phase([small])
    dmix = small.value
    (gq1, gk1, gv1, dx1, df1, dl1, ds1, dn1, low0, du0, after0, alow0, dg0, dw0, mine, other) = call(
        back_kernel,
        (n, *dmix, tok1, attn1, *mix(1), dw1, x1, fm1, s1, e1, p1, *lead(1))
        + (after1, mid0, u0, p0, tok0, (wo, 0), g2, (w1, 0), (w2, 0)),
        REVERSE_OUTS + BACK_OUTS,
        "back",
        cost=cost(2000000000, 8000000),
    )
    mine, other = phase([finish1], mine, other)
    small = Sum(small_sum(mine, other))
    held = phase(
        [small], hid0, low0, b0, du0, y0, alow0, dg0, a1, dx1, df1, xm1, dl1, ds1, dn1
    )
    halves0 = call(
        second_grads_kernel, held, [((SECOND_PAD, D), F32)] * 2, "second_grads",
        cost=cost(600000000, 6000000),
    )
    halves0 = phase([small, finish1], *halves0)
    second = Sum(scatter_sum(*halves0))
    for _ in range(3):
        phase([small, second])
    phase([small])
    dmix = small.value
    gq0, gk0, gv0, point, mine, other = call(
        last_kernel,
        (n, *dmix, tok0, attn0, *mix(0), dw0, x0, fm0, s0, e0, p0, *lead(0), after0, a0, xm0),
        TOKEN_GRADS + [((PTS, D), F32)] + [((FRONT_PAD, D), F32)] * 2,
        "last",
        scratch=[pltpu.VMEM(s, t) for s, t in (LOW, LOW, BY_SLICE, BY_HEAD, ROW)],
        cost=cost(2000000000, 6000000),
    )
    mine, other = phase([second], mine, other)
    front0 = Sum(mid_sum(mine, other))
    phase([front0, second])
    early = Sum(across_z(jnp.concatenate([finish1.value, second.value])))
    phase([front0, early])
    phase([front0, early])
    got = gather(early.value, SAME_X)
    (got,) = phase([front0], got)
    got = gather(got, SAME_Y).reshape((16,) + got.shape[1:])
    phase([front0])
    phase([front0])
    (got,) = phase([front0], got)
    phase([front0])
    got_o = swap(got, **CORE)
    grads = call(
        unpack_kernel,
        (got, got_o, *front0.value, gq0, gq1, gk0, gk1, gv0, gv1),
        [(v.shape, F32) for v in (g1, wx, wf, en, so, wq, wk, wv, wo, g2, w1, w2)],
        "unpack",
        scratch=[pltpu.VMEM((2, r, D), F32) for r in (FINISH_PAD, SECOND_PAD, FRONT_PAD)],
    )
    return point, *grads


def solution(mesh):
    split = P(("row", "col"), None)
    in_specs = (split, P(("row", "col")), split) + (P(),) * 12
    out_specs = (split,) + (P(),) * 12
    return jax.shard_map(body, mesh=mesh, in_specs=in_specs, out_specs=out_specs, check_vma=False)
```

```python
import functools
import math

import jax
import jax.numpy as jnp
from jax import lax
from jax.experimental import pallas as pl
from jax.experimental.pallas import tpu as pltpu
from jax.sharding import PartitionSpec as P

BF = jnp.bfloat16
F32 = jnp.float32
PTS = 256
D = 256
FF = 1024
HEADS = 8
WIDTH = 32
SLICES = 64
PAIRS = HEADS // 2
EPS = 1e-05


def dot(a, b, ca=1, cb=0):
    return lax.dot_general(a, b, (((ca,), (cb,)), ((), ())), preferred_element_type=F32)


def exact(a, b, ca=1, cb=0):
    return lax.dot_general(
        a,
        b,
        (((ca,), (cb,)), ((), ())),
        precision=lax.Precision.HIGH,
        preferred_element_type=F32,
    )


def head(v, h, n=WIDTH):
    return v[h * n : (h + 1) * n]


def stack(pieces):
    return jnp.concatenate(pieces, axis=0)


def iota(shape, axis):
    return lax.broadcasted_iota(jnp.int32, shape, axis)


def column(row):
    return jnp.transpose(jnp.broadcast_to(row, (PTS, D)))


def row_sum(v):
    return jnp.sum(jnp.transpose(v), axis=0, keepdims=True)


def normed(x):
    c = x - jnp.mean(x, axis=0, keepdims=True)
    r = lax.rsqrt(jnp.mean(c * c, axis=0, keepdims=True) + EPS)
    return c * r, r


def norm_back(xhat, r, gain, g):
    dh = g * gain
    return r * (
        dh
        - jnp.mean(dh, axis=0, keepdims=True)
        - xhat * jnp.mean(dh * xhat, axis=0, keepdims=True)
    )


def live_rows(n):
    keep = (iota((8, PTS), 0) == 0) & (iota((8, PTS), 1) < n)
    return jnp.where(keep, 1.0, 0.0)


def softness_rows(s):
    wide = jnp.concatenate([s] * HEADS, axis=1)
    return jnp.where((iota((HEADS, D), 1) >> 5) == iota((HEADS, D), 0), wide, 0.0)


def block_diagonal(w):
    wide = jnp.concatenate([w.reshape(D, WIDTH)] * HEADS, axis=1)
    return jnp.where((iota((D, D), 0) >> 5) == (iota((D, D), 1) >> 5), wide, 0.0)


def pair_rows(r):
    return jnp.where(iota((WIDTH, 128), 1) < SLICES, r[:WIDTH], r[WIDTH : 2 * WIDTH])


def front(x, gain, wx, wf, energy, softness, live8):
    xhat, _ = normed(x)
    a = (xhat * gain).astype(BF)
    xm = dot(wx, a, 0, 0)
    fm = dot(wf, a, 0, 0)
    s = exact(softness_rows(softness), xm)
    temp = 0.5 + jnp.maximum(s, 0.0) + jnp.log1p(jnp.exp(-jnp.abs(s)))
    es, ws = [], []
    for h in range(HEADS):
        e = exact(energy[h], head(xm, h), 0, 0) / temp[h : h + 1]
        p = jnp.exp(e - jnp.max(e, axis=0, keepdims=True))
        es.append(e)
        ws.append(p / jnp.sum(p, axis=0, keepdims=True))
    w = stack(ws)
    masked = fm * live8[:1]
    rows = []
    for j in range(PAIRS):
        r = exact(stack([head(masked, j, 64), live8]), head(w, j, 128), 1, 1)
        rows += [pair_rows(r), r[64:72]]
    return a, xm, fm, s, stack(es), w, stack(rows)


def token_mix(numer, wq, wk, wv):
    toks, invs = [], []
    for j in range(PAIRS):
        inv = 1.0 / (numer[40 * j + 32 : 40 * j + 33] + EPS)
        t = numer[40 * j : 40 * j + 32] / (numer[40 * j + 32 : 40 * j + 33] + EPS)
        inv = jnp.broadcast_to(inv, (WIDTH, 128))
        toks += [t[:, :SLICES], t[:, SLICES:]]
        invs += [inv[:, :SLICES], inv[:, SLICES:]]
    tok = stack(toks)
    q, k, v = (exact(block_diagonal(w), tok, 0, 0) for w in (wq, wk, wv))
    attns, mixes = [], []
    for h in range(HEADS):
        sc = exact(head(k, h), head(q, h), 0, 0) * (1.0 / math.sqrt(WIDTH))
        p = jnp.exp(sc - jnp.max(sc, axis=0, keepdims=True))
        attn = p / jnp.sum(p, axis=0, keepdims=True)
        attns.append(attn)
        mixes.append(exact(head(v, h), attn))
    return (tok, q, k, v, stack(invs), stack(mixes)), stack(attns)


def token_back(dmix, toks, attn, wq, wk, wv):
    tok, q, k, v, inv = (toks[i] for i in range(5))
    dqs, dks, dvs = [], [], []
    for h in range(HEADS):
        at, dm = head(attn, h, SLICES), head(dmix, h)
        dvs.append(exact(dm, at, 1, 1))
        da = exact(head(v, h), dm, 0, 0)
        ds = at * (da - jnp.sum(at * da, axis=0, keepdims=True)) * (1.0 / math.sqrt(WIDTH))
        dqs.append(exact(head(k, h), ds))
        dks.append(exact(head(q, h), ds, 1, 1))
    dq, dk, dv = stack(dqs), stack(dks), stack(dvs)
    dtok = exact(block_diagonal(wq), dq) + exact(block_diagonal(wk), dk)
    dtok = dtok + exact(block_diagonal(wv), dv)
    dnumer = dtok * inv
    return dnumer, dnumer * tok, (dq, dk, dv)


def finish(x, w, mixed, wo, gain, w1):
    y = stack([exact(head(mixed, h), head(w, h, SLICES)) for h in range(HEADS)]).astype(BF)
    x1 = x + dot(wo, y, 0, 0)
    xhat, _ = normed(x1)
    b = (xhat * gain).astype(BF)
    return y, x1, b, dot(w1, b, 0, 0)


C0 = math.sqrt(2.0 / math.pi)
C1 = 0.044715


def gelu(u):
    return 0.5 * u * (1.0 + jnp.tanh(C0 * (u + C1 * (u * u * u))))


def gelu_slope(u):
    t = jnp.tanh(C0 * (u + C1 * (u * u * u)))
    return 0.5 * (1.0 + t) + 0.5 * u * (1.0 - t * t) * (C0 * (1.0 + 3.0 * C1 * (u * u)))


def finish_back(up, x1, u, w, mixed, wo, gain, w1, w2):
    low = up.astype(BF)
    du = (dot(w2, low) * gelu_slope(u)).astype(BF)
    db = dot(w1, du)
    xhat, r = normed(x1)
    dgain = row_sum(db * xhat)
    after = norm_back(xhat, r, gain, db) + up
    after_low = after.astype(BF)
    dy = dot(wo, after_low)
    dmix = stack(
        [
            pair_rows(exact(head(dy, j, 64), head(w, j, 128), 1, 1))
            for j in range(PAIRS)
        ]
    )
    dw = stack([exact(head(mixed, h), head(dy, h), 0, 0) for h in range(HEADS)])
    return low, du, after, after_low, dgain, dw, dmix


def unpair(v):
    out = []
    for j in range(PAIRS):
        blk = head(v, j)
        out += [blk[:, :SLICES], blk[:, SLICES:]]
    return stack(out)


def front_back(dnumer, share, dw, x, gain, fm, s, e, w, wx, wf, energy, softness, live8):
    live = live8[:1]
    masked = fm * live
    temp = 0.5 + jnp.maximum(s, 0.0) + jnp.log1p(jnp.exp(-jnp.abs(s)))
    inv_temp = 1.0 / temp
    first = iota((8, SLICES), 0) == 0
    dls, dts, dfs, dxs = [], [], [], []
    for h in range(HEADS):
        dn, wh = head(dnumer, h), head(w, h, SLICES)
        dtot = jnp.where(first, -jnp.sum(head(share, h), axis=0, keepdims=True), 0.0)
        dwh = head(dw, h, SLICES) + exact(
            stack([dn, dtot]), stack([head(masked, h), live8]), 0, 0
        )
        de = wh * (dwh - jnp.sum(wh * dwh, axis=0, keepdims=True))
        dl = de * inv_temp[h : h + 1]
        dts.append(-jnp.sum(dl * head(e, h, SLICES), axis=0, keepdims=True))
        dls.append(dl)
        dfs.append(exact(dn, wh))
        dxs.append(exact(energy[h], dl))
    ds = stack(dts) / (1.0 + jnp.exp(-s))
    dx = (stack(dxs) + exact(softness_rows(softness), ds, 0, 0)).astype(BF)
    df = (stack(dfs) * live).astype(BF)
    da = dot(wx, dx) + dot(wf, df)
    xhat, r = normed(x)
    return dx, df, stack(dls), ds, norm_back(xhat, r, gain, da), row_sum(da * xhat)


def core_index():
    return lax.rem(lax.axis_index("row"), 2)


def put_halves(v, mine, other):
    h = v.shape[0] // 2
    zero = core_index() == 0
    mine[...] = jnp.where(zero, v[:h], v[h:])
    other[...] = jnp.where(zero, v[h:], v[:h])


def join_halves(mine, other):
    zero = core_index() == 0
    return stack([jnp.where(zero, mine, other), jnp.where(zero, other, mine)])


def put(refs, values):
    for ref, value in zip(refs, values):
        ref[...] = value


def first_kernel(n, x, g1, wx, wf, en, so, xt, *out):
    v = jnp.transpose(x[...].astype(F32))
    xt[...] = v
    r = front(v, column(g1[0:1]), wx[...], wf[...], en[...], so[0], live_rows(n[0]))
    put(out, r[:6])
    put_halves(r[6], *out[6:])


def save_tokens(toks, attn, tok_ref, attn_ref):
    for i, t in enumerate(toks):
        tok_ref[i] = t
    attn_ref[...] = attn


def middle_kernel(
    n, numer, numer_o, x, w, wq, wk, wv, wo, g2, w1, w2, g1, wx, wf, en, so,
    tok_ref, attn_ref, y_ref, x1_ref, b_ref, u_ref, hid_ref, xt, *out
):
    toks, attn = token_mix(join_halves(numer[...], numer_o[...]), wq[...], wk[...], wv[...])
    save_tokens(toks, attn, tok_ref, attn_ref)
    y, x1, b, u = finish(x[...], w[...], toks[5], wo[...], column(g2[0:1]), w1[...])
    hid = gelu(u).astype(BF)
    put((y_ref, x1_ref, b_ref, u_ref, hid_ref), (y, x1, b, u, hid))
    v = x1 + dot(w2[...], hid, 0, 0)
    xt[...] = v
    r = front(v, column(g1[1:2]), wx[...], wf[...], en[...], so[1], live_rows(n[0]))
    put(out, r[:6])
    put_halves(r[6], *out[6:])


def turn_kernel(
    n, numer, numer_o, x, w, wq, wk, wv, wo, g2, w1, w2, up,
    tok_ref, attn_ref, y_ref, b_ref, hid_ref, *out
):
    toks, attn = token_mix(join_halves(numer[...], numer_o[...]), wq[...], wk[...], wv[...])
    save_tokens(toks, attn, tok_ref, attn_ref)
    gain = column(g2[1:2])
    y, x1, b, u = finish(x[...], w[...], toks[5], wo[...], gain, w1[...])
    put((y_ref, b_ref, hid_ref), (y, b, gelu(u).astype(BF)))
    upt = jnp.transpose(up[...].astype(F32)) * live_rows(n[0])[:1]
    r = finish_back(upt, x1, u, w[...], toks[5], wo[...], gain, w1[...], w2[...])
    put(out, r[:6])
    put_halves(r[6], *out[6:])


def token_grads(tok, dqkv, refs):
    for ref, d in zip(refs, dqkv):
        for h in range(HEADS):
            ref[h] = exact(head(tok, h), head(d, h), 1, 1)


def reverse(layer, n, dmix, dmix_o, tok_ref, attn, wq, wk, wv, dw, x, fm, s, e, w, g1, wx, wf, en, so):
    dnumer, share, dqkv = token_back(
        unpair(join_halves(dmix[...], dmix_o[...])), tok_ref, attn[...], wq[...], wk[...], wv[...]
    )
    out = front_back(
        dnumer, share, dw[...], x[...], column(g1[layer : layer + 1]), fm[...], s[...],
        e[...], w[...], wx[...], wf[...], en[...], so[layer], live_rows(n[0]),
    )
    return out, dqkv


def back_kernel(
    n, dmix, dmix_o, tok_ref, attn, wq, wk, wv, dw, x, fm, s, e, w, g1, wx, wf, en, so,
    after, x1, u, w_below, tok_below, wo, g2, w1, w2,
    dwq, dwk, dwv, dx, df, dl, ds, dg, *out
):
    r, dqkv = reverse(1, n, dmix, dmix_o, tok_ref, attn, wq, wk, wv, dw, x, fm, s, e, w, g1, wx, wf, en, so)
    put((dx, df, dl, ds), r[:4])
    dg[...] = r[5]
    up = after[...] + r[4]
    r = finish_back(
        up, x1[...], u[...], w_below[...], tok_below[5], wo[...], column(g2[0:1]),
        w1[...], w2[...],
    )
    put(out, r[:6])
    put_halves(r[6], *out[6:])
    token_grads(tok_ref[0], dqkv, (dwq, dwk, dwv))


def last_kernel(
    n, dmix, dmix_o, tok_ref, attn, wq, wk, wv, dw, x, fm, s, e, w, g1, wx, wf, en, so,
    after, a, xm, dwq, dwk, dwv, point, mine, other, dx, df, dl, ds, dg
):
    r, dqkv = reverse(
        0, n, dmix, dmix_o, tok_ref, attn, wq, wk, wv, dw, x, fm, s, e, w, g1, wx, wf, en, so
    )
    put((dx, df, dl, ds), r[:4])
    dg[...] = r[5]
    both(front_half, (a, dx, df, xm, dl, ds, dg), mine, other, 0)
    clear(FRONT_HALF, mine, other)
    point[...] = jnp.transpose(after[...] + r[4])
    token_grads(tok_ref[0], dqkv, (dwq, dwk, dwv))


def first_row(v):
    return jnp.where(iota((8, D), 0) == 0, v, 0.0)


FINISH_HALF = 1160
FRONT_HALF = 296


def finish_half(c, hid, up, b, du, y, after, dg, out, at):
    out[at : at + 512] = dot(hid[pl.ds(c * 512, 512)], up[...], 1, 1)
    for k in range(2):
        t = dot(b[...], du[pl.ds(c * 512 + 256 * k, 256)], 1, 1)
        out[at + 512 + 256 * k : at + 768 + 256 * k] = t
    out[at + 1024 : at + 1152] = dot(y[pl.ds(c * 128, 128)], after[...], 1, 1)
    out[at + 1152 : at + 1160] = first_row(dg[...])


def front_half(c, a, dx, df, xm, dl, ds, dg, out, at):
    rows = a[pl.ds(c * 128, 128)]
    out[at : at + 128] = dot(rows, dx[...], 1, 1)
    out[at + 128 : at + 256] = dot(rows, df[...], 1, 1)
    for j in range(2):
        r = exact(xm[pl.ds(c * 128 + 64 * j, 64)], dl[pl.ds(c * 256 + 128 * j, 128)], 1, 1)
        out[at + 256 : at + 288, 128 * j : 128 * (j + 1)] = pair_rows(r)
    t = exact(ds[...], xm[...], 1, 1)
    t = jnp.where((iota((HEADS, D), 1) >> 5) == iota((HEADS, D), 0), t, 0.0)
    t = jnp.sum(t, axis=0, keepdims=True)
    out[at + 288 : at + 296] = first_row(dg[...]) + jnp.where(iota((8, D), 0) == 1, t, 0.0)


def both(half, refs, mine, other, at):
    c = core_index()
    half(c, *refs, mine, at)
    half(1 - c, *refs, other, at)


def clear(rows, *outs):
    for out in outs:
        out[rows:] = jnp.zeros((out.shape[0] - rows, D), F32)


def finish_grads_kernel(*refs):
    both(finish_half, refs[:7], *refs[7:], 0)
    clear(FINISH_HALF, *refs[7:])


def second_grads_kernel(*refs):
    both(finish_half, refs[:7], *refs[14:], 0)
    both(front_half, refs[7:14], *refs[14:], FINISH_HALF)
    clear(FINISH_HALF + FRONT_HALF, *refs[14:])


def ordered(mine, other, out):
    r, h = mine.shape[1], out.shape[1]
    zero = core_index() == 0
    for q in range(16):
        at = place(q, h)
        m, o = mine[q], other[q]
        out[0, at : at + r] = jnp.where(zero, m, o)
        out[1, at : at + r] = jnp.where(zero, o, m)


def unpack_kernel(
    fin, fin_o, sec, sec_o, fro, fro_o, q0, q1, k0, k1, v0, v1,
    ln1, gx, gf, ge, gs, gq, gk, gv, go, ln2, g1, g2, one, two, three
):
    for ref, below, above in ((gq, q0, q1), (gk, k0, k1), (gv, v0, v1)):
        ref[0] = below[...]
        ref[1] = above[...]
    ordered(fin, fin_o, one)
    zero = core_index() == 0
    for mine, other, out in ((sec, sec_o, two), (fro, fro_o, three)):
        out[0] = jnp.where(zero, mine[...], other[...])
        out[1] = jnp.where(zero, other[...], mine[...])
    for l, (fin, fro, at) in enumerate(((two, three, 0), (one, two, FINISH_HALF))):
        for c in range(2):
            g2[l, 512 * c : 512 * (c + 1)] = fin[c, 0:512]
            for k in range(2):
                lane = 512 * c + 256 * k
                g1[l, :, lane : lane + 256] = fin[c, 512 + 256 * k : 768 + 256 * k]
            go[l, 128 * c : 128 * (c + 1)] = fin[c, 1024:1152]
            gx[l, 128 * c : 128 * (c + 1)] = fro[c, at : at + 128]
            gf[l, 128 * c : 128 * (c + 1)] = fro[c, at + 128 : at + 256]
            for h in range(4):
                t = fro[c, at + 256 : at + 288, 128 * (h // 2) : 128 * (h // 2 + 1)]
                ge[l, 4 * c + h] = t[:, 64 * (h % 2) : 64 * (h % 2 + 1)]
        ln2[l : l + 1] = fin[0, 1152:1153]
        ln1[l : l + 1] = fro[0, at + 288 : at + 289]
        for h in range(HEADS):
            gs[l, h : h + 1] = fro[0, at + 289 : at + 290, 32 * h : 32 * (h + 1)]


AXES = ("row", "col")


def linear(z, c, y, x):
    return (z * 2 + c) * 16 + y * 4 + x


def swap(v, zm=0, cm=0, ym=0, xm=0):
    pairs = [
        (linear(z, c, y, x), linear(z ^ zm, c ^ cm, y ^ ym, x ^ xm))
        for z in range(8)
        for c in range(2)
        for y in range(4)
        for x in range(4)
    ]
    return lax.ppermute(v, AXES, pairs)


def coords():
    r = lax.axis_index("row")
    q = lax.axis_index("col")
    return r // 2, r % 2, q // 4, q % 4


def gray(v):
    return ((v ^ (v >> 1)) & 1, v >> 1)


def halves(v, b):
    h = v.shape[0] // 2
    return (
        lax.dynamic_slice_in_dim(v, b * h, h, 0),
        lax.dynamic_slice_in_dim(v, (1 - b) * h, h, 0),
    )


CORE = dict(cm=1)
ALONG_X = (dict(xm=1), dict(xm=2), dict(xm=3))
ALONG_Y = (dict(ym=1), dict(ym=2), dict(ym=3))
NEAR_Z = (dict(zm=1), dict(zm=7), dict(zm=6))


def all_to(v, partners):
    return [(v, k) for k in partners]


def four(v, got):
    return (v + got[0]) + (got[1] + got[2])


def small_sum(mine, other):
    m = mine + (yield [(other, CORE)])[0]
    m = four(m, (yield all_to(m, ALONG_X)))
    m = four(m, (yield all_to(m, ALONG_Y)))
    m = four(m, (yield all_to(m, NEAR_Z)))
    m = m + (yield [(m, dict(zm=2))])[0]
    return m, (yield [(m, CORE)])[0]


def place(q, rows):
    (x0, x1), (y0, y1) = gray(q % 4), gray(q // 4)
    index = x0 * 2 + x1 if y0 == 0 else x1 * 2 + x0
    return y0 * rows // 2 + index * rows // 8 + y1 * rows // 16


def scatter_sum(mine, other, at_once=False):
    z, c, y, x = coords()
    (x0, x1), (y0, y1) = gray(x), gray(y)
    m = mine + (yield [(other, CORE)])[0]
    h = m.shape[0] // 2
    parts = [m[:h], m[h:]]
    for first, second in (((x0, 1), (x1, 3)), ((x1, 3), (x0, 1))):
        cut = [halves(parts[0], first[0]), halves(parts[1], second[0])]
        got = yield [(cut[0][1], dict(xm=first[1])), (cut[1][1], dict(xm=second[1]))]
        parts = [keep + g for (keep, _), g in zip(cut, got)]
    m = jnp.concatenate(parts)
    if at_once:
        t = m.reshape(4, -1, m.shape[-1])
        b = [gray(y ^ k) for k in range(4)]
        cut = [take(t, first * 2 + second) for first, second in b]
        m = four(cut[0], (yield list(zip(cut[1:], ALONG_Y))))
    else:
        for bit, ym in ((y0, 1), (y1, 3)):
            keep, o = halves(m, bit)
            m = keep + (yield [(o, dict(ym=ym))])[0]
    for zm in (1, 2, 7):
        m = m + (yield [(m, dict(zm=zm))])[0]
    return m


def join(bit, v, o):
    return jnp.where(bit == 0, jnp.concatenate([v, o]), jnp.concatenate([o, v]))


def whole_sum(mine, other):
    z, c, y, x = coords()
    (x0, x1), (y0, y1) = gray(x), gray(y)
    m = yield from scatter_sum(mine, other, True)
    for bit, ym in ((y1, 3), (y0, 1)):
        m = join(bit, m, (yield [(m, dict(ym=ym))])[0])
    h = m.shape[0] // 2
    a, b = m[:h], m[h:]
    for first, second in (((x1, 3), (x0, 1)), ((x0, 1), (x1, 3))):
        got = yield [(a, dict(xm=first[1])), (b, dict(xm=second[1]))]
        a, b = join(first[0], a, got[0]), join(second[0], b, got[1])
    m = jnp.concatenate([a, b])
    return m, (yield [(m, CORE)])[0]


def gather(m):
    return lax.all_gather(m, "col")


def take(v, i):
    return lax.dynamic_index_in_dim(v, i, 0, keepdims=False)


def in_order(v, got, i):
    t = [v] + list(got)
    odd = [t[1], t[0], t[3], t[2]]
    t = [jnp.where(i & 1 == 1, b, a) for a, b in zip(t, odd)]
    return jnp.concatenate(
        [jnp.where(i & 2 == 2, b, a) for a, b in zip(t, (t[2], t[3], t[0], t[1]))]
    )


def mid_sum(mine, other):
    z, c, y, x = coords()
    m = mine + (yield [(other, CORE)])[0]
    for i, along in ((x, ALONG_X), (y, ALONG_Y)):
        t = m.reshape(4, -1, m.shape[-1])
        got = yield [(take(t, i ^ (k + 1)), partner) for k, partner in enumerate(along)]
        m = four(take(t, i), got)
    m = four(m, (yield all_to(m, NEAR_Z)))
    m = m + (yield [(m, dict(zm=2))])[0]
    for i, along in ((y, ALONG_Y), (x, ALONG_X)):
        m = in_order(m, (yield all_to(m, along)), i)
    return m, (yield [(m, CORE)])[0]


class Sum:
    def __init__(self, steps_of):
        self.steps_of = steps_of
        self.wanted = next(steps_of)
        self.value = None
        self.done = False

    def send(self, got):
        try:
            self.wanted = self.steps_of.send(got)
        except StopIteration as end:
            self.value, self.done = end.value, True


def phase(sums, *beside):
    sums = [s for s in sums if not s.done]
    moved = [[swap(v, **k) for v, k in s.wanted] for s in sums]
    moved, beside = lax.optimization_barrier((moved, beside))
    for s, got in zip(sums, moved):
        s.send(got)
    return beside


def call(kernel, args, outs, name, scratch=(), cost=None):
    specs, values = [], []
    for a in args:
        if isinstance(a, tuple):
            v, layer = a
            block = (None,) + v.shape[1:]
            zeros = (0,) * (v.ndim - 1)
            specs.append(pl.BlockSpec(block, functools.partial(lambda t, i: t, (layer,) + zeros)))
        else:
            v = a
            if v.dtype == jnp.int32:
                specs.append(pl.BlockSpec(memory_space=pltpu.SMEM))
            else:
                specs.append(
                    pl.BlockSpec(v.shape, functools.partial(lambda t, i: t, (0,) * v.ndim))
                )
        values.append(v)
    out_shape = [jax.ShapeDtypeStruct(s, t) for s, t in outs]
    out_specs = [
        pl.BlockSpec(s, functools.partial(lambda t, i: t, (0,) * len(s))) for s, t in outs
    ]
    return pl.pallas_call(
        kernel,
        grid=(1,),
        in_specs=specs,
        out_specs=out_specs,
        out_shape=out_shape,
        scratch_shapes=list(scratch),
        cost_estimate=cost,
        name=name,
        compiler_params=pltpu.CompilerParams(vmem_limit_bytes=63 * 1024 * 1024),
    )(*values)


WIDE = ((D, PTS), F32)
LOW = ((D, PTS), BF)
BY_SLICE = ((HEADS * SLICES, PTS), F32)
BY_HEAD = ((HEADS, PTS), F32)
HIDDEN = ((FF, PTS), BF)
ROW = ((1, D), F32)
FRONT_OUTS = [LOW, WIDE, WIDE, BY_HEAD, BY_SLICE, BY_SLICE] + [((80, 128), F32)] * 2
TOKEN_OUTS = [((6, D, SLICES), F32), ((HEADS * SLICES, SLICES), F32)]
BACK_OUTS = [LOW, HIDDEN, WIDE, LOW, ROW, BY_SLICE] + [((64, 128), F32)] * 2
TOKEN_GRADS = [((HEADS, WIDTH, WIDTH), F32)] * 3
REVERSE_OUTS = TOKEN_GRADS + [LOW, LOW, BY_SLICE, BY_HEAD, ROW]


FINISH_PAD = 1280
SECOND_PAD = 1536
FRONT_PAD = 384


def cost(flops, nbytes):
    return pl.CostEstimate(flops=flops, bytes_accessed=nbytes, transcendentals=0)


def body(x, n, up, g1, wx, wf, en, so, wq, wk, wv, wo, g2, w1, w2):
    def lead(l):
        return (g1, (wx, l), (wf, l), (en, l), so)

    def mix(l):
        return ((wq, l), (wk, l), (wv, l))

    def total(*part):
        s = Sum(small_sum(*part))
        while not s.done:
            phase([s])
        return s.value

    x0, a0, xm0, fm0, s0, e0, p0, mine, other = call(
        first_kernel, (n, x, *lead(0)), [WIDE] + FRONT_OUTS, "first"
    )
    numer = total(mine, other)
    tok0, attn0, y0, mid0, b0, u0, hid0, x1, a1, xm1, fm1, s1, e1, p1, mine, other = call(
        middle_kernel,
        (n, *numer, x0, p0, *mix(0), (wo, 0), g2, (w1, 0), (w2, 0), *lead(1)),
        TOKEN_OUTS + [LOW, WIDE, LOW, ((FF, PTS), F32), HIDDEN, WIDE] + FRONT_OUTS,
        "middle",
    )
    numer = total(mine, other)
    tok1, attn1, y1, b1, hid1, low1, du1, after1, alow1, dg1, dw1, mine, other = call(
        turn_kernel,
        (n, *numer, x1, p1, *mix(1), (wo, 1), g2, (w1, 1), (w2, 1), up),
        TOKEN_OUTS + [LOW, LOW, HIDDEN] + BACK_OUTS,
        "turn",
    )
    small = Sum(small_sum(mine, other))
    held = phase([small], hid1, low1, b1, du1, y1, alow1, dg1)
    halves1 = call(
        finish_grads_kernel, held, [((FINISH_PAD, D), F32)] * 2, "finish_grads",
        cost=cost(310000000, 4500000),
    )
    halves1 = phase([small], *halves1)
    finish1 = Sum(scatter_sum(*halves1))
    for _ in range(3):
        phase([small, finish1])
    phase([small])
    dmix = small.value
    (gq1, gk1, gv1, dx1, df1, dl1, ds1, dn1, low0, du0, after0, alow0, dg0, dw0, mine, other) = call(
        back_kernel,
        (n, *dmix, tok1, attn1, *mix(1), dw1, x1, fm1, s1, e1, p1, *lead(1))
        + (after1, mid0, u0, p0, tok0, (wo, 0), g2, (w1, 0), (w2, 0)),
        REVERSE_OUTS + BACK_OUTS,
        "back",
        cost=cost(2000000000, 8000000),
    )
    mine, other = phase([finish1], mine, other)
    small = Sum(small_sum(mine, other))
    held = phase(
        [small], hid0, low0, b0, du0, y0, alow0, dg0, a1, dx1, df1, xm1, dl1, ds1, dn1
    )
    halves0 = call(
        second_grads_kernel, held, [((SECOND_PAD, D), F32)] * 2, "second_grads",
        cost=cost(600000000, 6000000),
    )
    halves0 = phase([small, finish1], *halves0)
    second = Sum(whole_sum(*halves0))
    for _ in range(3):
        phase([small, second, finish1])
    fin1 = gather(finish1.value)
    phase([small])
    dmix = small.value
    gq0, gk0, gv0, point, mine, other = call(
        last_kernel,
        (n, *dmix, tok0, attn0, *mix(0), dw0, x0, fm0, s0, e0, p0, *lead(0), after0, a0, xm0),
        TOKEN_GRADS + [((PTS, D), F32)] + [((FRONT_PAD, D), F32)] * 2,
        "last",
        scratch=[pltpu.VMEM(s, t) for s, t in (LOW, LOW, BY_SLICE, BY_HEAD, ROW)],
        cost=cost(2000000000, 6000000),
    )
    mine, other = phase([second], mine, other)
    front0 = Sum(mid_sum(mine, other))
    for _ in range(5):
        phase([front0, second])
    (fin1,) = phase([front0, second], fin1)
    fin1_o = swap(fin1, **CORE)
    (fin1_o,) = phase([front0, second], fin1_o)
    phase([front0, second])
    grads = call(
        unpack_kernel,
        (fin1, fin1_o, *second.value, *front0.value, gq0, gq1, gk0, gk1, gv0, gv1),
        [(v.shape, F32) for v in (g1, wx, wf, en, so, wq, wk, wv, wo, g2, w1, w2)],
        "unpack",
        scratch=[pltpu.VMEM((2, r, D), F32) for r in (FINISH_PAD, SECOND_PAD, FRONT_PAD)],
    )
    return point, *grads


def solution(mesh):
    split = P(("row", "col"), None)
    in_specs = (split, P(("row", "col")), split) + (P(),) * 12
    out_specs = (split,) + (P(),) * 12
    return jax.shard_map(body, mesh=mesh, in_specs=in_specs, out_specs=out_specs, check_vma=False)
```

```python
import functools
import math

import jax
import jax.numpy as jnp
from jax import lax
from jax.experimental import pallas as pl
from jax.experimental.pallas import tpu as pltpu
from jax.sharding import PartitionSpec as P

BF = jnp.bfloat16
F32 = jnp.float32
PTS = 256
D = 256
FF = 1024
HEADS = 8
WIDTH = 32
SLICES = 64
PAIRS = HEADS // 2
EPS = 1e-05


def dot(a, b, ca=1, cb=0):
    return lax.dot_general(a, b, (((ca,), (cb,)), ((), ())), preferred_element_type=F32)


def exact(a, b, ca=1, cb=0):
    return lax.dot_general(
        a,
        b,
        (((ca,), (cb,)), ((), ())),
        precision=lax.Precision.HIGH,
        preferred_element_type=F32,
    )


def head(v, h, n=WIDTH):
    return v[h * n : (h + 1) * n]


def stack(pieces):
    return jnp.concatenate(pieces, axis=0)


def iota(shape, axis):
    return lax.broadcasted_iota(jnp.int32, shape, axis)


def column(row):
    return jnp.transpose(jnp.broadcast_to(row, (PTS, D)))


def row_sum(v):
    return jnp.sum(jnp.transpose(v), axis=0, keepdims=True)


def normed(x):
    c = x - jnp.mean(x, axis=0, keepdims=True)
    r = lax.rsqrt(jnp.mean(c * c, axis=0, keepdims=True) + EPS)
    return c * r, r


def norm_back(xhat, r, gain, g):
    dh = g * gain
    return r * (
        dh
        - jnp.mean(dh, axis=0, keepdims=True)
        - xhat * jnp.mean(dh * xhat, axis=0, keepdims=True)
    )


def live_rows(n):
    keep = (iota((8, PTS), 0) == 0) & (iota((8, PTS), 1) < n)
    return jnp.where(keep, 1.0, 0.0)


def softness_rows(s):
    wide = jnp.concatenate([s] * HEADS, axis=1)
    return jnp.where((iota((HEADS, D), 1) >> 5) == iota((HEADS, D), 0), wide, 0.0)


def block_diagonal(w):
    wide = jnp.concatenate([w.reshape(D, WIDTH)] * HEADS, axis=1)
    return jnp.where((iota((D, D), 0) >> 5) == (iota((D, D), 1) >> 5), wide, 0.0)


def pair_rows(r):
    return jnp.where(iota((WIDTH, 128), 1) < SLICES, r[:WIDTH], r[WIDTH : 2 * WIDTH])


def front(x, gain, wx, wf, energy, softness, live8):
    xhat, _ = normed(x)
    a = (xhat * gain).astype(BF)
    xm = dot(wx, a, 0, 0)
    fm = dot(wf, a, 0, 0)
    s = exact(softness_rows(softness), xm)
    temp = 0.5 + jnp.maximum(s, 0.0) + jnp.log1p(jnp.exp(-jnp.abs(s)))
    es, ws = [], []
    for h in range(HEADS):
        e = exact(energy[h], head(xm, h), 0, 0) / temp[h : h + 1]
        p = jnp.exp(e - jnp.max(e, axis=0, keepdims=True))
        es.append(e)
        ws.append(p / jnp.sum(p, axis=0, keepdims=True))
    w = stack(ws)
    masked = fm * live8[:1]
    rows = []
    for j in range(PAIRS):
        r = exact(stack([head(masked, j, 64), live8]), head(w, j, 128), 1, 1)
        rows += [pair_rows(r), r[64:72]]
    return a, xm, fm, s, stack(es), w, stack(rows)


def token_mix(numer, wq, wk, wv):
    toks, invs = [], []
    for j in range(PAIRS):
        inv = 1.0 / (numer[40 * j + 32 : 40 * j + 33] + EPS)
        t = numer[40 * j : 40 * j + 32] / (numer[40 * j + 32 : 40 * j + 33] + EPS)
        inv = jnp.broadcast_to(inv, (WIDTH, 128))
        toks += [t[:, :SLICES], t[:, SLICES:]]
        invs += [inv[:, :SLICES], inv[:, SLICES:]]
    tok = stack(toks)
    q, k, v = (exact(block_diagonal(w), tok, 0, 0) for w in (wq, wk, wv))
    attns, mixes = [], []
    for h in range(HEADS):
        sc = exact(head(k, h), head(q, h), 0, 0) * (1.0 / math.sqrt(WIDTH))
        p = jnp.exp(sc - jnp.max(sc, axis=0, keepdims=True))
        attn = p / jnp.sum(p, axis=0, keepdims=True)
        attns.append(attn)
        mixes.append(exact(head(v, h), attn))
    return (tok, q, k, v, stack(invs), stack(mixes)), stack(attns)


def token_back(dmix, toks, attn, wq, wk, wv):
    tok, q, k, v, inv = (toks[i] for i in range(5))
    dqs, dks, dvs = [], [], []
    for h in range(HEADS):
        at, dm = head(attn, h, SLICES), head(dmix, h)
        dvs.append(exact(dm, at, 1, 1))
        da = exact(head(v, h), dm, 0, 0)
        ds = at * (da - jnp.sum(at * da, axis=0, keepdims=True)) * (1.0 / math.sqrt(WIDTH))
        dqs.append(exact(head(k, h), ds))
        dks.append(exact(head(q, h), ds, 1, 1))
    dq, dk, dv = stack(dqs), stack(dks), stack(dvs)
    dtok = exact(block_diagonal(wq), dq) + exact(block_diagonal(wk), dk)
    dtok = dtok + exact(block_diagonal(wv), dv)
    dnumer = dtok * inv
    return dnumer, dnumer * tok, (dq, dk, dv)


def finish(x, w, mixed, wo, gain, w1):
    y = stack([exact(head(mixed, h), head(w, h, SLICES)) for h in range(HEADS)]).astype(BF)
    x1 = x + dot(wo, y, 0, 0)
    xhat, _ = normed(x1)
    b = (xhat * gain).astype(BF)
    return y, x1, b, dot(w1, b, 0, 0)


C0 = math.sqrt(2.0 / math.pi)
C1 = 0.044715


def gelu(u):
    return 0.5 * u * (1.0 + jnp.tanh(C0 * (u + C1 * (u * u * u))))


def gelu_slope(u):
    t = jnp.tanh(C0 * (u + C1 * (u * u * u)))
    return 0.5 * (1.0 + t) + 0.5 * u * (1.0 - t * t) * (C0 * (1.0 + 3.0 * C1 * (u * u)))


def finish_back(up, x1, u, w, mixed, wo, gain, w1, w2):
    low = up.astype(BF)
    du = (dot(w2, low) * gelu_slope(u)).astype(BF)
    db = dot(w1, du)
    xhat, r = normed(x1)
    dgain = row_sum(db * xhat)
    after = norm_back(xhat, r, gain, db) + up
    after_low = after.astype(BF)
    dy = dot(wo, after_low)
    dmix = stack(
        [
            pair_rows(exact(head(dy, j, 64), head(w, j, 128), 1, 1))
            for j in range(PAIRS)
        ]
    )
    dw = stack([exact(head(mixed, h), head(dy, h), 0, 0) for h in range(HEADS)])
    return low, du, after, after_low, dgain, dw, dmix


def unpair(v):
    out = []
    for j in range(PAIRS):
        blk = head(v, j)
        out += [blk[:, :SLICES], blk[:, SLICES:]]
    return stack(out)


def front_back(dnumer, share, dw, x, gain, fm, s, e, w, wx, wf, energy, softness, live8):
    live = live8[:1]
    masked = fm * live
    temp = 0.5 + jnp.maximum(s, 0.0) + jnp.log1p(jnp.exp(-jnp.abs(s)))
    inv_temp = 1.0 / temp
    first = iota((8, SLICES), 0) == 0
    dls, dts, dfs, dxs = [], [], [], []
    for h in range(HEADS):
        dn, wh = head(dnumer, h), head(w, h, SLICES)
        dtot = jnp.where(first, -jnp.sum(head(share, h), axis=0, keepdims=True), 0.0)
        dwh = head(dw, h, SLICES) + exact(
            stack([dn, dtot]), stack([head(masked, h), live8]), 0, 0
        )
        de = wh * (dwh - jnp.sum(wh * dwh, axis=0, keepdims=True))
        dl = de * inv_temp[h : h + 1]
        dts.append(-jnp.sum(dl * head(e, h, SLICES), axis=0, keepdims=True))
        dls.append(dl)
        dfs.append(exact(dn, wh))
        dxs.append(exact(energy[h], dl))
    ds = stack(dts) / (1.0 + jnp.exp(-s))
    dx = (stack(dxs) + exact(softness_rows(softness), ds, 0, 0)).astype(BF)
    df = (stack(dfs) * live).astype(BF)
    da = dot(wx, dx) + dot(wf, df)
    xhat, r = normed(x)
    return dx, df, stack(dls), ds, norm_back(xhat, r, gain, da), row_sum(da * xhat)


def core_index():
    return lax.rem(lax.axis_index("row"), 2)


def put_halves(v, mine, other):
    h = v.shape[0] // 2
    zero = core_index() == 0
    mine[...] = jnp.where(zero, v[:h], v[h:])
    other[...] = jnp.where(zero, v[h:], v[:h])


def join_halves(mine, other):
    zero = core_index() == 0
    return stack([jnp.where(zero, mine, other), jnp.where(zero, other, mine)])


def put(refs, values):
    for ref, value in zip(refs, values):
        ref[...] = value


def first_kernel(n, x, g1, wx, wf, en, so, xt, *out):
    v = jnp.transpose(x[...].astype(F32))
    xt[...] = v
    r = front(v, column(g1[0:1]), wx[...], wf[...], en[...], so[0], live_rows(n[0]))
    put(out, r[:6])
    put_halves(r[6], *out[6:])


def save_tokens(toks, attn, tok_ref, attn_ref):
    for i, t in enumerate(toks):
        tok_ref[i] = t
    attn_ref[...] = attn


def middle_kernel(
    n, numer, numer_o, x, w, wq, wk, wv, wo, g2, w1, w2, g1, wx, wf, en, so,
    tok_ref, attn_ref, y_ref, x1_ref, b_ref, u_ref, hid_ref, xt, *out
):
    toks, attn = token_mix(join_halves(numer[...], numer_o[...]), wq[...], wk[...], wv[...])
    save_tokens(toks, attn, tok_ref, attn_ref)
    y, x1, b, u = finish(x[...], w[...], toks[5], wo[...], column(g2[0:1]), w1[...])
    hid = gelu(u).astype(BF)
    put((y_ref, x1_ref, b_ref, u_ref, hid_ref), (y, x1, b, u, hid))
    v = x1 + dot(w2[...], hid, 0, 0)
    xt[...] = v
    r = front(v, column(g1[1:2]), wx[...], wf[...], en[...], so[1], live_rows(n[0]))
    put(out, r[:6])
    put_halves(r[6], *out[6:])


def turn_kernel(
    n, numer, numer_o, x, w, wq, wk, wv, wo, g2, w1, w2, up,
    tok_ref, attn_ref, y_ref, b_ref, hid_ref, *out
):
    toks, attn = token_mix(join_halves(numer[...], numer_o[...]), wq[...], wk[...], wv[...])
    save_tokens(toks, attn, tok_ref, attn_ref)
    gain = column(g2[1:2])
    y, x1, b, u = finish(x[...], w[...], toks[5], wo[...], gain, w1[...])
    put((y_ref, b_ref, hid_ref), (y, b, gelu(u).astype(BF)))
    upt = jnp.transpose(up[...].astype(F32)) * live_rows(n[0])[:1]
    r = finish_back(upt, x1, u, w[...], toks[5], wo[...], gain, w1[...], w2[...])
    put(out, r[:6])
    put_halves(r[6], *out[6:])


def token_grads(tok, dqkv, refs):
    for ref, d in zip(refs, dqkv):
        for h in range(HEADS):
            ref[h] = exact(head(tok, h), head(d, h), 1, 1)


def reverse(layer, n, dmix, dmix_o, tok_ref, attn, wq, wk, wv, dw, x, fm, s, e, w, g1, wx, wf, en, so):
    dnumer, share, dqkv = token_back(
        unpair(join_halves(dmix[...], dmix_o[...])), tok_ref, attn[...], wq[...], wk[...], wv[...]
    )
    out = front_back(
        dnumer, share, dw[...], x[...], column(g1[layer : layer + 1]), fm[...], s[...],
        e[...], w[...], wx[...], wf[...], en[...], so[layer], live_rows(n[0]),
    )
    return out, dqkv


def back_kernel(
    n, dmix, dmix_o, tok_ref, attn, wq, wk, wv, dw, x, fm, s, e, w, g1, wx, wf, en, so,
    after, x1, u, w_below, tok_below, wo, g2, w1, w2,
    dwq, dwk, dwv, dx, df, dl, ds, dg, *out
):
    r, dqkv = reverse(1, n, dmix, dmix_o, tok_ref, attn, wq, wk, wv, dw, x, fm, s, e, w, g1, wx, wf, en, so)
    put((dx, df, dl, ds), r[:4])
    dg[...] = r[5]
    up = after[...] + r[4]
    r = finish_back(
        up, x1[...], u[...], w_below[...], tok_below[5], wo[...], column(g2[0:1]),
        w1[...], w2[...],
    )
    put(out, r[:6])
    put_halves(r[6], *out[6:])
    token_grads(tok_ref[0], dqkv, (dwq, dwk, dwv))


def last_kernel(
    n, dmix, dmix_o, tok_ref, attn, wq, wk, wv, dw, x, fm, s, e, w, g1, wx, wf, en, so,
    after, a, xm, dwq, dwk, dwv, point, mine, other, dx, df, dl, ds, dg
):
    r, dqkv = reverse(
        0, n, dmix, dmix_o, tok_ref, attn, wq, wk, wv, dw, x, fm, s, e, w, g1, wx, wf, en, so
    )
    put((dx, df, dl, ds), r[:4])
    dg[...] = r[5]
    both(front_half, (a, dx, df, xm, dl, ds, dg), mine, other, 0)
    clear(FRONT_HALF, mine, other)
    point[...] = jnp.transpose(after[...] + r[4])
    token_grads(tok_ref[0], dqkv, (dwq, dwk, dwv))


def first_row(v):
    return jnp.where(iota((8, D), 0) == 0, v, 0.0)


FINISH_HALF = 1160
FRONT_HALF = 296


def finish_half(c, hid, up, b, du, y, after, dg, out, at):
    out[at : at + 512] = dot(hid[pl.ds(c * 512, 512)], up[...], 1, 1)
    for k in range(2):
        t = dot(b[...], du[pl.ds(c * 512 + 256 * k, 256)], 1, 1)
        out[at + 512 + 256 * k : at + 768 + 256 * k] = t
    out[at + 1024 : at + 1152] = dot(y[pl.ds(c * 128, 128)], after[...], 1, 1)
    out[at + 1152 : at + 1160] = first_row(dg[...])


def front_half(c, a, dx, df, xm, dl, ds, dg, out, at):
    rows = a[pl.ds(c * 128, 128)]
    out[at : at + 128] = dot(rows, dx[...], 1, 1)
    out[at + 128 : at + 256] = dot(rows, df[...], 1, 1)
    for j in range(2):
        r = exact(xm[pl.ds(c * 128 + 64 * j, 64)], dl[pl.ds(c * 256 + 128 * j, 128)], 1, 1)
        out[at + 256 : at + 288, 128 * j : 128 * (j + 1)] = pair_rows(r)
    t = exact(ds[...], xm[...], 1, 1)
    t = jnp.where((iota((HEADS, D), 1) >> 5) == iota((HEADS, D), 0), t, 0.0)
    t = jnp.sum(t, axis=0, keepdims=True)
    out[at + 288 : at + 296] = first_row(dg[...]) + jnp.where(iota((8, D), 0) == 1, t, 0.0)


def both(half, refs, mine, other, at):
    c = core_index()
    half(c, *refs, mine, at)
    half(1 - c, *refs, other, at)


def clear(rows, *outs):
    for out in outs:
        out[rows:] = jnp.zeros((out.shape[0] - rows, D), F32)


def finish_grads_kernel(*refs):
    both(finish_half, refs[:7], *refs[7:], 0)
    clear(FINISH_HALF, *refs[7:])


def second_grads_kernel(*refs):
    both(finish_half, refs[:7], *refs[14:], 0)
    both(front_half, refs[7:14], *refs[14:], FINISH_HALF)
    clear(FINISH_HALF + FRONT_HALF, *refs[14:])


def ordered(mine, other, out):
    r, h = mine.shape[1], out.shape[1]
    zero = core_index() == 0
    for q in range(16):
        at = place(q, h)
        m, o = mine[q], other[q]
        out[0, at : at + r] = jnp.where(zero, m, o)
        out[1, at : at + r] = jnp.where(zero, o, m)


def halves_of(mine, other):
    size = mine[0].shape[0]
    zero = core_index() == 0

    def rows(c, first, last):
        i = first // size
        cut = slice(first - i * size, last - i * size)
        m, o = mine[i][cut], other[i][cut]
        return jnp.where(zero, m, o) if c == 0 else jnp.where(zero, o, m)

    return rows


def unpack_kernel(
    fin, fin_o, sec_a, sec_b, sec_a_o, sec_b_o, fro, fro_o, q0, q1, k0, k1, v0, v1,
    ln1, gx, gf, ge, gs, gq, gk, gv, go, ln2, g1, g2, one
):
    for ref, below, above in ((gq, q0, q1), (gk, k0, k1), (gv, v0, v1)):
        ref[0] = below[...]
        ref[1] = above[...]
    ordered(fin, fin_o, one)

    def upper(c, first, last):
        return one[c, first:last]

    both_of = halves_of((sec_a, sec_b), (sec_a_o, sec_b_o))
    lower = halves_of((fro,), (fro_o,))
    for l, (fin, fro, at) in enumerate(((both_of, lower, 0), (upper, both_of, FINISH_HALF))):
        for c in range(2):
            g2[l, 512 * c : 512 * (c + 1)] = fin(c, 0, 512)
            for k in range(2):
                lane = 512 * c + 256 * k
                g1[l, :, lane : lane + 256] = fin(c, 512 + 256 * k, 768 + 256 * k)
            go[l, 128 * c : 128 * (c + 1)] = fin(c, 1024, 1152)
            gx[l, 128 * c : 128 * (c + 1)] = fro(c, at, at + 128)
            gf[l, 128 * c : 128 * (c + 1)] = fro(c, at + 128, at + 256)
            pairs = fro(c, at + 256, at + 288)
            for h in range(4):
                t = pairs[:, 128 * (h // 2) : 128 * (h // 2 + 1)]
                ge[l, 4 * c + h] = t[:, 64 * (h % 2) : 64 * (h % 2 + 1)]
        ln2[l : l + 1] = fin(0, 1152, 1160)[0:1]
        last = fro(0, at + 288, at + 296)
        ln1[l : l + 1] = last[0:1]
        for h in range(HEADS):
            gs[l, h : h + 1] = last[1:2, 32 * h : 32 * (h + 1)]


AXES = ("row", "col")


def linear(z, c, y, x):
    return (z * 2 + c) * 16 + y * 4 + x


def swap(v, zm=0, cm=0, ym=0, xm=0):
    pairs = [
        (linear(z, c, y, x), linear(z ^ zm, c ^ cm, y ^ ym, x ^ xm))
        for z in range(8)
        for c in range(2)
        for y in range(4)
        for x in range(4)
    ]
    return lax.ppermute(v, AXES, pairs)


def coords():
    r = lax.axis_index("row")
    q = lax.axis_index("col")
    return r // 2, r % 2, q // 4, q % 4


def gray(v):
    return ((v ^ (v >> 1)) & 1, v >> 1)


def halves(v, b):
    h = v.shape[0] // 2
    return (
        lax.dynamic_slice_in_dim(v, b * h, h, 0),
        lax.dynamic_slice_in_dim(v, (1 - b) * h, h, 0),
    )


CORE = dict(cm=1)
ALONG_X = (dict(xm=1), dict(xm=2), dict(xm=3))
ALONG_Y = (dict(ym=1), dict(ym=2), dict(ym=3))
NEAR_Z = (dict(zm=1), dict(zm=7), dict(zm=6))


def all_to(v, partners):
    return [(v, k) for k in partners]


def four(v, got):
    return (v + got[0]) + (got[1] + got[2])


def small_sum(mine, other):
    m = mine + (yield [(other, CORE)])[0]
    m = four(m, (yield all_to(m, ALONG_X)))
    m = four(m, (yield all_to(m, ALONG_Y)))
    m = four(m, (yield all_to(m, NEAR_Z)))
    m = m + (yield [(m, dict(zm=2))])[0]
    return m, (yield [(m, CORE)])[0]


def place(q, rows):
    (x0, x1), (y0, y1) = gray(q % 4), gray(q // 4)
    index = x0 * 2 + x1 if y0 == 0 else x1 * 2 + x0
    return y0 * rows // 2 + index * rows // 8 + y1 * rows // 16


def scatter_sum(mine, other, at_once=False):
    z, c, y, x = coords()
    (x0, x1), (y0, y1) = gray(x), gray(y)
    m = mine + (yield [(other, CORE)])[0]
    h = m.shape[0] // 2
    parts = [m[:h], m[h:]]
    for first, second in (((x0, 1), (x1, 3)), ((x1, 3), (x0, 1))):
        cut = [halves(parts[0], first[0]), halves(parts[1], second[0])]
        got = yield [(cut[0][1], dict(xm=first[1])), (cut[1][1], dict(xm=second[1]))]
        parts = [keep + g for (keep, _), g in zip(cut, got)]
    m = jnp.concatenate(parts)
    if at_once:
        t = m.reshape(4, -1, m.shape[-1])
        b = [gray(y ^ k) for k in range(4)]
        cut = [take(t, first * 2 + second) for first, second in b]
        m = four(cut[0], (yield list(zip(cut[1:], ALONG_Y))))
    else:
        for bit, ym in ((y0, 1), (y1, 3)):
            keep, o = halves(m, bit)
            m = keep + (yield [(o, dict(ym=ym))])[0]
    for zm in (1, 2, 7):
        m = m + (yield [(m, dict(zm=zm))])[0]
    return m


def join(bit, v, o):
    return jnp.where(bit == 0, jnp.concatenate([v, o]), jnp.concatenate([o, v]))


def whole_sum(mine, other):
    z, c, y, x = coords()
    (x0, x1), (y0, y1) = gray(x), gray(y)
    m = yield from scatter_sum(mine, other, True)
    for bit, ym in ((y1, 3), (y0, 1)):
        m = join(bit, m, (yield [(m, dict(ym=ym))])[0])
    h = m.shape[0] // 2
    a, b = m[:h], m[h:]
    for first, second in (((x1, 3), (x0, 1)), ((x0, 1), (x1, 3))):
        got = yield [(a, dict(xm=first[1])), (b, dict(xm=second[1]))]
        a, b = join(first[0], a, got[0]), join(second[0], b, got[1])
    return [a, b], (yield [(a, CORE), (b, CORE)])


def gather(m):
    return lax.all_gather(m, "col")


def take(v, i):
    return lax.dynamic_index_in_dim(v, i, 0, keepdims=False)


def in_order(v, got, i):
    t = [v] + list(got)
    odd = [t[1], t[0], t[3], t[2]]
    t = [jnp.where(i & 1 == 1, b, a) for a, b in zip(t, odd)]
    return jnp.concatenate(
        [jnp.where(i & 2 == 2, b, a) for a, b in zip(t, (t[2], t[3], t[0], t[1]))]
    )


def mid_sum(mine, other):
    z, c, y, x = coords()
    m = mine + (yield [(other, CORE)])[0]
    for i, along in ((x, ALONG_X), (y, ALONG_Y)):
        t = m.reshape(4, -1, m.shape[-1])
        got = yield [(take(t, i ^ (k + 1)), partner) for k, partner in enumerate(along)]
        m = four(take(t, i), got)
    m = four(m, (yield all_to(m, NEAR_Z)))
    m = m + (yield [(m, dict(zm=2))])[0]
    for i, along in ((y, ALONG_Y), (x, ALONG_X)):
        m = in_order(m, (yield all_to(m, along)), i)
    return m, (yield [(m, CORE)])[0]


class Sum:
    def __init__(self, steps_of):
        self.steps_of = steps_of
        self.wanted = next(steps_of)
        self.value = None
        self.done = False

    def send(self, got):
        try:
            self.wanted = self.steps_of.send(got)
        except StopIteration as end:
            self.value, self.done = end.value, True


def phase(sums, *beside):
    sums = [s for s in sums if not s.done]
    moved = [[swap(v, **k) for v, k in s.wanted] for s in sums]
    moved, beside = lax.optimization_barrier((moved, beside))
    for s, got in zip(sums, moved):
        s.send(got)
    return beside


def call(kernel, args, outs, name, scratch=(), cost=None):
    specs, values = [], []
    for a in args:
        if isinstance(a, tuple):
            v, layer = a
            block = (None,) + v.shape[1:]
            zeros = (0,) * (v.ndim - 1)
            specs.append(pl.BlockSpec(block, functools.partial(lambda t, i: t, (layer,) + zeros)))
        else:
            v = a
            if v.dtype == jnp.int32:
                specs.append(pl.BlockSpec(memory_space=pltpu.SMEM))
            else:
                specs.append(
                    pl.BlockSpec(v.shape, functools.partial(lambda t, i: t, (0,) * v.ndim))
                )
        values.append(v)
    out_shape = [jax.ShapeDtypeStruct(s, t) for s, t in outs]
    out_specs = [
        pl.BlockSpec(s, functools.partial(lambda t, i: t, (0,) * len(s))) for s, t in outs
    ]
    return pl.pallas_call(
        kernel,
        grid=(1,),
        in_specs=specs,
        out_specs=out_specs,
        out_shape=out_shape,
        scratch_shapes=list(scratch),
        cost_estimate=cost,
        name=name,
        compiler_params=pltpu.CompilerParams(vmem_limit_bytes=63 * 1024 * 1024),
    )(*values)


WIDE = ((D, PTS), F32)
LOW = ((D, PTS), BF)
BY_SLICE = ((HEADS * SLICES, PTS), F32)
BY_HEAD = ((HEADS, PTS), F32)
HIDDEN = ((FF, PTS), BF)
ROW = ((1, D), F32)
FRONT_OUTS = [LOW, WIDE, WIDE, BY_HEAD, BY_SLICE, BY_SLICE] + [((80, 128), F32)] * 2
TOKEN_OUTS = [((6, D, SLICES), F32), ((HEADS * SLICES, SLICES), F32)]
BACK_OUTS = [LOW, HIDDEN, WIDE, LOW, ROW, BY_SLICE] + [((64, 128), F32)] * 2
TOKEN_GRADS = [((HEADS, WIDTH, WIDTH), F32)] * 3
REVERSE_OUTS = TOKEN_GRADS + [LOW, LOW, BY_SLICE, BY_HEAD, ROW]


FINISH_PAD = 1280
SECOND_PAD = 1536
FRONT_PAD = 384


def cost(flops, nbytes):
    return pl.CostEstimate(flops=flops, bytes_accessed=nbytes, transcendentals=0)


def body(x, n, up, g1, wx, wf, en, so, wq, wk, wv, wo, g2, w1, w2):
    def lead(l):
        return (g1, (wx, l), (wf, l), (en, l), so)

    def mix(l):
        return ((wq, l), (wk, l), (wv, l))

    def total(*part):
        s = Sum(small_sum(*part))
        while not s.done:
            phase([s])
        return s.value

    x0, a0, xm0, fm0, s0, e0, p0, mine, other = call(
        first_kernel, (n, x, *lead(0)), [WIDE] + FRONT_OUTS, "first"
    )
    numer = total(mine, other)
    tok0, attn0, y0, mid0, b0, u0, hid0, x1, a1, xm1, fm1, s1, e1, p1, mine, other = call(
        middle_kernel,
        (n, *numer, x0, p0, *mix(0), (wo, 0), g2, (w1, 0), (w2, 0), *lead(1)),
        TOKEN_OUTS + [LOW, WIDE, LOW, ((FF, PTS), F32), HIDDEN, WIDE] + FRONT_OUTS,
        "middle",
    )
    numer = total(mine, other)
    tok1, attn1, y1, b1, hid1, low1, du1, after1, alow1, dg1, dw1, mine, other = call(
        turn_kernel,
        (n, *numer, x1, p1, *mix(1), (wo, 1), g2, (w1, 1), (w2, 1), up),
        TOKEN_OUTS + [LOW, LOW, HIDDEN] + BACK_OUTS,
        "turn",
    )
    small = Sum(small_sum(mine, other))
    held = phase([small], hid1, low1, b1, du1, y1, alow1, dg1)
    halves1 = call(
        finish_grads_kernel, held, [((FINISH_PAD, D), F32)] * 2, "finish_grads",
        cost=cost(310000000, 4500000),
    )
    halves1 = phase([small], *halves1)
    finish1 = Sum(scatter_sum(*halves1))
    for _ in range(3):
        phase([small, finish1])
    phase([small])
    dmix = small.value
    (gq1, gk1, gv1, dx1, df1, dl1, ds1, dn1, low0, du0, after0, alow0, dg0, dw0, mine, other) = call(
        back_kernel,
        (n, *dmix, tok1, attn1, *mix(1), dw1, x1, fm1, s1, e1, p1, *lead(1))
        + (after1, mid0, u0, p0, tok0, (wo, 0), g2, (w1, 0), (w2, 0)),
        REVERSE_OUTS + BACK_OUTS,
        "back",
        cost=cost(2000000000, 8000000),
    )
    mine, other = phase([finish1], mine, other)
    small = Sum(small_sum(mine, other))
    held = phase(
        [small], hid0, low0, b0, du0, y0, alow0, dg0, a1, dx1, df1, xm1, dl1, ds1, dn1
    )
    halves0 = call(
        second_grads_kernel, held, [((SECOND_PAD, D), F32)] * 2, "second_grads",
        cost=cost(600000000, 6000000),
    )
    halves0 = phase([small, finish1], *halves0)
    second = Sum(whole_sum(*halves0))
    for _ in range(3):
        phase([small, second, finish1])
    fin1 = gather(finish1.value)
    phase([small])
    dmix = small.value
    gq0, gk0, gv0, point, mine, other = call(
        last_kernel,
        (n, *dmix, tok0, attn0, *mix(0), dw0, x0, fm0, s0, e0, p0, *lead(0), after0, a0, xm0),
        TOKEN_GRADS + [((PTS, D), F32)] + [((FRONT_PAD, D), F32)] * 2,
        "last",
        scratch=[pltpu.VMEM(s, t) for s, t in (LOW, LOW, BY_SLICE, BY_HEAD, ROW)],
        cost=cost(2000000000, 6000000),
    )
    mine, other = phase([second], mine, other)
    front0 = Sum(mid_sum(mine, other))
    for _ in range(5):
        phase([front0, second])
    (fin1,) = phase([front0, second], fin1)
    fin1_o = swap(fin1, **CORE)
    (fin1_o,) = phase([front0, second], fin1_o)
    phase([front0, second])
    grads = call(
        unpack_kernel,
        (fin1, fin1_o, *second.value[0], *second.value[1], *front0.value, gq0, gq1, gk0, gk1, gv0, gv1),
        [(v.shape, F32) for v in (g1, wx, wf, en, so, wq, wk, wv, wo, g2, w1, w2)],
        "unpack",
        scratch=[pltpu.VMEM((2, FINISH_PAD, D), F32)],
    )
    return point, *grads


def solution(mesh):
    split = P(("row", "col"), None)
    in_specs = (split, P(("row", "col")), split) + (P(),) * 12
    out_specs = (split,) + (P(),) * 12
    return jax.shard_map(body, mesh=mesh, in_specs=in_specs, out_specs=out_specs, check_vma=False)
```
